32 devices in a mesh: dp: 16 (over z, x, core), tensor: 2 (over y).
Axes of the slice: x: 2, y: 2, z: 4, core: 2. Of those that a mesh axis runs over, the one named last changes fastest.
Arguments:
- tokens: bfloat16 [32768, 1024], P(('dp', 'tensor')), may hold values from -6 to 6
- cotangent: bfloat16 [32768, 1024], P(('dp', 'tensor')), may hold values from -6 to 6
- w_qkv: bfloat16 [3, 1024, 1024], P(None, None, 'tensor'), may hold values from -0.1875 to 0.1875
- bias_q: float32 [1024], P('tensor'), may hold values from -2 to 2
- bias_v: float32 [1024], P('tensor'), may hold values from -2 to 2
- w_out: bfloat16 [1024, 1024], P('tensor'), may hold values from -3 to 3
- bias_o: float32 [1024], replicated, may hold values from -2 to 2
- gain_one: float32 [1024], replicated, may hold values from 0.25 to 1.75
- shift_one: float32 [1024], replicated, may hold values from -2 to 2
- w_up: bfloat16 [1024, 4096], P(None, 'tensor'), may hold values from -0.1875 to 0.1875
- bias_up: float32 [4096], P('tensor'), may hold values from -2 to 2
- w_down: bfloat16 [4096, 1024], P('tensor'), may hold values from -0.09375 to 0.09375
- bias_down: float32 [1024], replicated, may hold values from -2 to 2
- gain_two: float32 [1024], replicated, may hold values from 0.25 to 1.75
- shift_two: float32 [1024], replicated, may hold values from -2 to 2
Outputs:
- output: bfloat16 [32768, 1024], P(('dp', 'tensor'))
- grad_input: float32 [32768, 1024], P(('dp', 'tensor'))
- grad_qkv: float32 [3, 1024, 1024], P(None, 'dp', 'tensor')
- grad_bias_q: float32 [1024], replicated
- grad_bias_v: float32 [1024], replicated
- grad_out: float32 [1024, 1024], P('tensor', 'dp')
- grad_bias_o: float32 [1024], replicated
- grad_gain_one: float32 [1024], replicated
- grad_shift_one: float32 [1024], replicated
- grad_up: float32 [1024, 4096], P('dp', 'tensor')
- grad_bias_up: float32 [4096], replicated
- grad_down: float32 [4096, 1024], P('tensor', 'dp')
- grad_bias_down: float32 [1024], replicated
- grad_gain_two: float32 [1024], replicated
- grad_shift_two: float32 [1024], replicated
The draws below stay inside these ranges and needn't reach their ends.
All inputs are finite; a program needn't handle non-finite values.
Results may differ from the reference program's by a relative error of at most 0.019.
Values may be sent and summed in bfloat16 or wider, within the bound.
A program may use at most 192 MiB of HBM per device.

```python
import jax
import jax.numpy as jnp
from jax import lax

D = 1024
FF = 4096
HEADS = 16
HEAD_DIM = 64
SEQ = 512
SEQ_DEV = 4
TOKENS = 32768
N_DP = 16


def shard_levels(own_key, dims, shards, low, high):
    level, own = 1.0, jax.random.fold_in(own_key, 6)
    for position, blocks in shards:
        draws = jnp.exp(jax.random.uniform(jax.random.fold_in(own, position), (blocks,), jnp.float32, low / len(shards), high / len(shards)))
        level = level * jnp.repeat(draws, dims[position] // blocks).reshape([-1 if axis == position else 1 for axis in range(len(dims))])
    return level


def gaussian(rng, dims, width, reach, cuts=(), kind=jnp.bfloat16):
    values = width * jax.random.normal(rng, dims, jnp.float32)
    if cuts:
        values = values * shard_levels(rng, dims, cuts, -0.22, 0.18)
    return jnp.clip(values, -reach, reach).astype(kind)


def setup_inputs(seed: int = 0) -> dict:
    key_of = jax.random.split(jax.random.key(seed), 16)
    tokens = gaussian(key_of[0], (TOKENS, D), 1.0, 6.0, ((0, 32),))
    cotangent = gaussian(key_of[1], (TOKENS, D), 1.0, 6.0, ((0, 32),))
    w_qkv = gaussian(key_of[2], (3, D, D), D ** -0.5, 0.1875, ((2, 2),))
    bias_q = gaussian(key_of[3], (D,), 0.3, 2.0, ((0, 2),), jnp.float32)
    bias_v = gaussian(key_of[4], (D,), 0.3, 2.0, ((0, 2),), jnp.float32)
    w_out = gaussian(key_of[5], (D, D), (max(1, D // 256)) ** -0.5, 3.0, ((0, 2),))
    bias_o = gaussian(key_of[6], (D,), 0.3, 2.0, (), jnp.float32)
    gain_one = jnp.clip(1.0 + 0.15 * jax.random.normal(key_of[7], (D,), jnp.float32), 0.25, 1.75)
    shift_one = gaussian(key_of[8], (D,), 0.3, 2.0, (), jnp.float32)
    w_up = gaussian(key_of[9], (D, FF), D ** -0.5, 0.1875, ((1, 2),))
    bias_up = gaussian(key_of[10], (FF,), 0.3, 2.0, ((0, 2),), jnp.float32)
    w_down = gaussian(key_of[11], (FF, D), FF ** -0.5, 0.09375, ((0, 2),))
    bias_down = gaussian(key_of[12], (D,), 0.3, 2.0, (), jnp.float32)
    gain_two = jnp.clip(1.0 + 0.15 * jax.random.normal(key_of[13], (D,), jnp.float32), 0.25, 1.75)
    shift_two = gaussian(key_of[14], (D,), 0.3, 2.0, (), jnp.float32)
    return {"tokens": tokens, "cotangent": cotangent, "w_qkv": w_qkv, "bias_q": bias_q, "bias_v": bias_v, "w_out": w_out, "bias_o": bias_o, "gain_one": gain_one, "shift_one": shift_one, "w_up": w_up, "bias_up": bias_up, "w_down": w_down, "bias_down": bias_down, "gain_two": gain_two, "shift_two": shift_two}


@jax.custom_vjp
def low(v):
    return lax.optimization_barrier(v.astype(jnp.bfloat16)).astype(jnp.float32)

@jax.custom_vjp
def low_back(v):
    return v

def low_keep(v):
    return (low(v), None)

def low_pass(kept, grad):
    return (grad,)

def back_keep(v):
    return (v, None)

def back_low(kept, grad):
    return (low(grad),)
low.defvjp(low_keep, low_pass)
low_back.defvjp(back_keep, back_low)

def matmul(left, right):
    return jnp.dot(left, right, precision=lax.Precision.HIGHEST, preferred_element_type=jnp.float32)

def gelu_exact(inner_pre):
    return 0.5 * inner_pre * (1.0 + jax.scipy.special.erf(inner_pre * 0.7071067811865476))

def layer_norm(summed, gain, shift):
    centre = summed - lax.optimization_barrier(jnp.mean(summed, axis=-1, keepdims=True))
    spread = lax.optimization_barrier(jnp.mean(centre * centre, axis=-1, keepdims=True))
    return centre * lax.rsqrt(spread + 1e-05) * gain + shift

def attend_one(block):
    queries, key_rows, values = block
    raw_scores = jnp.einsum('qhd,khd->hqk', queries, key_rows, precision=lax.Precision.HIGHEST)
    scores = low_back(raw_scores * HEAD_DIM ** (-0.5))
    peak_score = lax.optimization_barrier(jnp.max(scores, axis=-1, keepdims=True))
    lifted = jnp.exp(scores - peak_score)
    weights = lifted / lax.optimization_barrier(jnp.sum(lifted, axis=-1, keepdims=True))
    return jnp.einsum('hqk,khd->qhd', low(weights), values, precision=lax.Precision.HIGHEST)

def encoder(inputs, params):
    w_qkv, bias_q, bias_v, w_out, bias_o, gain_one, shift_one, w_up, bias_up, w_down, bias_down, gain_two, shift_two = params
    seq_count = inputs.shape[0] // SEQ
    head_shape = (seq_count, SEQ, HEADS, HEAD_DIM)
    queries = low_back(low(matmul(inputs, w_qkv[0]) + bias_q))
    key_rows = low_back(low(matmul(inputs, w_qkv[1])))
    values = low_back(low(matmul(inputs, w_qkv[2]) + bias_v))
    context = lax.map(jax.checkpoint(attend_one), (queries.reshape(head_shape), key_rows.reshape(head_shape), values.reshape(head_shape)))
    context = low_back(low(context.reshape(inputs.shape[0], D)))
    attended = low_back(matmul(context, w_out) + bias_o)
    hidden_one = layer_norm(inputs + attended, gain_one, shift_one)
    inner_pre = low_back(matmul(low(hidden_one), w_up) + bias_up)
    active = low(gelu_exact(inner_pre))
    branch = low_back(matmul(active, w_down) + bias_down)
    return layer_norm(hidden_one + branch, gain_two, shift_two)

def reference(tokens, cotangent, w_qkv, bias_q, bias_v, w_out, bias_o, gain_one, shift_one, w_up, bias_up, w_down, bias_down, gain_two, shift_two):
    params = tuple((array.astype(jnp.float32) for array in (w_qkv, bias_q, bias_v, w_out, bias_o, gain_one, shift_one, w_up, bias_up, w_down, bias_down, gain_two, shift_two)))
    group_size = SEQ_DEV * SEQ
    inputs = tokens.astype(jnp.float32).reshape(N_DP, group_size, D)
    cot_rows = cotangent.astype(jnp.float32).reshape(N_DP, group_size, D)

    def group_step(totals, item):
        row_block, back_block = item
        result, pullback = jax.vjp(encoder, row_block, params)
        grad_rows, grad_params = pullback(back_block)
        totals = jax.tree.map(jnp.add, totals, grad_params)
        return (totals, (result.astype(jnp.bfloat16), grad_rows))
    zero_grads = jax.tree.map(jnp.zeros_like, params)
    totals, (results, grad_inputs) = lax.scan(group_step, zero_grads, (inputs, cot_rows))
    return (results.reshape(TOKENS, D), grad_inputs.reshape(TOKENS, D), totals[0], totals[1], totals[2], totals[3], totals[4], totals[5], totals[6], totals[7], totals[8], totals[9], totals[10], totals[11], totals[12])
```

```python
import functools

import jax
import jax.numpy as jnp
from jax import lax
from jax.experimental import pallas as pl
from jax.experimental.pallas import tpu as pltpu
from jax.sharding import PartitionSpec as P

D = 1024
FF = 4096
HEAD_DIM = 64
SEQ = 512


def gelu_pair(inner_pre):
    normal_cdf = 0.5 * (1.0 + jax.scipy.special.erf(inner_pre * 0.7071067811865476))
    density = jnp.exp(-0.5 * inner_pre * inner_pre) * 0.3989422804014327
    return (inner_pre * normal_cdf, normal_cdf + inner_pre * density)


def norm_forward(summed, gain, shift):
    centre = summed - jnp.mean(summed, axis=-1, keepdims=True)
    scaled = lax.rsqrt(jnp.mean(centre * centre, axis=-1, keepdims=True) + 1e-05)
    normed = centre * scaled
    return (normed * gain + shift, normed, scaled)


def norm_backward(upstream, gain, normed, scaled):
    grad_norm = upstream * gain
    return scaled * (
        grad_norm
        - jnp.mean(grad_norm, axis=-1, keepdims=True)
        - normed * jnp.mean(grad_norm * normed, axis=-1, keepdims=True)
    )


def attend_block(block):
    queries, key_rows, values = block
    scores = jnp.einsum(
        "qhd,khd->hqk", queries, key_rows, preferred_element_type=jnp.float32
    ) * HEAD_DIM ** (-0.5)
    peak_score = jnp.max(scores, axis=-1, keepdims=True)
    lifted = jnp.exp(scores - peak_score)
    totals = jnp.sum(lifted, axis=-1, keepdims=True)
    weights = (lifted / totals).astype(jnp.bfloat16)
    context = jnp.einsum("hqk,khd->qhd", weights, values, preferred_element_type=jnp.float32)
    return (context.astype(jnp.bfloat16), (peak_score + jnp.log(totals))[..., 0])


def attend_back(block):
    queries, key_rows, values, logsum, grad_ctx = block
    scale = HEAD_DIM ** (-0.5)
    scores = (
        jnp.einsum("qhd,khd->hqk", queries, key_rows, preferred_element_type=jnp.float32) * scale
    )
    weights = jnp.exp(scores - logsum[..., None])
    grad_weights = jnp.einsum("qhd,khd->hqk", grad_ctx, values, preferred_element_type=jnp.float32)
    grad_scores = weights * (grad_weights - jnp.sum(weights * grad_weights, axis=-1, keepdims=True))
    grad_low = grad_scores.astype(jnp.bfloat16)
    grad_v = jnp.einsum(
        "hqk,qhd->khd", weights.astype(jnp.bfloat16), grad_ctx, preferred_element_type=jnp.float32
    )
    grad_q = (
        jnp.einsum("hqk,khd->qhd", grad_low, key_rows, preferred_element_type=jnp.float32) * scale
    )
    grad_k = (
        jnp.einsum("hqk,qhd->khd", grad_low, queries, preferred_element_type=jnp.float32) * scale
    )
    return (grad_q.astype(jnp.bfloat16), grad_k.astype(jnp.bfloat16), grad_v.astype(jnp.bfloat16))


def body_tensor(
    tokens,
    cotangent,
    w_qkv,
    bias_q,
    bias_v,
    w_out,
    bias_o,
    gain_one,
    shift_one,
    w_up,
    bias_up,
    w_down,
    bias_down,
    gain_two,
    shift_two,
):
    rank = lax.axis_index("tensor")
    full_rows = lax.all_gather(tokens, "tensor", axis=0, tiled=True)
    group_rows = full_rows.shape[0]
    local_width = w_qkv.shape[2]
    head_shape = (group_rows // SEQ, SEQ, local_width // HEAD_DIM, HEAD_DIM)
    projected = jnp.einsum("td,kde->kte", full_rows, w_qkv, preferred_element_type=jnp.float32)
    queries = (projected[0] + bias_q).astype(jnp.bfloat16).reshape(head_shape)
    key_rows = projected[1].astype(jnp.bfloat16).reshape(head_shape)
    values = (projected[2] + bias_v).astype(jnp.bfloat16).reshape(head_shape)
    context, logsum = lax.map(attend_block, (queries, key_rows, values))
    context = context.reshape(group_rows, local_width)
    attended = (
        lax.psum_scatter(
            jnp.dot(context, w_out, preferred_element_type=jnp.float32),
            "tensor",
            scatter_dimension=0,
            tiled=True,
        )
        + bias_o
    )
    hidden_one, normed_one, scaled_one = norm_forward(
        tokens.astype(jnp.float32) + attended, gain_one, shift_one
    )
    hidden_rows = lax.all_gather(hidden_one.astype(jnp.bfloat16), "tensor", axis=0, tiled=True)
    inner_pre = jnp.dot(hidden_rows, w_up, preferred_element_type=jnp.float32) + bias_up
    activated, slope = gelu_pair(inner_pre)
    active_low = activated.astype(jnp.bfloat16)
    branch = (
        lax.psum_scatter(
            jnp.dot(active_low, w_down, preferred_element_type=jnp.float32),
            "tensor",
            scatter_dimension=0,
            tiled=True,
        )
        + bias_down
    )
    result, normed_two, scaled_two = norm_forward(hidden_one + branch, gain_two, shift_two)
    upstream = cotangent.astype(jnp.float32)
    grad_two = norm_backward(upstream, gain_two, normed_two, scaled_two)
    grad_branch = grad_two.astype(jnp.bfloat16)
    branch_rows = lax.all_gather(grad_branch, "tensor", axis=0, tiled=True)
    grad_down = jnp.einsum("tf,td->fd", active_low, branch_rows, preferred_element_type=jnp.float32)
    grad_inner = (
        jnp.einsum("td,fd->tf", branch_rows, w_down, preferred_element_type=jnp.float32) * slope
    ).astype(jnp.bfloat16)
    grad_up = jnp.einsum("td,tf->df", hidden_rows, grad_inner, preferred_element_type=jnp.float32)
    grad_hidden = grad_two + lax.psum_scatter(
        jnp.einsum("tf,df->td", grad_inner, w_up, preferred_element_type=jnp.float32),
        "tensor",
        scatter_dimension=0,
        tiled=True,
    )
    grad_one = norm_backward(grad_hidden, gain_one, normed_one, scaled_one)
    grad_attended = grad_one.astype(jnp.bfloat16)
    attended_rows = lax.all_gather(grad_attended, "tensor", axis=0, tiled=True)
    grad_out = jnp.einsum("te,td->ed", context, attended_rows, preferred_element_type=jnp.float32)
    grad_context = jnp.einsum(
        "td,ed->te", attended_rows, w_out, preferred_element_type=jnp.float32
    ).astype(jnp.bfloat16)
    grad_q, grad_k, grad_v = lax.map(
        attend_back, (queries, key_rows, values, logsum, grad_context.reshape(head_shape))
    )
    grad_stack = jnp.stack(
        [
            grad_q.reshape(group_rows, local_width),
            grad_k.reshape(group_rows, local_width),
            grad_v.reshape(group_rows, local_width),
        ]
    )
    weight_qkv = jnp.einsum(
        "td,kte->kde", full_rows, grad_stack, preferred_element_type=jnp.float32
    )
    grad_input = grad_one + lax.psum_scatter(
        jnp.einsum("kte,kde->td", grad_stack, w_qkv, preferred_element_type=jnp.float32).astype(
            jnp.bfloat16
        ),
        "tensor",
        scatter_dimension=0,
        tiled=True,
    ).astype(jnp.float32)

    def placed(piece, length):
        return lax.dynamic_update_slice_in_dim(
            jnp.zeros((length,), jnp.float32), piece, rank * piece.shape[0], 0
        )

    vectors = lax.psum(
        (
            placed(jnp.sum(grad_stack[0].astype(jnp.float32), axis=0), D),
            placed(jnp.sum(grad_stack[2].astype(jnp.float32), axis=0), D),
            jnp.sum(grad_attended.astype(jnp.float32), axis=0),
            jnp.sum(grad_hidden * normed_one, axis=0),
            jnp.sum(grad_hidden, axis=0),
            placed(jnp.sum(grad_inner.astype(jnp.float32), axis=0), FF),
            jnp.sum(grad_branch.astype(jnp.float32), axis=0),
            jnp.sum(upstream * normed_two, axis=0),
            jnp.sum(upstream, axis=0),
        ),
        ("dp", "tensor"),
    )
    weight_parts = (
        lax.psum_scatter(
            weight_qkv.astype(jnp.bfloat16), "dp", scatter_dimension=1, tiled=True
        ).astype(jnp.float32),
        lax.psum_scatter(
            grad_out.astype(jnp.bfloat16), "dp", scatter_dimension=1, tiled=True
        ).astype(jnp.float32),
        lax.psum_scatter(
            grad_up.astype(jnp.bfloat16), "dp", scatter_dimension=0, tiled=True
        ).astype(jnp.float32),
        lax.psum_scatter(
            grad_down.astype(jnp.bfloat16), "dp", scatter_dimension=1, tiled=True
        ).astype(jnp.float32),
    )
    return (
        result.astype(jnp.bfloat16),
        grad_input,
        weight_parts[0],
        vectors[0],
        vectors[1],
        weight_parts[1],
        vectors[2],
        vectors[3],
        vectors[4],
        weight_parts[2],
        vectors[5],
        weight_parts[3],
        vectors[6],
        vectors[7],
        vectors[8],
    )


AXES = ("dp", "tensor")
LOG2E = 1.4426950408889634
VMEM = 56 * 1024 * 1024
NT = (((1,), (1,)), ((), ()))


def dot(left, right):
    return jnp.dot(left, right, preferred_element_type=jnp.float32)


def dot_nt(left, right):
    return lax.dot_general(left, right, NT, preferred_element_type=jnp.float32)


def head_masks(width):
    lane = lax.broadcasted_iota(jnp.int32, (1, width), 1)
    return lane < HEAD_DIM


def attend_kernel(q_ref, k_ref, v_ref, c_ref, l_ref):
    width = q_ref.shape[1]
    first = head_masks(128)
    for pair in range(width // 128):
        cols = slice(pair * 128, pair * 128 + 128)
        queries, key_rows = q_ref[:, cols], k_ref[:, cols]
        values_t = v_ref[:, cols].T
        parts = []
        for head in range(2):
            mask = first if head == 0 else jnp.logical_not(first)
            picked = jnp.where(mask, queries, jnp.zeros_like(queries))
            scores = dot_nt(key_rows, picked) * (LOG2E * HEAD_DIM**-0.5)
            peak = jnp.max(scores, axis=0, keepdims=True)
            lifted = jnp.exp2(scores - peak)
            totals = jnp.sum(lifted, axis=0, keepdims=True)
            context = dot(
                values_t[head * HEAD_DIM : (head + 1) * HEAD_DIM], lifted.astype(jnp.bfloat16)
            )
            parts.append(context * (1.0 / totals))
            l_ref[0, pair * 2 + head : pair * 2 + head + 1, :] = peak + jnp.log2(totals)
        c_ref[:, cols] = jnp.concatenate(parts, axis=0).T.astype(jnp.bfloat16)


def attend_forward(queries, key_rows, values):
    rows, width = queries.shape
    block = min(width, 512)
    heads = block // HEAD_DIM
    seqs, groups = rows // SEQ, width // block
    spec = pl.BlockSpec((SEQ, block), lambda s, g: (s, g))
    return pl.pallas_call(
        attend_kernel,
        grid=(seqs, groups),
        in_specs=[spec] * 3,
        out_specs=[spec, pl.BlockSpec((1, heads, SEQ), lambda s, g: (s * groups + g, 0, 0))],
        out_shape=[
            jax.ShapeDtypeStruct((rows, width), jnp.bfloat16),
            jax.ShapeDtypeStruct((seqs * groups, heads, SEQ), jnp.float32),
        ],
        compiler_params=pltpu.CompilerParams(vmem_limit_bytes=VMEM),
        cost_estimate=pl.CostEstimate(
            flops=rows * width * SEQ * 4, bytes_accessed=rows * width * 8, transcendentals=rows * SEQ * width // HEAD_DIM
        ),
        name="attend_forward",
    )(queries, key_rows, values)


def attend_back_kernel(q_ref, k_ref, v_ref, l_ref, dc_ref, d_ref):
    width = q_ref.shape[1]
    scale = HEAD_DIM**-0.5
    first = head_masks(128)
    for pair in range(width // 128):
        cols = slice(pair * 128, pair * 128 + 128)
        queries, key_rows, values = q_ref[:, cols], k_ref[:, cols], v_ref[:, cols]
        grad_ctx = dc_ref[:, cols]
        keys_t = key_rows.T
        parts = []
        grad_k = grad_v = None
        for head in range(2):
            mask = first if head == 0 else jnp.logical_not(first)
            picked = jnp.where(mask, queries, jnp.zeros_like(queries))
            grad_picked = jnp.where(mask, grad_ctx, jnp.zeros_like(grad_ctx))
            level = l_ref[0, pair * 2 + head : pair * 2 + head + 1, :]
            weights = jnp.exp2(dot_nt(key_rows, picked) * (LOG2E * scale) - level)
            grad_weights = dot_nt(values, grad_picked)
            rowsum = jnp.sum(weights * grad_weights, axis=0, keepdims=True)
            grad_low = (weights * (grad_weights - rowsum)).astype(jnp.bfloat16)
            piece_v = dot(weights.astype(jnp.bfloat16), grad_picked)
            piece_k = dot(grad_low, picked)
            grad_v = piece_v if grad_v is None else grad_v + piece_v
            grad_k = piece_k if grad_k is None else grad_k + piece_k
            parts.append(dot(keys_t[head * HEAD_DIM : (head + 1) * HEAD_DIM], grad_low))
        grad_q = jnp.concatenate(parts, axis=0).T
        d_ref[0, :, cols] = (grad_q * scale).astype(jnp.bfloat16)
        d_ref[1, :, cols] = (grad_k * scale).astype(jnp.bfloat16)
        d_ref[2, :, cols] = grad_v.astype(jnp.bfloat16)


def attend_backward(queries, key_rows, values, level, grad_ctx):
    rows, width = queries.shape
    block = min(width, 512)
    heads = block // HEAD_DIM
    seqs, groups = rows // SEQ, width // block
    spec = pl.BlockSpec((SEQ, block), lambda s, g: (s, g))
    return pl.pallas_call(
        attend_back_kernel,
        grid=(seqs, groups),
        in_specs=[spec] * 3
        + [pl.BlockSpec((1, heads, SEQ), lambda s, g: (s * groups + g, 0, 0)), spec],
        out_specs=pl.BlockSpec((3, SEQ, block), lambda s, g: (0, s, g)),
        out_shape=jax.ShapeDtypeStruct((3, rows, width), jnp.bfloat16),
        compiler_params=pltpu.CompilerParams(vmem_limit_bytes=VMEM),
        cost_estimate=pl.CostEstimate(
            flops=rows * width * SEQ * 10, bytes_accessed=rows * width * 14, transcendentals=rows * SEQ * width // HEAD_DIM
        ),
        name="attend_backward",
    )(queries, key_rows, values, level, grad_ctx)


def weight_grad_kernel(me_ref, a_ref, by_own, bx_own, by_oth, bx_oth, keep_y, send_y, keep_x, send_x, turned):
    rel, step = pl.program_id(0), pl.program_id(1)
    pieces = 16
    height = turned.shape[0] // pieces

    @pl.when(jnp.logical_and(rel == 0, step == 0))
    def _():
        whole = a_ref[...].T
        me = me_ref[0]
        for piece in range(pieces):
            same = (me ^ piece) ^ 15
            spot = (same & 1) * 8 + (same & 2) * 2 + (same & 4) // 2 + (same & 8) // 8
            turned[pl.ds(pl.multiple_of(spot * height, height), height), :] = whole[
                piece * height : (piece + 1) * height
            ]

    half = turned.shape[0] // 2

    def work(y_ref, x_ref):
        for src, keep, send in ((y_ref, keep_y, send_y), (x_ref, keep_x, send_x)):
            right = src[...].reshape(src.shape[-2:])
            send[...] = dot(turned[:half], right).astype(jnp.bfloat16).reshape(send.shape)
            keep[...] = dot(turned[half:], right).astype(jnp.bfloat16).reshape(keep.shape)

    @pl.when(rel == 0)
    def _():
        work(by_oth, bx_oth)

    @pl.when(rel == 1)
    def _():
        work(by_own, bx_own)


def weight_grad(place, left, own, other, tile):
    rows, depth = left.shape
    stacked = own.ndim == 3
    if stacked:
        kinds, _, width = own.shape
        steps = kinds
        assert tile * 2 == width
        shape = (1, rows, tile)
        y_map, x_map = (lambda j: (j, 0, 0)), (lambda j: (j, 0, 1))
        columns = kinds * width // 2
    else:
        width = own.shape[1]
        steps = width // 2 // tile
        shape = (rows, tile)
        y_map, x_map = (lambda j: (0, j)), (lambda j: (0, j + steps))
        columns = width // 2
    height = depth // 16

    def own_map(index_map):
        return lambda r, j, me: index_map(j * r)

    def other_map(index_map):
        return lambda r, j, me: index_map(jnp.where(r == 0, j, steps - 1))

    y_shape = jax.ShapeDtypeStruct((2, 2, 2, 2, height, columns), jnp.bfloat16)
    y_spec = pl.BlockSpec((1, 2, 2, 2, height, tile), lambda r, j, me: (r, 0, 0, 0, 0, j))
    x_spec = pl.BlockSpec((2, 1, 2, 2, height, tile), lambda r, j, me: (0, r, 0, 0, 0, j))
    return pl.pallas_call(
        weight_grad_kernel,
        grid_spec=pltpu.PrefetchScalarGridSpec(
            num_scalar_prefetch=1,
            grid=(2, steps),
            in_specs=[
                pl.BlockSpec((rows, depth), lambda r, j, me: (0, 0)),
                pl.BlockSpec(shape, own_map(y_map)),
                pl.BlockSpec(shape, own_map(x_map)),
                pl.BlockSpec(shape, other_map(y_map)),
                pl.BlockSpec(shape, other_map(x_map)),
            ],
            out_specs=[y_spec, y_spec, x_spec, x_spec],
            scratch_shapes=[pltpu.VMEM((depth, rows), jnp.bfloat16)],
        ),
        out_shape=[y_shape] * 4,
        compiler_params=pltpu.CompilerParams(vmem_limit_bytes=VMEM),
        cost_estimate=pl.CostEstimate(
            flops=rows * depth * columns * 8, bytes_accessed=rows * depth * 2 + rows * columns * 8 + depth * columns * 8, transcendentals=0
        ),
        name="weight_grad",
    )(place, left, own, own, other, other)


def add_low(*parts):
    total = parts[0].astype(jnp.float32)
    for part in parts[1:]:
        total = total + part.astype(jnp.float32)
    return total


def body(mesh, *args):
    tokens, w_qkv = args[0], args[2]
    n_dp, n_tensor = mesh.shape["dp"], mesh.shape["tensor"]
    if n_dp == 16 and n_tensor == 2 and tokens.shape[0] % SEQ == 0 and w_qkv.shape[2] % 256 == 0:
        return body_tokens(*args)
    return body_tensor(*args)


def body_tokens(
    tokens,
    cotangent,
    w_qkv,
    bias_q,
    bias_v,
    w_out,
    bias_o,
    gain_one,
    shift_one,
    w_up,
    bias_up,
    w_down,
    bias_down,
    gain_two,
    shift_two,
):
    me_dp, me_t = lax.axis_index("dp"), lax.axis_index("tensor")
    core = me_dp % 2
    place = me_dp.reshape(1).astype(jnp.int32)

    def swap(value, dp_bit=0, tensor_bit=0):
        pairs = [
            ((d * 2 + t), ((d ^ dp_bit) * 2 + (t ^ tensor_bit))) for d in range(16) for t in range(2)
        ]
        return lax.ppermute(value, AXES, pairs)

    def other_half(weight, axis):
        size = weight.shape[axis] // 2
        mine = lax.dynamic_slice_in_dim(weight, core * size, size, axis)
        mine = swap(mine, tensor_bit=1)
        theirs = swap(mine, dp_bit=1)
        return jnp.where(
            core == 0,
            jnp.concatenate([mine, theirs], axis),
            jnp.concatenate([theirs, mine], axis),
        )

    widths = (bias_q.shape[0], bias_v.shape[0], bias_up.shape[0])
    biases = swap(jnp.concatenate([bias_q, bias_v, bias_up]), tensor_bit=1)
    bias_q2 = biases[: widths[0]]
    bias_v2 = biases[widths[0] : widths[0] + widths[1]]
    bias_up2 = biases[widths[0] + widths[1] :]
    w_qkv2 = other_half(w_qkv, 1)
    w_out2 = other_half(w_out, 0)
    w_up2 = other_half(w_up, 0)
    w_down2 = other_half(w_down, 0)

    halves = ((w_qkv, bias_q, bias_v), (w_qkv2, bias_q2, bias_v2))
    kept = []
    for weight, b_q, b_v in halves:
        queries = (dot(tokens, weight[0]) + b_q).astype(jnp.bfloat16)
        key_rows = dot(tokens, weight[1]).astype(jnp.bfloat16)
        values = (dot(tokens, weight[2]) + b_v).astype(jnp.bfloat16)
        context, level = attend_forward(queries, key_rows, values)
        kept.append((queries, key_rows, values, level, context))
    ctx, ctx2 = kept[0][4], kept[1][4]
    attended = dot(ctx, w_out) + dot(ctx2, w_out2) + bias_o
    hidden_one, normed_one, scaled_one = norm_forward(
        tokens.astype(jnp.float32) + attended, gain_one, shift_one
    )
    hidden_rows = hidden_one.astype(jnp.bfloat16)

    def expand(weight, bias):
        activated, slope = gelu_pair(dot(hidden_rows, weight) + bias)
        return activated.astype(jnp.bfloat16), slope.astype(jnp.bfloat16)

    active, slope = expand(w_up, bias_up)
    active2, slope2 = expand(w_up2, bias_up2)
    branch = dot(active, w_down) + dot(active2, w_down2) + bias_down
    result, normed_two, scaled_two = norm_forward(hidden_one + branch, gain_two, shift_two)
    upstream = cotangent.astype(jnp.float32)
    grad_two = norm_backward(upstream, gain_two, normed_two, scaled_two)
    grad_branch = grad_two.astype(jnp.bfloat16)

    parts_down = weight_grad(place, grad_branch, active, active2, 512)
    grad_inner = (dot_nt(grad_branch, w_down) * slope.astype(jnp.float32)).astype(jnp.bfloat16)
    grad_inner2 = (dot_nt(grad_branch, w_down2) * slope2.astype(jnp.float32)).astype(jnp.bfloat16)
    parts_up = weight_grad(place, hidden_rows, grad_inner, grad_inner2, 512)
    grad_hidden = grad_two + dot_nt(grad_inner, w_up) + dot_nt(grad_inner2, w_up2)
    grad_one = norm_backward(grad_hidden, gain_one, normed_one, scaled_one)
    grad_attended = grad_one.astype(jnp.bfloat16)
    parts_out = weight_grad(place, grad_attended, ctx, ctx2, 256)
    grad_stack = attend_backward(*kept[0][:4], dot_nt(grad_attended, w_out).astype(jnp.bfloat16))
    grad_stack2 = attend_backward(*kept[1][:4], dot_nt(grad_attended, w_out2).astype(jnp.bfloat16))
    parts_qkv = weight_grad(place, tokens, grad_stack, grad_stack2, 256)
    grad_input = grad_one
    for stack, weight in ((grad_stack, w_qkv), (grad_stack2, w_qkv2)):
        for kind in range(3):
            grad_input = grad_input + dot_nt(stack[kind], weight[kind])

    def scatter(parts):
        keep_y, send_y, keep_x, send_x = parts
        outs = []
        for keep, send, order in (
            (keep_y, send_y, ((0, 1), (2, 0), (4, 0), (8, 0))),
            (keep_x, send_x, ((2, 0), (0, 1), (4, 0), (8, 0))),
        ):
            addends = [keep, swap(send, dp_bit=1)]
            for dp_bit, tensor_bit in order:
                leaving = add_low(*[a[0] for a in addends]).astype(jnp.bfloat16)
                arrived = swap(leaving, dp_bit, tensor_bit)
                addends = [add_low(*[a[1] for a in addends]).astype(jnp.bfloat16), arrived]
            outs.append(add_low(*addends))
        return outs

    down_y, down_x = scatter(parts_down)
    up_y, up_x = scatter(parts_up)
    out_y, out_x = scatter(parts_out)
    qkv_y, qkv_x = scatter(parts_qkv)
    grad_down = jnp.concatenate([down_y, down_x], axis=1).T
    grad_up = jnp.concatenate([up_y, up_x], axis=1)
    grad_out = jnp.concatenate([out_y, out_x], axis=1).T
    rows = qkv_y.shape[0]
    grad_qkv = jnp.concatenate([qkv_y.reshape(rows, 3, -1), qkv_x.reshape(rows, 3, -1)], axis=2)
    grad_qkv = jnp.transpose(grad_qkv, (1, 0, 2))

    def whole(own, other):
        own, other = (jnp.sum(v.astype(jnp.float32), axis=0) for v in (own, other))
        return jnp.where(
            me_t == 0, jnp.concatenate([own, other]), jnp.concatenate([other, own])
        )

    def all_sum(pieces):
        sizes = [piece.shape[0] for piece in pieces]
        total = jnp.concatenate(pieces)
        for dp_bit, tensor_bit in ((1, 0), (0, 1), (2, 0), (4, 0), (8, 0)):
            total = total + swap(total, dp_bit, tensor_bit)
        result, at = [], 0
        for size in sizes:
            result.append(total[at : at + size])
            at += size
        return result

    g_shift_two, g_gain_two, g_bias_down, g_bias_up, g_shift_one, g_gain_one, g_bias_o = all_sum(
        [
            jnp.sum(upstream, axis=0),
            jnp.sum(upstream * normed_two, axis=0),
            jnp.sum(grad_branch.astype(jnp.float32), axis=0),
            whole(grad_inner, grad_inner2),
            jnp.sum(grad_hidden, axis=0),
            jnp.sum(grad_hidden * normed_one, axis=0),
            jnp.sum(grad_attended.astype(jnp.float32), axis=0),
        ]
    )
    g_bias_q, g_bias_v = all_sum(
        [whole(grad_stack[0], grad_stack2[0]), whole(grad_stack[2], grad_stack2[2])]
    )
    return (
        result.astype(jnp.bfloat16),
        grad_input,
        grad_qkv,
        g_bias_q,
        g_bias_v,
        grad_out,
        g_bias_o,
        g_gain_one,
        g_shift_one,
        grad_up,
        g_bias_up,
        grad_down,
        g_bias_down,
        g_gain_two,
        g_shift_two,
    )


def solution(mesh):
    in_specs = (
        P(("dp", "tensor"), None),
        P(("dp", "tensor"), None),
        P(None, None, "tensor"),
        P("tensor"),
        P("tensor"),
        P("tensor", None),
        P(),
        P(),
        P(),
        P(None, "tensor"),
        P("tensor"),
        P("tensor", None),
        P(),
        P(),
        P(),
    )
    out_specs = (
        P(("dp", "tensor"), None),
        P(("dp", "tensor"), None),
        P(None, "dp", "tensor"),
        P(),
        P(),
        P("tensor", "dp"),
        P(),
        P(),
        P(),
        P("dp", "tensor"),
        P(),
        P("tensor", "dp"),
        P(),
        P(),
        P(),
    )
    return jax.shard_map(functools.partial(body, mesh), mesh=mesh, in_specs=in_specs, out_specs=out_specs, check_vma=False)
```

```python
import functools

import jax
import jax.numpy as jnp
from jax import lax
from jax.experimental import pallas as pl
from jax.experimental.pallas import tpu as pltpu
from jax.sharding import PartitionSpec as P

D = 1024
FF = 4096
HEAD_DIM = 64
SEQ = 512


def gelu_pair(inner_pre):
    normal_cdf = 0.5 * (1.0 + jax.scipy.special.erf(inner_pre * 0.7071067811865476))
    density = jnp.exp(-0.5 * inner_pre * inner_pre) * 0.3989422804014327
    return (inner_pre * normal_cdf, normal_cdf + inner_pre * density)


def norm_forward(summed, gain, shift):
    centre = summed - jnp.mean(summed, axis=-1, keepdims=True)
    scaled = lax.rsqrt(jnp.mean(centre * centre, axis=-1, keepdims=True) + 1e-05)
    normed = centre * scaled
    return (normed * gain + shift, normed, scaled)


def norm_backward(upstream, gain, normed, scaled):
    grad_norm = upstream * gain
    return scaled * (
        grad_norm
        - jnp.mean(grad_norm, axis=-1, keepdims=True)
        - normed * jnp.mean(grad_norm * normed, axis=-1, keepdims=True)
    )


def attend_block(block):
    queries, key_rows, values = block
    scores = jnp.einsum(
        "qhd,khd->hqk", queries, key_rows, preferred_element_type=jnp.float32
    ) * HEAD_DIM ** (-0.5)
    peak_score = jnp.max(scores, axis=-1, keepdims=True)
    lifted = jnp.exp(scores - peak_score)
    totals = jnp.sum(lifted, axis=-1, keepdims=True)
    weights = (lifted / totals).astype(jnp.bfloat16)
    context = jnp.einsum("hqk,khd->qhd", weights, values, preferred_element_type=jnp.float32)
    return (context.astype(jnp.bfloat16), (peak_score + jnp.log(totals))[..., 0])


def attend_back(block):
    queries, key_rows, values, logsum, grad_ctx = block
    scale = HEAD_DIM ** (-0.5)
    scores = (
        jnp.einsum("qhd,khd->hqk", queries, key_rows, preferred_element_type=jnp.float32) * scale
    )
    weights = jnp.exp(scores - logsum[..., None])
    grad_weights = jnp.einsum("qhd,khd->hqk", grad_ctx, values, preferred_element_type=jnp.float32)
    grad_scores = weights * (grad_weights - jnp.sum(weights * grad_weights, axis=-1, keepdims=True))
    grad_low = grad_scores.astype(jnp.bfloat16)
    grad_v = jnp.einsum(
        "hqk,qhd->khd", weights.astype(jnp.bfloat16), grad_ctx, preferred_element_type=jnp.float32
    )
    grad_q = (
        jnp.einsum("hqk,khd->qhd", grad_low, key_rows, preferred_element_type=jnp.float32) * scale
    )
    grad_k = (
        jnp.einsum("hqk,qhd->khd", grad_low, queries, preferred_element_type=jnp.float32) * scale
    )
    return (grad_q.astype(jnp.bfloat16), grad_k.astype(jnp.bfloat16), grad_v.astype(jnp.bfloat16))


def body_tensor(
    tokens,
    cotangent,
    w_qkv,
    bias_q,
    bias_v,
    w_out,
    bias_o,
    gain_one,
    shift_one,
    w_up,
    bias_up,
    w_down,
    bias_down,
    gain_two,
    shift_two,
):
    rank = lax.axis_index("tensor")
    full_rows = lax.all_gather(tokens, "tensor", axis=0, tiled=True)
    group_rows = full_rows.shape[0]
    local_width = w_qkv.shape[2]
    head_shape = (group_rows // SEQ, SEQ, local_width // HEAD_DIM, HEAD_DIM)
    projected = jnp.einsum("td,kde->kte", full_rows, w_qkv, preferred_element_type=jnp.float32)
    queries = (projected[0] + bias_q).astype(jnp.bfloat16).reshape(head_shape)
    key_rows = projected[1].astype(jnp.bfloat16).reshape(head_shape)
    values = (projected[2] + bias_v).astype(jnp.bfloat16).reshape(head_shape)
    context, logsum = lax.map(attend_block, (queries, key_rows, values))
    context = context.reshape(group_rows, local_width)
    attended = (
        lax.psum_scatter(
            jnp.dot(context, w_out, preferred_element_type=jnp.float32),
            "tensor",
            scatter_dimension=0,
            tiled=True,
        )
        + bias_o
    )
    hidden_one, normed_one, scaled_one = norm_forward(
        tokens.astype(jnp.float32) + attended, gain_one, shift_one
    )
    hidden_rows = lax.all_gather(hidden_one.astype(jnp.bfloat16), "tensor", axis=0, tiled=True)
    inner_pre = jnp.dot(hidden_rows, w_up, preferred_element_type=jnp.float32) + bias_up
    activated, slope = gelu_pair(inner_pre)
    active_low = activated.astype(jnp.bfloat16)
    branch = (
        lax.psum_scatter(
            jnp.dot(active_low, w_down, preferred_element_type=jnp.float32),
            "tensor",
            scatter_dimension=0,
            tiled=True,
        )
        + bias_down
    )
    result, normed_two, scaled_two = norm_forward(hidden_one + branch, gain_two, shift_two)
    upstream = cotangent.astype(jnp.float32)
    grad_two = norm_backward(upstream, gain_two, normed_two, scaled_two)
    grad_branch = grad_two.astype(jnp.bfloat16)
    branch_rows = lax.all_gather(grad_branch, "tensor", axis=0, tiled=True)
    grad_down = jnp.einsum("tf,td->fd", active_low, branch_rows, preferred_element_type=jnp.float32)
    grad_inner = (
        jnp.einsum("td,fd->tf", branch_rows, w_down, preferred_element_type=jnp.float32) * slope
    ).astype(jnp.bfloat16)
    grad_up = jnp.einsum("td,tf->df", hidden_rows, grad_inner, preferred_element_type=jnp.float32)
    grad_hidden = grad_two + lax.psum_scatter(
        jnp.einsum("tf,df->td", grad_inner, w_up, preferred_element_type=jnp.float32),
        "tensor",
        scatter_dimension=0,
        tiled=True,
    )
    grad_one = norm_backward(grad_hidden, gain_one, normed_one, scaled_one)
    grad_attended = grad_one.astype(jnp.bfloat16)
    attended_rows = lax.all_gather(grad_attended, "tensor", axis=0, tiled=True)
    grad_out = jnp.einsum("te,td->ed", context, attended_rows, preferred_element_type=jnp.float32)
    grad_context = jnp.einsum(
        "td,ed->te", attended_rows, w_out, preferred_element_type=jnp.float32
    ).astype(jnp.bfloat16)
    grad_q, grad_k, grad_v = lax.map(
        attend_back, (queries, key_rows, values, logsum, grad_context.reshape(head_shape))
    )
    grad_stack = jnp.stack(
        [
            grad_q.reshape(group_rows, local_width),
            grad_k.reshape(group_rows, local_width),
            grad_v.reshape(group_rows, local_width),
        ]
    )
    weight_qkv = jnp.einsum(
        "td,kte->kde", full_rows, grad_stack, preferred_element_type=jnp.float32
    )
    grad_input = grad_one + lax.psum_scatter(
        jnp.einsum("kte,kde->td", grad_stack, w_qkv, preferred_element_type=jnp.float32).astype(
            jnp.bfloat16
        ),
        "tensor",
        scatter_dimension=0,
        tiled=True,
    ).astype(jnp.float32)

    def placed(piece, length):
        return lax.dynamic_update_slice_in_dim(
            jnp.zeros((length,), jnp.float32), piece, rank * piece.shape[0], 0
        )

    vectors = lax.psum(
        (
            placed(jnp.sum(grad_stack[0].astype(jnp.float32), axis=0), D),
            placed(jnp.sum(grad_stack[2].astype(jnp.float32), axis=0), D),
            jnp.sum(grad_attended.astype(jnp.float32), axis=0),
            jnp.sum(grad_hidden * normed_one, axis=0),
            jnp.sum(grad_hidden, axis=0),
            placed(jnp.sum(grad_inner.astype(jnp.float32), axis=0), FF),
            jnp.sum(grad_branch.astype(jnp.float32), axis=0),
            jnp.sum(upstream * normed_two, axis=0),
            jnp.sum(upstream, axis=0),
        ),
        ("dp", "tensor"),
    )
    weight_parts = (
        lax.psum_scatter(
            weight_qkv.astype(jnp.bfloat16), "dp", scatter_dimension=1, tiled=True
        ).astype(jnp.float32),
        lax.psum_scatter(
            grad_out.astype(jnp.bfloat16), "dp", scatter_dimension=1, tiled=True
        ).astype(jnp.float32),
        lax.psum_scatter(
            grad_up.astype(jnp.bfloat16), "dp", scatter_dimension=0, tiled=True
        ).astype(jnp.float32),
        lax.psum_scatter(
            grad_down.astype(jnp.bfloat16), "dp", scatter_dimension=1, tiled=True
        ).astype(jnp.float32),
    )
    return (
        result.astype(jnp.bfloat16),
        grad_input,
        weight_parts[0],
        vectors[0],
        vectors[1],
        weight_parts[1],
        vectors[2],
        vectors[3],
        vectors[4],
        weight_parts[2],
        vectors[5],
        weight_parts[3],
        vectors[6],
        vectors[7],
        vectors[8],
    )


AXES = ("dp", "tensor")
LOG2E = 1.4426950408889634
VMEM = 56 * 1024 * 1024
NT = (((1,), (1,)), ((), ()))


def dot(left, right):
    return jnp.dot(left, right, preferred_element_type=jnp.float32)


def dot_nt(left, right):
    return lax.dot_general(left, right, NT, preferred_element_type=jnp.float32)


def head_masks(width):
    lane = lax.broadcasted_iota(jnp.int32, (1, width), 1)
    return lane < HEAD_DIM


def attend_kernel(q_ref, k_ref, v_ref, c_ref, l_ref):
    width = q_ref.shape[1]
    first = head_masks(128)
    for pair in range(width // 128):
        cols = slice(pair * 128, pair * 128 + 128)
        queries, key_rows = q_ref[:, cols], k_ref[:, cols]
        values_t = v_ref[:, cols].T
        parts = []
        for head in range(2):
            mask = first if head == 0 else jnp.logical_not(first)
            picked = jnp.where(mask, queries, jnp.zeros_like(queries))
            scores = dot_nt(key_rows, picked) * (LOG2E * HEAD_DIM**-0.5)
            peak = jnp.max(scores, axis=0, keepdims=True)
            lifted = jnp.exp2(scores - peak)
            totals = jnp.sum(lifted, axis=0, keepdims=True)
            context = dot(
                values_t[head * HEAD_DIM : (head + 1) * HEAD_DIM], lifted.astype(jnp.bfloat16)
            )
            parts.append(context * (1.0 / totals))
            l_ref[0, pair * 2 + head : pair * 2 + head + 1, :] = peak + jnp.log2(totals)
        c_ref[:, cols] = jnp.concatenate(parts, axis=0).T.astype(jnp.bfloat16)


def attend_forward(queries, key_rows, values):
    rows, width = queries.shape
    block = min(width, 512)
    heads = block // HEAD_DIM
    seqs, groups = rows // SEQ, width // block
    spec = pl.BlockSpec((SEQ, block), lambda s, g: (s, g))
    return pl.pallas_call(
        attend_kernel,
        grid=(seqs, groups),
        in_specs=[spec] * 3,
        out_specs=[spec, pl.BlockSpec((1, heads, SEQ), lambda s, g: (s * groups + g, 0, 0))],
        out_shape=[
            jax.ShapeDtypeStruct((rows, width), jnp.bfloat16),
            jax.ShapeDtypeStruct((seqs * groups, heads, SEQ), jnp.float32),
        ],
        compiler_params=pltpu.CompilerParams(vmem_limit_bytes=VMEM),
        cost_estimate=pl.CostEstimate(
            flops=rows * width * SEQ * 4, bytes_accessed=rows * width * 8, transcendentals=rows * SEQ * width // HEAD_DIM
        ),
        name="attend_forward",
    )(queries, key_rows, values)


MESH = pl.DeviceIdType.MESH
CHUNKS = 8
SPAN = 256


def bit_of(index, bit):
    return lax.rem(lax.div(index, bit), 2)


def flip(index, bit):
    return index + bit - 2 * bit * bit_of(index, bit)


def mine():
    return lax.axis_index("dp"), lax.axis_index("tensor")


def greet():
    dp, t = mine()
    barrier = pltpu.get_barrier_semaphore()
    peers = [(flip(dp, 1), t), (dp, flip(t, 1)), (flip(dp, 2), t), (flip(dp, 4), t), (flip(dp, 8), t)]
    for peer in peers:
        pl.semaphore_signal(barrier, inc=1, device_id=peer, device_id_type=MESH)
    pl.semaphore_wait(barrier, len(peers))


def turn(left_ref, turned):
    dp, _ = mine()
    height = turned.shape[0] // 16
    whole = left_ref[...].T
    for piece in range(16):
        spot = 0
        for bit, weight in ((1, 8), (2, 4), (4, 2), (8, 1)):
            own = bit_of(dp, bit)
            spot = spot + weight * (own if piece & bit else 1 - own)
        turned[pl.ds(pl.multiple_of(spot * height, height), height), :] = whole[
            piece * height : (piece + 1) * height
        ]


class Scatter:
    def __init__(self, keep, lands, sems):
        self.keep = keep
        self.lands = lands
        self.sent, self.got = sems

    def copy(self, stage, m):
        dp, t = mine()
        odd = lax.rem(m, 2)
        rows = self.keep.shape[3]
        if stage == 1:
            src, peer = self.keep.at[m, 0], (dp + odd * (flip(dp, 2) - dp), t + (1 - odd) * (1 - 2 * t))
        elif stage == 2:
            src, peer = self.keep.at[m, 1, 0], (dp + (1 - odd) * (flip(dp, 2) - dp), t + odd * (1 - 2 * t))
        elif stage == 3:
            src, peer = self.keep.at[m, 1, 1, pl.ds(0, rows // 2)], (flip(dp, 4), t)
        else:
            src, peer = self.keep.at[m, 1, 1, pl.ds(rows // 2, rows // 4)], (flip(dp, 8), t)
        return pltpu.make_async_remote_copy(
            src_ref=src,
            dst_ref=self.lands[stage - 1].at[m],
            send_sem=self.sent.at[stage, m],
            recv_sem=self.got.at[stage, m],
            device_id=peer,
            device_id_type=MESH,
        )

    def add(self, stage, m):
        rows = self.keep.shape[3]
        self.copy(stage, m).wait_recv()
        land = self.lands[stage - 1]
        if stage == 1:
            self.keep[m, 1] = plus(self.keep[m, 1], land[m])
        elif stage == 2:
            self.keep[m, 1, 1] = plus(self.keep[m, 1, 1], land[m])
        elif stage == 3:
            half = pl.ds(rows // 2, rows // 2)
            self.keep[m, 1, 1, half] = plus(self.keep[m, 1, 1, half], land[m])

    def last(self, m):
        rows = self.keep.shape[3]
        self.copy(4, m).wait_recv()
        rest = pl.ds(3 * rows // 4, rows // 4)
        return self.keep[m, 1, 1, rest].astype(jnp.float32) + self.lands[3][m].astype(jnp.float32)

    def drain(self, m):
        for stage in (1, 2, 3, 4):
            self.copy(stage, m).wait_send()


class Pair:
    def __init__(self, keep, send, land, sems):
        self.keep, self.send, self.land = keep, send, land
        self.sent, self.got = sems

    def copy(self, m):
        dp, t = mine()
        return pltpu.make_async_remote_copy(
            src_ref=self.send.at[lax.rem(m, 2)],
            dst_ref=self.land.at[m],
            send_sem=self.sent.at[0, m],
            recv_sem=self.got.at[0, m],
            device_id=(flip(dp, 1), t),
            device_id_type=MESH,
        )

    def store(self, m, product, own):
        half = product.shape[0] // 2
        rows = half // 2
        odd = lax.rem(m, 2)
        for x in range(2):
            first = odd * x + (1 - odd) * own
            second = odd * own + (1 - odd) * x
            self.send[odd, first, second] = product[x * rows : (x + 1) * rows].astype(jnp.bfloat16)
            self.keep[m, first, second] = product[half + x * rows : half + (x + 1) * rows].astype(
                jnp.bfloat16
            )

    def free(self, m):
        @pl.when(m >= 2)
        def _():
            self.copy(m - 2).wait_send()

    def add(self, m):
        self.copy(m).wait_recv()
        for a in range(2):
            for b in range(2):
                self.keep[m, a, b] = plus(self.keep[m, a, b], self.land[m, a, b])


def plus(left, right):
    return (left.astype(jnp.float32) + right.astype(jnp.float32)).astype(jnp.bfloat16)


def scatter_scratch(chunks, rows, width, pair):
    def buffer(*shape):
        return pltpu.VMEM(shape, jnp.bfloat16)

    out = [buffer(chunks, 2, 2, rows, width)]
    if pair:
        out += [buffer(2, 2, 2, rows, width), buffer(chunks, 2, 2, rows, width)]
    return out


def land_scratch(chunks, rows, width):
    def buffer(*shape):
        return pltpu.VMEM(shape, jnp.bfloat16)

    return [
        buffer(chunks, 2, rows, width),
        buffer(chunks, rows, width),
        buffer(chunks, rows // 2, width),
        buffer(chunks, rows // 4, width),
    ]


def guarded(low, high, m, action):
    @pl.when(jnp.logical_and(m >= low, m < high))
    def _():
        action(m)


def ffn_back_kernel(
    dm_ref, hr_ref, g_own, g_oth, s_own, s_oth, wd_own, wd_oth, wu_own, wu_oth,
    down_ref, bias_ref, up_hbm, dh_hbm,
    dm_turned, hr_turned, total,
    keep_d, send_d, land_d, d1, d2, d3, d4, keep_u, send_u, land_u,
    sent_d, got_d, sent_u, got_u, local_u, local_h,
):
    j = pl.program_id(0)
    chunks = pl.num_programs(0)
    pair_d = Pair(keep_d, send_d, land_d, (sent_d, got_d))
    pair_u = Pair(keep_u, send_u, land_u, (sent_u, got_u))
    scatter = Scatter(keep_d, (d1, d2, d3, d4), (sent_d, got_d))

    @pl.when(j == 0)
    def _():
        greet()
        turn(dm_ref, dm_turned)
        turn(hr_ref, hr_turned)
        total[...] = jnp.zeros_like(total)

    def out_copy(m):
        return pltpu.make_async_copy(keep_u.at[m], up_hbm.at[m], local_u.at[m])

    def finish(m):
        width = keep_d.shape[4]
        down_ref[pl.ds(pl.multiple_of(m * width, width), width), :] = scatter.last(m).T

    def pair_down(m):
        pair_d.add(m)
        scatter.copy(1, m).start()

    def pair_up(m):
        pair_u.add(m)
        out_copy(m).start()

    def step(stage):
        def run(m):
            scatter.add(stage, m)
            scatter.copy(stage + 1, m).start()

        return run

    def tick(n):
        guarded(0, chunks, n - 1, pair_down)
        guarded(0, chunks, n - 1, pair_up)
        guarded(0, chunks, n - 3, step(1))
        guarded(0, chunks, n - 5, step(2))
        guarded(0, chunks, n - 6, step(3))
        guarded(0, chunks, n - 7, finish)

    pair_d.free(j)
    for own, g_ref in ((0, g_oth), (1, g_own)):
        pair_d.store(j, dot(dm_turned[...], g_ref[...]), own)
    pair_d.copy(j).start()
    low = []
    for own, slope, weight in ((0, s_oth, wd_oth), (1, s_own, wd_own)):
        raised = dot_nt(dm_ref[...], weight[...]) * slope[...].astype(jnp.float32)
        low.append(raised.astype(jnp.bfloat16))
        bias_ref[own, pl.ds(j, 1), :] = jnp.sum(low[-1].astype(jnp.float32), axis=0, keepdims=True)
    pair_u.free(j)
    for own in range(2):
        pair_u.store(j, dot(hr_turned[...], low[own]), own)
    pair_u.copy(j).start()
    total[...] += dot_nt(low[0], wu_oth[...]) + dot_nt(low[1], wu_own[...])
    tick(j)

    @pl.when(j == chunks - 1)
    def _():
        out = pltpu.make_async_copy(total, dh_hbm, local_h)
        out.start()

        @pl.loop(0, 7)
        def _(extra):
            tick(chunks + extra)

        for m in range(max(0, CHUNKS - 2), CHUNKS):
            pair_d.copy(m).wait_send()
            pair_u.copy(m).wait_send()

        @pl.loop(0, CHUNKS)
        def _(m):
            scatter.drain(m)
            out_copy(m).wait()

        out.wait()


def ffn_backward(grad_branch, hidden_rows, act, act2, slope, slope2, w_down, w_down2, w_up, w_up2):
    rows, depth = grad_branch.shape
    inner = act.shape[1]
    tile = inner // CHUNKS
    whole = pl.BlockSpec((rows, depth), lambda j: (0, 0))
    column = pl.BlockSpec((rows, tile), lambda j: (0, j))
    row = pl.BlockSpec((tile, depth), lambda j: (j, 0))
    weight_column = pl.BlockSpec((depth, tile), lambda j: (0, j))
    sems = pltpu.SemaphoreType.DMA((5, CHUNKS))
    return pl.pallas_call(
        ffn_back_kernel,
        grid=(CHUNKS,),
        in_specs=[whole, whole, column, column, column, column, row, row, weight_column, weight_column],
        out_specs=[
            pl.BlockSpec((inner, depth // 16), lambda j: (0, 0)),
            pl.BlockSpec((2, CHUNKS, tile), lambda j: (0, 0, 0)),
            pl.BlockSpec(memory_space=pl.ANY),
            pl.BlockSpec(memory_space=pl.ANY),
        ],
        out_shape=[
            jax.ShapeDtypeStruct((inner, depth // 16), jnp.float32),
            jax.ShapeDtypeStruct((2, CHUNKS, tile), jnp.float32),
            jax.ShapeDtypeStruct((CHUNKS, 2, 2, SPAN, tile), jnp.bfloat16),
            jax.ShapeDtypeStruct((rows, depth), jnp.float32),
        ],
        scratch_shapes=[
            pltpu.VMEM((depth, rows), jnp.bfloat16),
            pltpu.VMEM((depth, rows), jnp.bfloat16),
            pltpu.VMEM((rows, depth), jnp.float32),
            *scatter_scratch(CHUNKS, SPAN, tile, True),
            *land_scratch(CHUNKS, SPAN, tile),
            *scatter_scratch(CHUNKS, SPAN, tile, True),
            sems, sems, sems, sems,
            pltpu.SemaphoreType.DMA((CHUNKS,)),
            pltpu.SemaphoreType.DMA,
        ],
        compiler_params=pltpu.CompilerParams(
            vmem_limit_bytes=VMEM, collective_id=1, has_side_effects=True
        ),
        cost_estimate=pl.CostEstimate(
            flops=rows * depth * inner * 16, bytes_accessed=60 * 1024 * 1024, transcendentals=0
        ),
        name="ffn_backward",
    )(grad_branch, hidden_rows, act, act2, slope, slope2, w_down, w_down2, w_up, w_up2)


def attend_back_one(queries, key_rows, values, grad_ctx, levels):
    scale = HEAD_DIM**-0.5
    first = head_masks(128)
    keys_t = key_rows.T
    parts = []
    grad_k = grad_v = None
    for head in range(2):
        mask = first if head == 0 else jnp.logical_not(first)
        picked = jnp.where(mask, queries, jnp.zeros_like(queries))
        grad_picked = jnp.where(mask, grad_ctx, jnp.zeros_like(grad_ctx))
        weights = jnp.exp2(dot_nt(key_rows, picked) * (LOG2E * scale) - levels[head])
        grad_weights = dot_nt(values, grad_picked)
        rowsum = jnp.sum(weights * grad_weights, axis=0, keepdims=True)
        grad_low = (weights * (grad_weights - rowsum)).astype(jnp.bfloat16)
        piece_v = dot(weights.astype(jnp.bfloat16), grad_picked)
        piece_k = dot(grad_low, picked)
        grad_v = piece_v if grad_v is None else grad_v + piece_v
        grad_k = piece_k if grad_k is None else grad_k + piece_k
        parts.append(dot(keys_t[head * HEAD_DIM : (head + 1) * HEAD_DIM], grad_low))
    grad_q = jnp.concatenate(parts, axis=0).T
    return (
        (grad_q * scale).astype(jnp.bfloat16),
        (grad_k * scale).astype(jnp.bfloat16),
        grad_v.astype(jnp.bfloat16),
    )


class Total:
    def __init__(self, sums, lands, sems):
        self.sums, self.lands = sums, lands
        self.sent, self.got = sems

    def copy(self, stage):
        dp, t = mine()
        peer = ((flip(dp, 1), t), (dp, 1 - t), (flip(dp, 2), t), (flip(dp, 4), t), (flip(dp, 8), t))[stage]
        return pltpu.make_async_remote_copy(
            src_ref=self.sums.at[stage],
            dst_ref=self.lands.at[stage],
            send_sem=self.sent.at[stage],
            recv_sem=self.got.at[stage],
            device_id=peer,
            device_id_type=MESH,
        )

    def step(self, stage):
        self.copy(stage).wait_recv()
        self.sums[stage + 1] = self.sums[stage] + self.lands[stage]
        if stage < 4:
            self.copy(stage + 1).start()

    def drain(self):
        for stage in range(5):
            self.copy(stage).wait_send()


def attend_back_kernel(
    da_ref, x_ref, up_hbm, dz_hbm, vec_ref, l_own, l_oth,
    q_own, k_own, v_own, c_own, wo_own, wq_own,
    q_oth, k_oth, v_oth, c_oth, wo_oth, wq_oth,
    gin_hbm, gup_ref, gout_ref, gqkv_ref, vec_out, bias_out,
    da_turned, x_turned, total, stack,
    keep_u, u1, u2, u3, u4,
    keep_a, send_a, land_a, a1, a2, a3, a4,
    vec_sums, vec_lands, bias_sums, bias_lands,
    sent_u, got_u, sent_a, got_a, sent_v, got_v, sent_b, got_b, local_u, local_z, local_g,
):
    g = pl.program_id(0)
    steps = pl.num_programs(0)
    seqs = x_ref.shape[0] // SEQ
    pair = Pair(keep_a, send_a, land_a, (sent_a, got_a))
    scatter_a = Scatter(keep_a, (a1, a2, a3, a4), (sent_a, got_a))
    scatter_u = Scatter(keep_u, (u1, u2, u3, u4), (sent_u, got_u))
    vec_total = Total(vec_sums, vec_lands, (sent_v, got_v))
    bias_total = Total(bias_sums, bias_lands, (sent_b, got_b))

    def load_up(m):
        return pltpu.make_async_copy(up_hbm.at[m], keep_u.at[m], local_u.at[m])

    load_z = pltpu.make_async_copy(dz_hbm, total, local_z)

    @pl.when(g == 0)
    def _():
        for m in range(CHUNKS):
            load_up(m).start()
        load_z.start()
        greet()
        for m in range(CHUNKS):
            load_up(m).wait()
            scatter_u.copy(1, m).start()
        vec_sums[0] = vec_ref[...]
        vec_total.copy(0).start()
        turn(x_ref, x_turned)
        turn(da_ref, da_turned)
        load_z.wait()

    def finish_u(m):
        width = keep_u.shape[4]
        gup_ref[:, pl.ds(pl.multiple_of(m * width, width), width)] = scatter_u.last(m)

    def finish_a(m):
        done = scatter_a.last(m)
        where = lax.div(m, 2)
        width = done.shape[1] // 2
        cols = pl.ds(pl.multiple_of(where * width, width), width)

        @pl.when(lax.rem(m, 2) == 0)
        def _():
            gout_ref[cols, :] = done[:, :width].T
            gqkv_ref[0, :, cols] = done[:, width:]

        @pl.when(lax.rem(m, 2) == 1)
        def _():
            gqkv_ref[1, :, cols] = done[:, :width]
            gqkv_ref[2, :, cols] = done[:, width:]

    def pair_a(m):
        pair.add(m)
        scatter_a.copy(1, m).start()

    def step(scatter, stage):
        def run(m):
            scatter.add(stage, m)
            scatter.copy(stage + 1, m).start()

        return run

    def tick_u(n):
        guarded(0, CHUNKS, n, step(scatter_u, 1))
        guarded(0, CHUNKS, n - 1, step(scatter_u, 2))
        guarded(0, CHUNKS, n - 2, step(scatter_u, 3))
        guarded(0, CHUNKS, n - 3, finish_u)

    def tick_a(n):
        guarded(0, CHUNKS, n, pair_a)
        guarded(0, CHUNKS, n - 2, step(scatter_a, 1))
        guarded(0, CHUNKS, n - 3, step(scatter_a, 2))
        guarded(0, CHUNKS, n - 4, step(scatter_a, 3))
        guarded(0, CHUNKS, n - 5, finish_a)

    _, t = mine()
    sides = (
        (0, q_oth, k_oth, v_oth, c_oth, l_oth, wo_oth),
        (1, q_own, k_own, v_own, c_own, l_own, wo_own),
    )
    for own, q_ref, k_ref, v_ref, _, l_ref, wo_ref in sides:
        grad_ctx = dot_nt(da_ref[...], wo_ref[...]).astype(jnp.bfloat16)
        for s in range(seqs):
            rows = slice(s * SEQ, (s + 1) * SEQ)
            levels = [l_ref[s, pl.ds(2 * g + head, 1), :] for head in range(2)]
            grads = attend_back_one(
                q_ref[rows, :], k_ref[rows, :], v_ref[rows, :], grad_ctx[rows], levels
            )
            for kind in range(3):
                stack[rows, (own * 3 + kind) * 128 : (own * 3 + kind + 1) * 128] = grads[kind]
        spot = t * own + (1 - t) * (1 - own)
        for kind, base in ((0, 0), (2, 8)):
            piece = stack[:, (own * 3 + kind) * 128 : (own * 3 + kind + 1) * 128]
            bias_sums[0, pl.ds(base + spot * 4 + g, 1), :] = jnp.sum(
                piece.astype(jnp.float32), axis=0, keepdims=True
            )
        tick_u(3 * g + own)
    pair.free(2 * g)
    for own, _, _, _, c_ref, _, _ in sides:
        first = dot(da_turned[...], c_ref[...])
        second = dot(x_turned[...], stack[:, own * 384 : own * 384 + 128])
        pair.store(2 * g, jnp.concatenate([first, second], axis=1), own)
    pair.copy(2 * g).start()
    pair.free(2 * g + 1)
    for own in range(2):
        pair.store(2 * g + 1, dot(x_turned[...], stack[:, own * 384 + 128 : own * 384 + 384]), own)
    pair.copy(2 * g + 1).start()
    weights = [wq_oth[kind] for kind in range(3)] + [wq_own[kind] for kind in range(3)]
    total[...] += dot_nt(stack[...], jnp.concatenate(weights, axis=1))
    tick_u(3 * g + 2)
    tick_a(2 * g)
    tick_a(2 * g + 1)
    for stage in range(3):
        @pl.when(g == stage + 1)
        def _():
            vec_total.step(stage)

    @pl.when(g == steps - 1)
    def _():
        bias_total.copy(0).start()
        out = pltpu.make_async_copy(total, gin_hbm, local_g)
        out.start()
        vec_total.step(3)
        for extra in range(5):
            tick_a(jnp.int32(CHUNKS + extra))
            bias_total.step(extra)
            if extra == 0:
                vec_total.step(4)
        vec_out[...] = vec_sums[5]
        bias_out[...] = bias_sums[5]
        for m in range(CHUNKS - 2, CHUNKS):
            pair.copy(m).wait_send()

        @pl.loop(0, CHUNKS)
        def _(m):
            scatter_u.drain(m)
            scatter_a.drain(m)

        vec_total.drain()
        bias_total.drain()
        out.wait()


def attend_backward(grad_attended, tokens, keep_up, grad_one, vectors, own, other):
    rows, depth = tokens.shape
    width = own[0].shape[1]
    steps = width // 128
    inner = keep_up.shape[0] * keep_up.shape[4]
    fixed = lambda *shape: pl.BlockSpec(shape, lambda g: (0,) * len(shape))
    anywhere = pl.BlockSpec(memory_space=pl.ANY)
    column = pl.BlockSpec((rows, 128), lambda g: (0, g))
    side = [column] * 4 + [
        pl.BlockSpec((128, depth), lambda g: (g, 0)),
        pl.BlockSpec((3, depth, 128), lambda g: (0, 0, g)),
    ]
    sems = pltpu.SemaphoreType.DMA((5, CHUNKS))
    few = pltpu.SemaphoreType.DMA((5,))
    n_vec = vectors.shape[0]
    f32 = jnp.float32
    return pl.pallas_call(
        attend_back_kernel,
        grid=(steps,),
        in_specs=[
            fixed(rows, depth), fixed(rows, depth), anywhere, anywhere, fixed(n_vec, 128),
            fixed(*own[4].shape), fixed(*other[4].shape),
        ] + side + side,
        out_specs=[
            anywhere, fixed(depth // 16, inner), fixed(width, depth // 16),
            fixed(3, depth // 16, width), fixed(n_vec, 128), fixed(16, 128),
        ],
        out_shape=[
            jax.ShapeDtypeStruct((rows, depth), f32),
            jax.ShapeDtypeStruct((depth // 16, inner), f32),
            jax.ShapeDtypeStruct((width, depth // 16), f32),
            jax.ShapeDtypeStruct((3, depth // 16, width), f32),
            jax.ShapeDtypeStruct((n_vec, 128), f32),
            jax.ShapeDtypeStruct((16, 128), f32),
        ],
        scratch_shapes=[
            pltpu.VMEM((depth, rows), jnp.bfloat16),
            pltpu.VMEM((depth, rows), jnp.bfloat16),
            pltpu.VMEM((rows, depth), f32),
            pltpu.VMEM((rows, 768), jnp.bfloat16),
            *scatter_scratch(CHUNKS, SPAN, 256, False),
            *land_scratch(CHUNKS, SPAN, 256),
            *scatter_scratch(CHUNKS, SPAN, 256, True),
            *land_scratch(CHUNKS, SPAN, 256),
            pltpu.VMEM((6, n_vec, 128), f32),
            pltpu.VMEM((5, n_vec, 128), f32),
            pltpu.VMEM((6, 16, 128), f32),
            pltpu.VMEM((5, 16, 128), f32),
            sems, sems, sems, sems, few, few, few, few,
            pltpu.SemaphoreType.DMA((CHUNKS,)),
            pltpu.SemaphoreType.DMA,
            pltpu.SemaphoreType.DMA,
        ],
        compiler_params=pltpu.CompilerParams(
            vmem_limit_bytes=VMEM, collective_id=2, has_side_effects=True
        ),
        cost_estimate=pl.CostEstimate(
            flops=rows * depth * width * 40, bytes_accessed=60 * 1024 * 1024, transcendentals=0
        ),
        name="attend_backward",
    )(
        grad_attended, tokens, keep_up, grad_one, vectors, own[4], other[4],
        *own[:4], own[5], own[6], *other[:4], other[5], other[6],
    )


def body(mesh, *args):
    tokens, w_qkv = args[0], args[2]
    n_dp, n_tensor = mesh.shape["dp"], mesh.shape["tensor"]
    local = (tokens.shape[0] % SEQ, w_qkv.shape[2], args[9].shape[1])
    if (n_dp, n_tensor) == (16, 2) and local == (0, 512, 2048):
        return body_tokens(*args)
    return body_tensor(*args)


def body_tokens(
    tokens,
    cotangent,
    w_qkv,
    bias_q,
    bias_v,
    w_out,
    bias_o,
    gain_one,
    shift_one,
    w_up,
    bias_up,
    w_down,
    bias_down,
    gain_two,
    shift_two,
):
    me_dp, me_t = lax.axis_index("dp"), lax.axis_index("tensor")
    core = me_dp % 2

    def swap(value, dp_bit=0, tensor_bit=0):
        pairs = [
            ((d * 2 + t), ((d ^ dp_bit) * 2 + (t ^ tensor_bit))) for d in range(16) for t in range(2)
        ]
        return lax.ppermute(value, AXES, pairs)

    def other_half(weight, axis):
        size = weight.shape[axis] // 2
        mine = lax.dynamic_slice_in_dim(weight, core * size, size, axis)
        mine = swap(mine, tensor_bit=1)
        theirs = swap(mine, dp_bit=1)
        return jnp.where(
            core == 0,
            jnp.concatenate([mine, theirs], axis),
            jnp.concatenate([theirs, mine], axis),
        )

    widths = (bias_q.shape[0], bias_v.shape[0], bias_up.shape[0])
    biases = swap(jnp.concatenate([bias_q, bias_v, bias_up]), tensor_bit=1)
    bias_q2 = biases[: widths[0]]
    bias_v2 = biases[widths[0] : widths[0] + widths[1]]
    bias_up2 = biases[widths[0] + widths[1] :]
    w_qkv2 = other_half(w_qkv, 1)
    w_out2 = other_half(w_out, 0)
    w_up2 = other_half(w_up, 0)
    w_down2 = other_half(w_down, 0)

    halves = ((w_qkv, bias_q, bias_v), (w_qkv2, bias_q2, bias_v2))
    kept = []
    for weight, b_q, b_v in halves:
        queries = (dot(tokens, weight[0]) + b_q).astype(jnp.bfloat16)
        key_rows = dot(tokens, weight[1]).astype(jnp.bfloat16)
        values = (dot(tokens, weight[2]) + b_v).astype(jnp.bfloat16)
        context, level = attend_forward(queries, key_rows, values)
        kept.append((queries, key_rows, values, level, context))
    ctx, ctx2 = kept[0][4], kept[1][4]
    attended = dot(ctx, w_out) + dot(ctx2, w_out2) + bias_o
    hidden_one, normed_one, scaled_one = norm_forward(
        tokens.astype(jnp.float32) + attended, gain_one, shift_one
    )
    hidden_rows = hidden_one.astype(jnp.bfloat16)

    def expand(weight, bias):
        activated, slope = gelu_pair(dot(hidden_rows, weight) + bias)
        return activated.astype(jnp.bfloat16), slope.astype(jnp.bfloat16)

    active, slope = expand(w_up, bias_up)
    active2, slope2 = expand(w_up2, bias_up2)
    branch = dot(active, w_down) + dot(active2, w_down2) + bias_down
    result, normed_two, scaled_two = norm_forward(hidden_one + branch, gain_two, shift_two)
    upstream = cotangent.astype(jnp.float32)
    grad_two = norm_backward(upstream, gain_two, normed_two, scaled_two)
    grad_branch = grad_two.astype(jnp.bfloat16)

    grad_down, bias_up_parts, keep_up, raised = ffn_backward(
        grad_branch, hidden_rows, active, active2, slope, slope2, w_down, w_down2, w_up, w_up2
    )
    grad_hidden = grad_two + raised
    grad_one = norm_backward(grad_hidden, gain_one, normed_one, scaled_one)
    grad_attended = grad_one.astype(jnp.bfloat16)
    bias_parts = bias_up_parts.reshape(2, -1)
    bias_parts = jnp.where(me_t == 0, bias_parts[::-1], bias_parts)
    vectors = jnp.concatenate(
        [
            jnp.sum(upstream, axis=0),
            jnp.sum(upstream * normed_two, axis=0),
            jnp.sum(grad_branch.astype(jnp.float32), axis=0),
            bias_parts.reshape(-1),
            jnp.sum(grad_hidden, axis=0),
            jnp.sum(grad_hidden * normed_one, axis=0),
            jnp.sum(grad_attended.astype(jnp.float32), axis=0),
        ]
    )
    (q1, k1, v1, l1, c1), (q2, k2, v2, l2, c2) = kept
    grad_input, grad_up, grad_out, grad_qkv, vectors, biases = attend_backward(
        grad_attended,
        tokens,
        keep_up,
        grad_one,
        vectors.reshape(-1, 128),
        (q1, k1, v1, c1, l1, w_out, w_qkv),
        (q2, k2, v2, c2, l2, w_out2, w_qkv2),
    )
    vectors = vectors.reshape(-1)
    d, at, pieces = tokens.shape[1], 0, []
    for size in (d, d, d, bias_parts.size, d, d, d):
        pieces.append(vectors[at : at + size])
        at += size
    g_shift_two, g_gain_two, g_bias_down, g_bias_up, g_shift_one, g_gain_one, g_bias_o = pieces
    g_bias_q, g_bias_v = biases[:8].reshape(-1), biases[8:].reshape(-1)
    return (
        result.astype(jnp.bfloat16),
        grad_input,
        grad_qkv,
        g_bias_q,
        g_bias_v,
        grad_out,
        g_bias_o,
        g_gain_one,
        g_shift_one,
        grad_up,
        g_bias_up,
        grad_down,
        g_bias_down,
        g_gain_two,
        g_shift_two,
    )


def solution(mesh):
    in_specs = (
        P(("dp", "tensor"), None),
        P(("dp", "tensor"), None),
        P(None, None, "tensor"),
        P("tensor"),
        P("tensor"),
        P("tensor", None),
        P(),
        P(),
        P(),
        P(None, "tensor"),
        P("tensor"),
        P("tensor", None),
        P(),
        P(),
        P(),
    )
    out_specs = (
        P(("dp", "tensor"), None),
        P(("dp", "tensor"), None),
        P(None, "dp", "tensor"),
        P(),
        P(),
        P("tensor", "dp"),
        P(),
        P(),
        P(),
        P("dp", "tensor"),
        P(),
        P("tensor", "dp"),
        P(),
        P(),
        P(),
    )
    return jax.shard_map(functools.partial(body, mesh), mesh=mesh, in_specs=in_specs, out_specs=out_specs, check_vma=False)
```

```python
import functools

import jax
import jax.numpy as jnp
from jax import lax
from jax.experimental import pallas as pl
from jax.experimental.pallas import tpu as pltpu
from jax.sharding import PartitionSpec as P

D = 1024
FF = 4096
HEAD_DIM = 64
SEQ = 512


def gelu_pair(inner_pre):
    normal_cdf = 0.5 * (1.0 + jax.scipy.special.erf(inner_pre * 0.7071067811865476))
    density = jnp.exp(-0.5 * inner_pre * inner_pre) * 0.3989422804014327
    return (inner_pre * normal_cdf, normal_cdf + inner_pre * density)


def norm_forward(summed, gain, shift):
    centre = summed - jnp.mean(summed, axis=-1, keepdims=True)
    scaled = lax.rsqrt(jnp.mean(centre * centre, axis=-1, keepdims=True) + 1e-05)
    normed = centre * scaled
    return (normed * gain + shift, normed, scaled)


def norm_backward(upstream, gain, normed, scaled):
    grad_norm = upstream * gain
    return scaled * (
        grad_norm
        - jnp.mean(grad_norm, axis=-1, keepdims=True)
        - normed * jnp.mean(grad_norm * normed, axis=-1, keepdims=True)
    )


def attend_block(block):
    queries, key_rows, values = block
    scores = jnp.einsum(
        "qhd,khd->hqk", queries, key_rows, preferred_element_type=jnp.float32
    ) * HEAD_DIM ** (-0.5)
    peak_score = jnp.max(scores, axis=-1, keepdims=True)
    lifted = jnp.exp(scores - peak_score)
    totals = jnp.sum(lifted, axis=-1, keepdims=True)
    weights = (lifted / totals).astype(jnp.bfloat16)
    context = jnp.einsum("hqk,khd->qhd", weights, values, preferred_element_type=jnp.float32)
    return (context.astype(jnp.bfloat16), (peak_score + jnp.log(totals))[..., 0])


def attend_back(block):
    queries, key_rows, values, logsum, grad_ctx = block
    scale = HEAD_DIM ** (-0.5)
    scores = (
        jnp.einsum("qhd,khd->hqk", queries, key_rows, preferred_element_type=jnp.float32) * scale
    )
    weights = jnp.exp(scores - logsum[..., None])
    grad_weights = jnp.einsum("qhd,khd->hqk", grad_ctx, values, preferred_element_type=jnp.float32)
    grad_scores = weights * (grad_weights - jnp.sum(weights * grad_weights, axis=-1, keepdims=True))
    grad_low = grad_scores.astype(jnp.bfloat16)
    grad_v = jnp.einsum(
        "hqk,qhd->khd", weights.astype(jnp.bfloat16), grad_ctx, preferred_element_type=jnp.float32
    )
    grad_q = (
        jnp.einsum("hqk,khd->qhd", grad_low, key_rows, preferred_element_type=jnp.float32) * scale
    )
    grad_k = (
        jnp.einsum("hqk,qhd->khd", grad_low, queries, preferred_element_type=jnp.float32) * scale
    )
    return (grad_q.astype(jnp.bfloat16), grad_k.astype(jnp.bfloat16), grad_v.astype(jnp.bfloat16))


def body_tensor(
    tokens,
    cotangent,
    w_qkv,
    bias_q,
    bias_v,
    w_out,
    bias_o,
    gain_one,
    shift_one,
    w_up,
    bias_up,
    w_down,
    bias_down,
    gain_two,
    shift_two,
):
    rank = lax.axis_index("tensor")
    full_rows = lax.all_gather(tokens, "tensor", axis=0, tiled=True)
    group_rows = full_rows.shape[0]
    local_width = w_qkv.shape[2]
    head_shape = (group_rows // SEQ, SEQ, local_width // HEAD_DIM, HEAD_DIM)
    projected = jnp.einsum("td,kde->kte", full_rows, w_qkv, preferred_element_type=jnp.float32)
    queries = (projected[0] + bias_q).astype(jnp.bfloat16).reshape(head_shape)
    key_rows = projected[1].astype(jnp.bfloat16).reshape(head_shape)
    values = (projected[2] + bias_v).astype(jnp.bfloat16).reshape(head_shape)
    context, logsum = lax.map(attend_block, (queries, key_rows, values))
    context = context.reshape(group_rows, local_width)
    attended = (
        lax.psum_scatter(
            jnp.dot(context, w_out, preferred_element_type=jnp.float32),
            "tensor",
            scatter_dimension=0,
            tiled=True,
        )
        + bias_o
    )
    hidden_one, normed_one, scaled_one = norm_forward(
        tokens.astype(jnp.float32) + attended, gain_one, shift_one
    )
    hidden_rows = lax.all_gather(hidden_one.astype(jnp.bfloat16), "tensor", axis=0, tiled=True)
    inner_pre = jnp.dot(hidden_rows, w_up, preferred_element_type=jnp.float32) + bias_up
    activated, slope = gelu_pair(inner_pre)
    active_low = activated.astype(jnp.bfloat16)
    branch = (
        lax.psum_scatter(
            jnp.dot(active_low, w_down, preferred_element_type=jnp.float32),
            "tensor",
            scatter_dimension=0,
            tiled=True,
        )
        + bias_down
    )
    result, normed_two, scaled_two = norm_forward(hidden_one + branch, gain_two, shift_two)
    upstream = cotangent.astype(jnp.float32)
    grad_two = norm_backward(upstream, gain_two, normed_two, scaled_two)
    grad_branch = grad_two.astype(jnp.bfloat16)
    branch_rows = lax.all_gather(grad_branch, "tensor", axis=0, tiled=True)
    grad_down = jnp.einsum("tf,td->fd", active_low, branch_rows, preferred_element_type=jnp.float32)
    grad_inner = (
        jnp.einsum("td,fd->tf", branch_rows, w_down, preferred_element_type=jnp.float32) * slope
    ).astype(jnp.bfloat16)
    grad_up = jnp.einsum("td,tf->df", hidden_rows, grad_inner, preferred_element_type=jnp.float32)
    grad_hidden = grad_two + lax.psum_scatter(
        jnp.einsum("tf,df->td", grad_inner, w_up, preferred_element_type=jnp.float32),
        "tensor",
        scatter_dimension=0,
        tiled=True,
    )
    grad_one = norm_backward(grad_hidden, gain_one, normed_one, scaled_one)
    grad_attended = grad_one.astype(jnp.bfloat16)
    attended_rows = lax.all_gather(grad_attended, "tensor", axis=0, tiled=True)
    grad_out = jnp.einsum("te,td->ed", context, attended_rows, preferred_element_type=jnp.float32)
    grad_context = jnp.einsum(
        "td,ed->te", attended_rows, w_out, preferred_element_type=jnp.float32
    ).astype(jnp.bfloat16)
    grad_q, grad_k, grad_v = lax.map(
        attend_back, (queries, key_rows, values, logsum, grad_context.reshape(head_shape))
    )
    grad_stack = jnp.stack(
        [
            grad_q.reshape(group_rows, local_width),
            grad_k.reshape(group_rows, local_width),
            grad_v.reshape(group_rows, local_width),
        ]
    )
    weight_qkv = jnp.einsum(
        "td,kte->kde", full_rows, grad_stack, preferred_element_type=jnp.float32
    )
    grad_input = grad_one + lax.psum_scatter(
        jnp.einsum("kte,kde->td", grad_stack, w_qkv, preferred_element_type=jnp.float32).astype(
            jnp.bfloat16
        ),
        "tensor",
        scatter_dimension=0,
        tiled=True,
    ).astype(jnp.float32)

    def placed(piece, length):
        return lax.dynamic_update_slice_in_dim(
            jnp.zeros((length,), jnp.float32), piece, rank * piece.shape[0], 0
        )

    vectors = lax.psum(
        (
            placed(jnp.sum(grad_stack[0].astype(jnp.float32), axis=0), D),
            placed(jnp.sum(grad_stack[2].astype(jnp.float32), axis=0), D),
            jnp.sum(grad_attended.astype(jnp.float32), axis=0),
            jnp.sum(grad_hidden * normed_one, axis=0),
            jnp.sum(grad_hidden, axis=0),
            placed(jnp.sum(grad_inner.astype(jnp.float32), axis=0), FF),
            jnp.sum(grad_branch.astype(jnp.float32), axis=0),
            jnp.sum(upstream * normed_two, axis=0),
            jnp.sum(upstream, axis=0),
        ),
        ("dp", "tensor"),
    )
    weight_parts = (
        lax.psum_scatter(
            weight_qkv.astype(jnp.bfloat16), "dp", scatter_dimension=1, tiled=True
        ).astype(jnp.float32),
        lax.psum_scatter(
            grad_out.astype(jnp.bfloat16), "dp", scatter_dimension=1, tiled=True
        ).astype(jnp.float32),
        lax.psum_scatter(
            grad_up.astype(jnp.bfloat16), "dp", scatter_dimension=0, tiled=True
        ).astype(jnp.float32),
        lax.psum_scatter(
            grad_down.astype(jnp.bfloat16), "dp", scatter_dimension=1, tiled=True
        ).astype(jnp.float32),
    )
    return (
        result.astype(jnp.bfloat16),
        grad_input,
        weight_parts[0],
        vectors[0],
        vectors[1],
        weight_parts[1],
        vectors[2],
        vectors[3],
        vectors[4],
        weight_parts[2],
        vectors[5],
        weight_parts[3],
        vectors[6],
        vectors[7],
        vectors[8],
    )


AXES = ("dp", "tensor")
LOG2E = 1.4426950408889634
VMEM = 56 * 1024 * 1024
NT = (((1,), (1,)), ((), ()))


def dot(left, right):
    return jnp.dot(left, right, preferred_element_type=jnp.float32)


def dot_nt(left, right):
    return lax.dot_general(left, right, NT, preferred_element_type=jnp.float32)


def head_masks(width):
    lane = lax.broadcasted_iota(jnp.int32, (1, width), 1)
    return lane < HEAD_DIM


MESH = pl.DeviceIdType.MESH
CHUNKS = 8
SPAN = 256


def bit_of(index, bit):
    return lax.rem(lax.div(index, bit), 2)


def flip(index, bit):
    return index + bit - 2 * bit * bit_of(index, bit)


def mine():
    return lax.axis_index("dp"), lax.axis_index("tensor")


def greet():
    dp, t = mine()
    barrier = pltpu.get_barrier_semaphore()
    peers = [(flip(dp, 1), t), (dp, flip(t, 1)), (flip(dp, 2), t), (flip(dp, 4), t), (flip(dp, 8), t)]
    for peer in peers:
        pl.semaphore_signal(barrier, inc=1, device_id=peer, device_id_type=MESH)
    pl.semaphore_wait(barrier, len(peers))


def turn(left_ref, turned):
    dp, _ = mine()
    height = turned.shape[0] // 16
    whole = left_ref[...].T
    for piece in range(16):
        spot = 0
        for bit, weight in ((1, 8), (2, 4), (4, 2), (8, 1)):
            own = bit_of(dp, bit)
            spot = spot + weight * (own if piece & bit else 1 - own)
        turned[pl.ds(pl.multiple_of(spot * height, height), height), :] = whole[
            piece * height : (piece + 1) * height
        ]


class Scatter:
    def __init__(self, keep, lands, sems):
        self.keep = keep
        self.lands = lands
        self.sent, self.got = sems

    def copy(self, stage, m):
        dp, t = mine()
        odd = lax.rem(m, 2)
        rows = self.keep.shape[3]
        if stage == 1:
            src, peer = self.keep.at[m, 0], (dp + odd * (flip(dp, 2) - dp), t + (1 - odd) * (1 - 2 * t))
        elif stage == 2:
            src, peer = self.keep.at[m, 1, 0], (dp + (1 - odd) * (flip(dp, 2) - dp), t + odd * (1 - 2 * t))
        elif stage == 3:
            src, peer = self.keep.at[m, 1, 1, pl.ds(0, rows // 2)], (flip(dp, 4), t)
        else:
            src, peer = self.keep.at[m, 1, 1, pl.ds(rows // 2, rows // 4)], (flip(dp, 8), t)
        return pltpu.make_async_remote_copy(
            src_ref=src,
            dst_ref=self.lands[stage - 1].at[m],
            send_sem=self.sent.at[stage, m],
            recv_sem=self.got.at[stage, m],
            device_id=peer,
            device_id_type=MESH,
        )

    def add(self, stage, m):
        rows = self.keep.shape[3]
        self.copy(stage, m).wait_recv()
        land = self.lands[stage - 1]
        if stage == 1:
            self.keep[m, 1] = plus(self.keep[m, 1], land[m])
        elif stage == 2:
            self.keep[m, 1, 1] = plus(self.keep[m, 1, 1], land[m])
        elif stage == 3:
            half = pl.ds(rows // 2, rows // 2)
            self.keep[m, 1, 1, half] = plus(self.keep[m, 1, 1, half], land[m])

    def last(self, m):
        rows = self.keep.shape[3]
        self.copy(4, m).wait_recv()
        rest = pl.ds(3 * rows // 4, rows // 4)
        return self.keep[m, 1, 1, rest].astype(jnp.float32) + self.lands[3][m].astype(jnp.float32)

    def drain(self, m):
        for stage in (1, 2, 3, 4):
            self.copy(stage, m).wait_send()


class Pair:
    def __init__(self, keep, send, land, sems):
        self.keep, self.send, self.land = keep, send, land
        self.sent, self.got = sems

    def copy(self, m):
        dp, t = mine()
        return pltpu.make_async_remote_copy(
            src_ref=self.send.at[lax.rem(m, 2)],
            dst_ref=self.land.at[m],
            send_sem=self.sent.at[0, m],
            recv_sem=self.got.at[0, m],
            device_id=(flip(dp, 1), t),
            device_id_type=MESH,
        )

    def store(self, m, product, own):
        half = product.shape[0] // 2
        rows = half // 2
        odd = lax.rem(m, 2)
        for x in range(2):
            first = odd * x + (1 - odd) * own
            second = odd * own + (1 - odd) * x
            self.send[odd, first, second] = product[x * rows : (x + 1) * rows].astype(jnp.bfloat16)
            self.keep[m, first, second] = product[half + x * rows : half + (x + 1) * rows].astype(
                jnp.bfloat16
            )

    def free(self, m):
        @pl.when(m >= 2)
        def _():
            self.copy(m - 2).wait_send()

    def add(self, m):
        self.copy(m).wait_recv()
        for a in range(2):
            for b in range(2):
                self.keep[m, a, b] = plus(self.keep[m, a, b], self.land[m, a, b])


def plus(left, right):
    return (left.astype(jnp.float32) + right.astype(jnp.float32)).astype(jnp.bfloat16)


def scatter_scratch(chunks, rows, width, pair):
    def buffer(*shape):
        return pltpu.VMEM(shape, jnp.bfloat16)

    out = [buffer(chunks, 2, 2, rows, width)]
    if pair:
        out += [buffer(2, 2, 2, rows, width), buffer(chunks, 2, 2, rows, width)]
    return out


def land_scratch(chunks, rows, width):
    def buffer(*shape):
        return pltpu.VMEM(shape, jnp.bfloat16)

    return [
        buffer(chunks, 2, rows, width),
        buffer(chunks, rows, width),
        buffer(chunks, rows // 2, width),
        buffer(chunks, rows // 4, width),
    ]


def guarded(low, high, m, action):
    @pl.when(jnp.logical_and(m >= low, m < high))
    def _():
        action(m)


def ffn_back_kernel(
    dm_ref, hr_ref, g_own, g_oth, s_own, s_oth, wd_own, wd_oth, wu_own, wu_oth,
    down_ref, bias_ref, up_hbm, dh_hbm,
    dm_turned, hr_turned, total,
    keep_d, send_d, land_d, d1, d2, d3, d4, keep_u, send_u, land_u,
    sent_d, got_d, sent_u, got_u, local_u, local_h,
):
    j = pl.program_id(0)
    chunks = pl.num_programs(0)
    pair_d = Pair(keep_d, send_d, land_d, (sent_d, got_d))
    pair_u = Pair(keep_u, send_u, land_u, (sent_u, got_u))
    scatter = Scatter(keep_d, (d1, d2, d3, d4), (sent_d, got_d))

    @pl.when(j == 0)
    def _():
        greet()
        turn(dm_ref, dm_turned)
        turn(hr_ref, hr_turned)
        total[...] = jnp.zeros_like(total)

    def out_copy(m):
        return pltpu.make_async_copy(keep_u.at[m], up_hbm.at[m], local_u.at[m])

    def finish(m):
        width = keep_d.shape[4]
        down_ref[pl.ds(pl.multiple_of(m * width, width), width), :] = scatter.last(m).T

    def pair_down(m):
        pair_d.add(m)
        scatter.copy(1, m).start()

    def pair_up(m):
        pair_u.add(m)
        out_copy(m).start()

    def step(stage):
        def run(m):
            scatter.add(stage, m)
            scatter.copy(stage + 1, m).start()

        return run

    def tick(n):
        guarded(0, chunks, n - 1, pair_down)
        guarded(0, chunks, n - 1, pair_up)
        guarded(0, chunks, n - 3, step(1))
        guarded(0, chunks, n - 5, step(2))
        guarded(0, chunks, n - 6, step(3))
        guarded(0, chunks, n - 7, finish)

    pair_d.free(j)
    for own, g_ref in ((0, g_oth), (1, g_own)):
        pair_d.store(j, dot(dm_turned[...], g_ref[...]), own)
    pair_d.copy(j).start()
    low = []
    for own, slope, weight in ((0, s_oth, wd_oth), (1, s_own, wd_own)):
        raised = dot_nt(dm_ref[...], weight[...]) * slope[...].astype(jnp.float32)
        low.append(raised.astype(jnp.bfloat16))
        bias_ref[own, pl.ds(j, 1), :] = jnp.sum(low[-1].astype(jnp.float32), axis=0, keepdims=True)
    pair_u.free(j)
    for own in range(2):
        pair_u.store(j, dot(hr_turned[...], low[own]), own)
    pair_u.copy(j).start()
    total[...] += dot_nt(low[0], wu_oth[...]) + dot_nt(low[1], wu_own[...])
    tick(j)

    @pl.when(j == chunks - 1)
    def _():
        out = pltpu.make_async_copy(total, dh_hbm, local_h)
        out.start()

        @pl.loop(0, 7)
        def _(extra):
            tick(chunks + extra)

        for m in range(max(0, CHUNKS - 2), CHUNKS):
            pair_d.copy(m).wait_send()
            pair_u.copy(m).wait_send()

        @pl.loop(0, CHUNKS)
        def _(m):
            scatter.drain(m)
            out_copy(m).wait()

        out.wait()


def ffn_backward(grad_branch, hidden_rows, act, act2, slope, slope2, w_down, w_down2, w_up, w_up2):
    rows, depth = grad_branch.shape
    inner = act.shape[1]
    tile = inner // CHUNKS
    whole = pl.BlockSpec((rows, depth), lambda j: (0, 0))
    column = pl.BlockSpec((rows, tile), lambda j: (0, j))
    row = pl.BlockSpec((tile, depth), lambda j: (j, 0))
    weight_column = pl.BlockSpec((depth, tile), lambda j: (0, j))
    sems = pltpu.SemaphoreType.DMA((5, CHUNKS))
    return pl.pallas_call(
        ffn_back_kernel,
        grid=(CHUNKS,),
        in_specs=[whole, whole, column, column, column, column, row, row, weight_column, weight_column],
        out_specs=[
            pl.BlockSpec((inner, depth // 16), lambda j: (0, 0)),
            pl.BlockSpec((2, CHUNKS, tile), lambda j: (0, 0, 0)),
            pl.BlockSpec(memory_space=pl.ANY),
            pl.BlockSpec(memory_space=pl.ANY),
        ],
        out_shape=[
            jax.ShapeDtypeStruct((inner, depth // 16), jnp.float32),
            jax.ShapeDtypeStruct((2, CHUNKS, tile), jnp.float32),
            jax.ShapeDtypeStruct((CHUNKS, 2, 2, SPAN, tile), jnp.bfloat16),
            jax.ShapeDtypeStruct((rows, depth), jnp.float32),
        ],
        scratch_shapes=[
            pltpu.VMEM((depth, rows), jnp.bfloat16),
            pltpu.VMEM((depth, rows), jnp.bfloat16),
            pltpu.VMEM((rows, depth), jnp.float32),
            *scatter_scratch(CHUNKS, SPAN, tile, True),
            *land_scratch(CHUNKS, SPAN, tile),
            *scatter_scratch(CHUNKS, SPAN, tile, True),
            sems, sems, sems, sems,
            pltpu.SemaphoreType.DMA((CHUNKS,)),
            pltpu.SemaphoreType.DMA,
        ],
        compiler_params=pltpu.CompilerParams(
            vmem_limit_bytes=VMEM, collective_id=1, has_side_effects=True
        ),
        cost_estimate=pl.CostEstimate(
            flops=rows * depth * inner * 16, bytes_accessed=60 * 1024 * 1024, transcendentals=0
        ),
        name="ffn_backward",
    )(grad_branch, hidden_rows, act, act2, slope, slope2, w_down, w_down2, w_up, w_up2)


def attend_back_one(queries, key_rows, values, grad_ctx, levels):
    scale = HEAD_DIM**-0.5
    first = head_masks(128)
    keys_t = key_rows.T
    parts = []
    grad_k = grad_v = None
    for head in range(2):
        mask = first if head == 0 else jnp.logical_not(first)
        picked = jnp.where(mask, queries, jnp.zeros_like(queries))
        grad_picked = jnp.where(mask, grad_ctx, jnp.zeros_like(grad_ctx))
        weights = jnp.exp2(dot_nt(key_rows, picked) * (LOG2E * scale) - levels[head])
        grad_weights = dot_nt(values, grad_picked)
        rowsum = jnp.sum(weights * grad_weights, axis=0, keepdims=True)
        grad_low = (weights * (grad_weights - rowsum)).astype(jnp.bfloat16)
        piece_v = dot(weights.astype(jnp.bfloat16), grad_picked)
        piece_k = dot(grad_low, picked)
        grad_v = piece_v if grad_v is None else grad_v + piece_v
        grad_k = piece_k if grad_k is None else grad_k + piece_k
        parts.append(dot(keys_t[head * HEAD_DIM : (head + 1) * HEAD_DIM], grad_low))
    grad_q = jnp.concatenate(parts, axis=0).T
    return (
        (grad_q * scale).astype(jnp.bfloat16),
        (grad_k * scale).astype(jnp.bfloat16),
        grad_v.astype(jnp.bfloat16),
    )


class Total:
    def __init__(self, sums, lands, sems):
        self.sums, self.lands = sums, lands
        self.sent, self.got = sems

    def copy(self, stage):
        dp, t = mine()
        peer = ((flip(dp, 1), t), (dp, 1 - t), (flip(dp, 2), t), (flip(dp, 4), t), (flip(dp, 8), t))[stage]
        return pltpu.make_async_remote_copy(
            src_ref=self.sums.at[stage],
            dst_ref=self.lands.at[stage],
            send_sem=self.sent.at[stage],
            recv_sem=self.got.at[stage],
            device_id=peer,
            device_id_type=MESH,
        )

    def step(self, stage):
        self.copy(stage).wait_recv()
        self.sums[stage + 1] = self.sums[stage] + self.lands[stage]
        if stage < 4:
            self.copy(stage + 1).start()

    def drain(self):
        for stage in range(5):
            self.copy(stage).wait_send()


def attend_back_kernel(
    da_ref, x_ref, up_hbm, dz_hbm, vec_ref, level_ref,
    qkv_own, c_own, wo_own, wq_own,
    qkv_oth, c_oth, wo_oth, wq_oth,
    gin_hbm, gup_ref, gout_ref, gqkv_ref, vec_out, bias_out,
    da_turned, x_turned, total, stack,
    keep_u, u1, u2, u3, u4,
    keep_a, send_a, land_a, a1, a2, a3, a4,
    vec_sums, vec_lands, bias_sums, bias_lands,
    sent_u, got_u, sent_a, got_a, sent_v, got_v, sent_b, got_b, local_u, local_z, local_g,
):
    g = pl.program_id(0)
    steps = pl.num_programs(0)
    seqs = x_ref.shape[0] // SEQ
    pair = Pair(keep_a, send_a, land_a, (sent_a, got_a))
    scatter_a = Scatter(keep_a, (a1, a2, a3, a4), (sent_a, got_a))
    scatter_u = Scatter(keep_u, (u1, u2, u3, u4), (sent_u, got_u))
    vec_total = Total(vec_sums, vec_lands, (sent_v, got_v))
    bias_total = Total(bias_sums, bias_lands, (sent_b, got_b))

    def load_up(m):
        return pltpu.make_async_copy(up_hbm.at[m], keep_u.at[m], local_u.at[m])

    load_z = pltpu.make_async_copy(dz_hbm, total, local_z)

    @pl.when(g == 0)
    def _():
        for m in range(CHUNKS):
            load_up(m).start()
        load_z.start()
        greet()
        for m in range(CHUNKS):
            load_up(m).wait()
            scatter_u.copy(1, m).start()
        vec_sums[0] = vec_ref[...]
        vec_total.copy(0).start()
        turn(x_ref, x_turned)
        turn(da_ref, da_turned)
        load_z.wait()

    def finish_u(m):
        width = keep_u.shape[4]
        gup_ref[:, pl.ds(pl.multiple_of(m * width, width), width)] = scatter_u.last(m)

    def finish_a(m):
        done = scatter_a.last(m)
        where = lax.div(m, 2)
        width = done.shape[1] // 2
        cols = pl.ds(pl.multiple_of(where * width, width), width)

        @pl.when(lax.rem(m, 2) == 0)
        def _():
            gout_ref[cols, :] = done[:, :width].T
            gqkv_ref[0, :, cols] = done[:, width:]

        @pl.when(lax.rem(m, 2) == 1)
        def _():
            gqkv_ref[1, :, cols] = done[:, :width]
            gqkv_ref[2, :, cols] = done[:, width:]

    def pair_a(m):
        pair.add(m)
        scatter_a.copy(1, m).start()

    def step(scatter, stage):
        def run(m):
            scatter.add(stage, m)
            scatter.copy(stage + 1, m).start()

        return run

    def tick_u(n):
        guarded(0, CHUNKS, n, step(scatter_u, 1))
        guarded(0, CHUNKS, n - 1, step(scatter_u, 2))
        guarded(0, CHUNKS, n - 2, step(scatter_u, 3))
        guarded(0, CHUNKS, n - 3, finish_u)

    def tick_a(n):
        guarded(0, CHUNKS, n, pair_a)
        guarded(0, CHUNKS, n - 2, step(scatter_a, 1))
        guarded(0, CHUNKS, n - 3, step(scatter_a, 2))
        guarded(0, CHUNKS, n - 4, step(scatter_a, 3))
        guarded(0, CHUNKS, n - 5, finish_a)

    _, t = mine()
    sides = (
        (0, qkv_oth, c_oth, wo_oth),
        (1, qkv_own, c_own, wo_own),
    )
    for own, qkv_ref, _, wo_ref in sides:
        grad_ctx = dot_nt(da_ref[...], wo_ref[...]).astype(jnp.bfloat16)
        for s in range(seqs):
            rows = slice(s * SEQ, (s + 1) * SEQ)
            levels = [level_ref[own, s, pl.ds(2 * g + head, 1), :] for head in range(2)]
            grads = attend_back_one(
                qkv_ref[0, rows, :], qkv_ref[1, rows, :], qkv_ref[2, rows, :], grad_ctx[rows], levels
            )
            for kind in range(3):
                stack[rows, (own * 3 + kind) * 128 : (own * 3 + kind + 1) * 128] = grads[kind]
        spot = t * own + (1 - t) * (1 - own)
        for kind, base in ((0, 0), (2, 8)):
            piece = stack[:, (own * 3 + kind) * 128 : (own * 3 + kind + 1) * 128]
            bias_sums[0, pl.ds(base + spot * 4 + g, 1), :] = jnp.sum(
                piece.astype(jnp.float32), axis=0, keepdims=True
            )
        tick_u(3 * g + own)
    pair.free(2 * g)
    for own, _, c_ref, _ in sides:
        first = dot(da_turned[...], c_ref[...])
        second = dot(x_turned[...], stack[:, own * 384 : own * 384 + 128])
        pair.store(2 * g, jnp.concatenate([first, second], axis=1), own)
    pair.copy(2 * g).start()
    pair.free(2 * g + 1)
    for own in range(2):
        pair.store(2 * g + 1, dot(x_turned[...], stack[:, own * 384 + 128 : own * 384 + 384]), own)
    pair.copy(2 * g + 1).start()
    weights = [wq_oth[kind] for kind in range(3)] + [wq_own[kind] for kind in range(3)]
    total[...] += dot_nt(stack[...], jnp.concatenate(weights, axis=1))
    tick_u(3 * g + 2)
    tick_a(2 * g)
    tick_a(2 * g + 1)
    for stage in range(3):
        @pl.when(g == stage + 1)
        def _():
            vec_total.step(stage)

    @pl.when(g == steps - 1)
    def _():
        bias_total.copy(0).start()
        out = pltpu.make_async_copy(total, gin_hbm, local_g)
        out.start()
        vec_total.step(3)
        for extra in range(5):
            tick_a(jnp.int32(CHUNKS + extra))
            bias_total.step(extra)
            if extra == 0:
                vec_total.step(4)
        vec_out[...] = vec_sums[5]
        bias_out[...] = bias_sums[5]
        for m in range(CHUNKS - 2, CHUNKS):
            pair.copy(m).wait_send()

        @pl.loop(0, CHUNKS)
        def _(m):
            scatter_u.drain(m)
            scatter_a.drain(m)

        vec_total.drain()
        bias_total.drain()
        out.wait()


def attend_backward(grad_attended, tokens, keep_up, grad_one, vectors, levels, own, other):
    rows, depth = tokens.shape
    width = own[1].shape[1]
    steps = width // 128
    inner = keep_up.shape[0] * keep_up.shape[4]
    fixed = lambda *shape: pl.BlockSpec(shape, lambda g: (0,) * len(shape))
    anywhere = pl.BlockSpec(memory_space=pl.ANY)
    column = pl.BlockSpec((rows, 128), lambda g: (0, g))
    side = [
        pl.BlockSpec((3, rows, 128), lambda g: (0, 0, g)),
        column,
        pl.BlockSpec((128, depth), lambda g: (g, 0)),
        pl.BlockSpec((3, depth, 128), lambda g: (0, 0, g)),
    ]
    sems = pltpu.SemaphoreType.DMA((5, CHUNKS))
    few = pltpu.SemaphoreType.DMA((5,))
    n_vec = vectors.shape[0]
    f32 = jnp.float32
    return pl.pallas_call(
        attend_back_kernel,
        grid=(steps,),
        in_specs=[
            fixed(rows, depth), fixed(rows, depth), anywhere, anywhere, fixed(n_vec, 128),
            fixed(*levels.shape),
        ] + side + side,
        out_specs=[
            anywhere, fixed(depth // 16, inner), fixed(width, depth // 16),
            fixed(3, depth // 16, width), fixed(n_vec, 128), fixed(16, 128),
        ],
        out_shape=[
            jax.ShapeDtypeStruct((rows, depth), f32),
            jax.ShapeDtypeStruct((depth // 16, inner), f32),
            jax.ShapeDtypeStruct((width, depth // 16), f32),
            jax.ShapeDtypeStruct((3, depth // 16, width), f32),
            jax.ShapeDtypeStruct((n_vec, 128), f32),
            jax.ShapeDtypeStruct((16, 128), f32),
        ],
        scratch_shapes=[
            pltpu.VMEM((depth, rows), jnp.bfloat16),
            pltpu.VMEM((depth, rows), jnp.bfloat16),
            pltpu.VMEM((rows, depth), f32),
            pltpu.VMEM((rows, 768), jnp.bfloat16),
            *scatter_scratch(CHUNKS, SPAN, 256, False),
            *land_scratch(CHUNKS, SPAN, 256),
            *scatter_scratch(CHUNKS, SPAN, 256, True),
            *land_scratch(CHUNKS, SPAN, 256),
            pltpu.VMEM((6, n_vec, 128), f32),
            pltpu.VMEM((5, n_vec, 128), f32),
            pltpu.VMEM((6, 16, 128), f32),
            pltpu.VMEM((5, 16, 128), f32),
            sems, sems, sems, sems, few, few, few, few,
            pltpu.SemaphoreType.DMA((CHUNKS,)),
            pltpu.SemaphoreType.DMA,
            pltpu.SemaphoreType.DMA,
        ],
        compiler_params=pltpu.CompilerParams(
            vmem_limit_bytes=VMEM, collective_id=2, has_side_effects=True
        ),
        cost_estimate=pl.CostEstimate(
            flops=rows * depth * width * 40, bytes_accessed=60 * 1024 * 1024, transcendentals=0
        ),
        name="attend_backward",
    )(
        grad_attended, tokens, keep_up, grad_one, vectors, levels, *own, *other,
    )


def attend_one(queries, key_rows, values):
    first = head_masks(128)
    values_t = values.T
    parts, levels = [], []
    for head in range(2):
        mask = first if head == 0 else jnp.logical_not(first)
        picked = jnp.where(mask, queries, jnp.zeros_like(queries))
        scores = dot_nt(key_rows, picked) * (LOG2E * HEAD_DIM**-0.5)
        peak = jnp.max(scores, axis=0, keepdims=True)
        lifted = jnp.exp2(scores - peak)
        totals = jnp.sum(lifted, axis=0, keepdims=True)
        context = dot(values_t[head * HEAD_DIM : (head + 1) * HEAD_DIM], lifted.astype(jnp.bfloat16))
        parts.append(context * (1.0 / totals))
        levels.append(peak + jnp.log2(totals))
    return jnp.concatenate(parts, axis=0).T.astype(jnp.bfloat16), levels


class Fetch:
    HOPS = 9

    def __init__(self, source, target, unit, index, sems):
        self.source, self.target, self.unit, self.index = source, target, unit, index
        self.sent, self.got = sems

    def copy(self, hop):
        dp, t = mine()
        core, x, z = bit_of(dp, 1), bit_of(dp, 2), bit_of(dp, 4)
        quarter = {0: x * 2 + z, 1: (1 - x) * 2 + z, 2: x * 2 + 1 - z, 3: (1 - x) * 2 + 1 - z}
        if hop == 0:
            which, part, peer = 0, None, (dp, 1 - t)
        elif hop == 1:
            which, part, peer = 0, None, (flip(dp, 2), t)
        elif hop == 2:
            which, part, peer = 0, None, (flip(dp, 4), t)
        elif hop == 3:
            which, part, peer = 2, 0, (flip(dp, 2), t)
        elif hop == 4:
            which, part, peer = 1, 1, (flip(dp, 4), t)
        else:
            which, part, peer = hop - 5, None, (flip(dp, 1), t)
        place = self.unit(core, quarter[which], part)
        origin = self.source if hop == 0 else self.target
        return pltpu.make_async_remote_copy(
            src_ref=origin.at[place],
            dst_ref=self.target.at[place],
            send_sem=self.sent.at[self.index, hop],
            recv_sem=self.got.at[self.index, hop],
            device_id=peer,
            device_id_type=MESH,
        )

    def start(self, *hops):
        for hop in hops:
            self.copy(hop).start()

    def arrive(self, *hops):
        for hop in hops:
            self.copy(hop).wait_recv()

    def advance(self, stage):
        if stage == 1:
            self.arrive(0)
            self.start(1, 2, 5)
        elif stage == 2:
            self.arrive(1, 2)
            self.start(3, 4, 6, 7)
        elif stage == 3:
            self.arrive(3, 4)
            self.start(8)
        else:
            self.arrive(5, 6, 7, 8)

    def drain(self):
        for hop in range(self.HOPS):
            self.copy(hop).wait_send()


def unit_of(total, lead=(), base=0, tail=()):
    def unit(core, quarter, part):
        size = total // 8
        start = base + core * (total // 2) + quarter * size
        if part is not None:
            size //= 2
            start = start + part * size
        return (*lead, pl.ds(pl.multiple_of(start, 16), size), *tail)

    return unit


def forward_kernel(
    x_hbm, cot_hbm, wq_hbm, wo_hbm, wu_hbm, wd_hbm,
    bias_ref, bo_ref, g1_ref, s1_ref, bd_ref, g2_ref, s2_ref,
    qkv_out1, qkv_out0, ctx_out1, ctx_out0, act_out1, act_out0, slope_out1, slope_out0,
    hr_out, n1_out, dm_out, dz_out, res_out, wq_out, wo_out, wu_out, wd_out,
    level_ref, scale_ref, sums_ref,
    x, cot, wq1, wq0, wo1, wo0, wu1, wu0, wd1, wd0, qkv1, qkv0, ctx1, ctx0, n1, hr, total, act, slope,
    bias_oth, sent, got, bias_sent, bias_got, load_sems, out_sems,
):
    dp, t = mine()
    rows, depth = x.shape
    seqs = rows // SEQ
    width = ctx1.shape[1]
    inner = wu1.shape[1]
    tiles = 4
    span = inner // tiles

    chunks = []

    def chunk(source, target, unit):
        chunks.append(Fetch(source, target, unit, len(chunks), (sent, got)))
        return len(chunks) - 1

    c_qkv = [chunk(wq_hbm, wq0, unit_of(depth, lead=(kind,))) for kind in range(3)]
    c_out = chunk(wo_hbm, wo0, unit_of(width))
    c_up, c_down = [], []
    for j in range(tiles):
        c_up.append(chunk(wu_hbm, wu0, unit_of(depth, tail=(pl.ds(j * span, span),))))
        c_down.append(chunk(wd_hbm, wd0, unit_of(span, base=j * span)))

    loads, outs, done = {}, [], []

    def finish(copy):
        copy.wait()
        done.append(copy)

    def load(name, source, target):
        copy = pltpu.make_async_copy(source, target, load_sems.at[len(loads)])
        loads[name] = copy
        copy.start()

    def save(source, target):
        copy = pltpu.make_async_copy(source, target, out_sems.at[len(outs)])
        outs.append(copy)
        copy.start()
        return copy

    load("x", x_hbm, x)
    for kind in range(3):
        load(("q", kind), wq_hbm.at[kind], wq1.at[kind])
    greet()
    ahead = 3
    for m in range(ahead):
        chunks[m].start(0)
    bias_copy = pltpu.make_async_remote_copy(
        src_ref=bias_ref, dst_ref=bias_oth, send_sem=bias_sent, recv_sem=bias_got,
        device_id=(dp, 1 - t), device_id_type=MESH,
    )
    bias_copy.start()
    load("o", wo_hbm, wo1)
    load("u", wu_hbm, wu1)
    load("d", wd_hbm, wd1)
    load("cot", cot_hbm, cot)

    events = []
    for m in range(len(chunks)):
        for stage, lag in ((1, 7.0), (2, 13.0), (3, 17.0), (4, 20.0)):
            events.append((lag + 4.3 * m, stage, m))
    events.sort()
    saves = {}
    for kind in range(3):
        saves[c_qkv[kind]] = (wq0.at[kind], wq_out.at[kind])
    saves[c_out] = (wo0, wo_out)
    for j in range(tiles):
        cols = pl.ds(j * span, span)
        saves[c_up[j]] = (wu0.at[:, cols], wu_out.at[:, cols])
        saves[c_down[j]] = (wd0.at[cols], wd_out.at[cols])

    def event():
        _, stage, m = events.pop(0)
        chunks[m].advance(stage)
        if stage == 1 and m + ahead < len(chunks):
            chunks[m + ahead].start(0)
        if stage == 4:
            save(*saves[m])

    clock = [0.0]

    def spend(us):
        clock[0] += us
        while events and events[0][0] <= clock[0]:
            event()

    def need(m):
        while any(e[1] == 4 and e[2] == m for e in events):
            clock[0] = max(clock[0], events[0][0])
            event()

    def project(weights, kind, kept, biases):
        product = dot(x[...], weights[kind])
        if kind != 1:
            at = 0 if kind == 0 else width
            product = product + biases[:, at : at + width]
        kept[kind] = product.astype(jnp.bfloat16)

    def attend(side, kept, context, pair):
        cols = slice(pair * 128, pair * 128 + 128)

        @pl.loop(0, seqs)
        def _(s):
            here = pl.ds(pl.multiple_of(s * SEQ, SEQ), SEQ)
            out, levels = attend_one(kept[0, here, cols], kept[1, here, cols], kept[2, here, cols])
            context[here, cols] = out
            for head in range(2):
                spot = 2 * pair + head
                level_ref[side, s, spot : spot + 1, :] = levels[head]

    loads["x"].wait()
    for kind in range(3):
        loads[("q", kind)].wait()
        project(wq1, kind, qkv1, bias_ref)
        spend(1.6)
    save(qkv1, qkv_out1)
    for pair in range(width // 128):
        attend(1, qkv1, ctx1, pair)
        spend(2.7)
    save(ctx1, ctx_out1)
    bias_copy.wait_recv()
    for kind in range(3):
        need(c_qkv[kind])
        project(wq0, kind, qkv0, bias_oth)
        spend(1.6)
    save(qkv0, qkv_out0)
    for pair in range(width // 128):
        attend(0, qkv0, ctx0, pair)
        spend(2.7)
    save(ctx0, ctx_out0)
    loads["o"].wait()
    need(c_out)
    step = 256

    @pl.loop(0, rows // step)
    def _(r):
        here = pl.ds(pl.multiple_of(r * step, step), step)
        attended = dot(ctx1[here, :], wo1[...]) + dot(ctx0[here, :], wo0[...])
        _, normed, scaled = norm_forward(
            x[here, :].astype(jnp.float32) + attended + bo_ref[...], g1_ref[...], s1_ref[...]
        )
        n1[here, :] = normed
        hr[here, :] = (normed * g1_ref[...] + s1_ref[...]).astype(jnp.bfloat16)
        scale_ref[here, :] = jnp.broadcast_to(scaled, (step, 128))

    save(n1, n1_out)
    hr_saved = save(hr, hr_out)
    spend(5.0)
    loads["u"].wait()
    loads["d"].wait()
    big = 512
    slots = []
    for side, up, down, biases, act_out, slope_out in (
        (1, wu1, wd1, bias_ref, act_out1, slope_out1),
        (0, wu0, wd0, bias_oth, act_out0, slope_out0),
    ):
        for j in range(tiles):
            cols = pl.ds(j * span, span)
            slot = len(slots) % 2
            if len(slots) >= 2:
                for copy in slots[-2]:
                    finish(copy)
            if side == 0:
                need(c_up[j])
                need(c_down[j])
            bias = biases[:, 2 * width + j * span : 2 * width + (j + 1) * span]
            fresh = not slots

            @pl.loop(0, rows // big)
            def _(r):
                here = pl.ds(pl.multiple_of(r * big, big), big)
                activated, leaning = gelu_pair(dot(hr[here, :], up[:, cols]) + bias)
                activated = activated.astype(jnp.bfloat16)
                act[slot, here, :] = activated
                slope[slot, here, :] = leaning.astype(jnp.bfloat16)
                product = dot(activated, down[cols, :])
                total[here, :] = product if fresh else total[here, :] + product

            slots.append((
                save(act.at[slot], act_out.at[:, cols]),
                save(slope.at[slot], slope_out.at[:, cols]),
            ))
            spend(3.6)
    while events:
        event()
    finish(hr_saved)
    loads["cot"].wait()
    sums_ref[...] = jnp.zeros_like(sums_ref)

    @pl.loop(0, rows // step)
    def _(r):
        here = pl.ds(pl.multiple_of(r * step, step), step)
        hidden = n1[here, :] * g1_ref[...] + s1_ref[...]
        result, normed, scaled = norm_forward(hidden + total[here, :] + bd_ref[...], g2_ref[...], s2_ref[...])
        x[here, :] = result.astype(jnp.bfloat16)
        upstream = cot[here, :].astype(jnp.float32)
        grad = norm_backward(upstream, g2_ref[...], normed, scaled)
        total[here, :] = grad
        low = grad.astype(jnp.bfloat16)
        hr[here, :] = low
        sums_ref[0:1, :] += jnp.sum(upstream, axis=0, keepdims=True)
        sums_ref[1:2, :] += jnp.sum(upstream * normed, axis=0, keepdims=True)
        sums_ref[2:3, :] += jnp.sum(low.astype(jnp.float32), axis=0, keepdims=True)

    save(x, res_out)
    save(hr, dm_out)
    save(total, dz_out)
    bias_copy.wait_send()
    for fetch in chunks:
        fetch.drain()
    for copy in outs:
        if not any(copy is other for other in done):
            copy.wait()


def forward(tokens, cotangent, w_qkv, w_out, w_up, w_down, biases, bias_o, gain_one, shift_one, bias_down, gain_two, shift_two):
    rows, depth = tokens.shape
    width, inner = w_out.shape[0], w_up.shape[1]
    seqs, heads = rows // SEQ, width // HEAD_DIM
    low, f32 = jnp.bfloat16, jnp.float32
    any_space = pl.BlockSpec(memory_space=pl.ANY)
    near = pl.BlockSpec(memory_space=pltpu.VMEM)
    qkv = (3, rows, width)
    outs = [
        (qkv, low), (qkv, low), ((rows, width), low), ((rows, width), low),
        ((rows, inner), low), ((rows, inner), low), ((rows, inner), low), ((rows, inner), low),
        ((rows, depth), low), ((rows, depth), f32), ((rows, depth), low), ((rows, depth), f32), ((rows, depth), low),
        (w_qkv.shape, low), (w_out.shape, low), (w_up.shape, low), (w_down.shape, low),
        ((2, seqs, heads, SEQ), f32), ((rows, 128), f32), ((8, depth), f32),
    ]
    span = inner // 4
    scratch = [
        ((rows, depth), low), ((rows, depth), low), (w_qkv.shape, low), (w_qkv.shape, low),
        (w_out.shape, low), (w_out.shape, low), (w_up.shape, low), (w_up.shape, low),
        (w_down.shape, low), (w_down.shape, low), (qkv, low), (qkv, low),
        ((rows, width), low), ((rows, width), low), ((rows, depth), f32), ((rows, depth), low),
        ((rows, depth), f32), ((2, rows, span), low), ((2, rows, span), low), (biases.shape, f32),
    ]
    sems = pltpu.SemaphoreType.DMA((12, Fetch.HOPS))
    one = pltpu.SemaphoreType.DMA
    return pl.pallas_call(
        forward_kernel,
        in_specs=[any_space] * 6 + [near] * 7,
        out_specs=[any_space] * 17 + [near] * 3,
        out_shape=[jax.ShapeDtypeStruct(*out) for out in outs],
        scratch_shapes=[pltpu.VMEM(*buffer) for buffer in scratch]
        + [sems, sems, one, one, pltpu.SemaphoreType.DMA((8,)), pltpu.SemaphoreType.DMA((40,))],
        compiler_params=pltpu.CompilerParams(
            vmem_limit_bytes=60 * 1024 * 1024, collective_id=3, has_side_effects=True
        ),
        cost_estimate=pl.CostEstimate(
            flops=rows * depth * (width * 16 + inner * 8), bytes_accessed=80 * 1024 * 1024, transcendentals=0
        ),
        name="forward",
    )(
        tokens, cotangent, w_qkv, w_out, w_up, w_down, biases,
        *(v.reshape(1, -1) for v in (bias_o, gain_one, shift_one, bias_down, gain_two, shift_two)),
    )


def body(mesh, *args):
    tokens, w_qkv = args[0], args[2]
    n_dp, n_tensor = mesh.shape["dp"], mesh.shape["tensor"]
    local = (tokens.shape[0] % SEQ, w_qkv.shape[2], args[9].shape[1])
    if (n_dp, n_tensor) == (16, 2) and local == (0, 512, 2048):
        return body_tokens(*args)
    return body_tensor(*args)


def body_tokens(
    tokens,
    cotangent,
    w_qkv,
    bias_q,
    bias_v,
    w_out,
    bias_o,
    gain_one,
    shift_one,
    w_up,
    bias_up,
    w_down,
    bias_down,
    gain_two,
    shift_two,
):
    me_t = lax.axis_index("tensor")
    biases = jnp.concatenate([bias_q, bias_v, bias_up]).reshape(1, -1)
    (
        qkv, qkv2, ctx, ctx2, active, active2, slope, slope2,
        hidden_rows, normed_one, grad_branch, grad_two, result,
        w_qkv2, w_out2, w_up2, w_down2, levels, scaled_one, sums,
    ) = forward(
        tokens, cotangent, w_qkv, w_out, w_up, w_down, biases,
        bias_o, gain_one, shift_one, bias_down, gain_two, shift_two,
    )
    scaled_one = scaled_one[:, :1]
    grad_down, bias_up_parts, keep_up, raised = ffn_backward(
        grad_branch, hidden_rows, active, active2, slope, slope2, w_down, w_down2, w_up, w_up2
    )
    grad_hidden = grad_two + raised
    grad_one = norm_backward(grad_hidden, gain_one, normed_one, scaled_one)
    grad_attended = grad_one.astype(jnp.bfloat16)
    bias_parts = bias_up_parts.reshape(2, -1)
    bias_parts = jnp.where(me_t == 0, bias_parts[::-1], bias_parts)
    vectors = jnp.concatenate(
        [
            sums[:3].reshape(-1),
            bias_parts.reshape(-1),
            jnp.sum(grad_hidden, axis=0),
            jnp.sum(grad_hidden * normed_one, axis=0),
            jnp.sum(grad_attended.astype(jnp.float32), axis=0),
        ]
    )
    grad_input, grad_up, grad_out, grad_qkv, vectors, biases = attend_backward(
        grad_attended,
        tokens,
        keep_up,
        grad_one,
        vectors.reshape(-1, 128),
        levels,
        (qkv, ctx, w_out, w_qkv),
        (qkv2, ctx2, w_out2, w_qkv2),
    )
    vectors = vectors.reshape(-1)
    d, at, pieces = tokens.shape[1], 0, []
    for size in (d, d, d, bias_parts.size, d, d, d):
        pieces.append(vectors[at : at + size])
        at += size
    g_shift_two, g_gain_two, g_bias_down, g_bias_up, g_shift_one, g_gain_one, g_bias_o = pieces
    g_bias_q, g_bias_v = biases[:8].reshape(-1), biases[8:].reshape(-1)
    return (
        result,
        grad_input,
        grad_qkv,
        g_bias_q,
        g_bias_v,
        grad_out,
        g_bias_o,
        g_gain_one,
        g_shift_one,
        grad_up,
        g_bias_up,
        grad_down,
        g_bias_down,
        g_gain_two,
        g_shift_two,
    )


def solution(mesh):
    in_specs = (
        P(("dp", "tensor"), None),
        P(("dp", "tensor"), None),
        P(None, None, "tensor"),
        P("tensor"),
        P("tensor"),
        P("tensor", None),
        P(),
        P(),
        P(),
        P(None, "tensor"),
        P("tensor"),
        P("tensor", None),
        P(),
        P(),
        P(),
    )
    out_specs = (
        P(("dp", "tensor"), None),
        P(("dp", "tensor"), None),
        P(None, "dp", "tensor"),
        P(),
        P(),
        P("tensor", "dp"),
        P(),
        P(),
        P(),
        P("dp", "tensor"),
        P(),
        P("tensor", "dp"),
        P(),
        P(),
        P(),
    )
    return jax.shard_map(functools.partial(body, mesh), mesh=mesh, in_specs=in_specs, out_specs=out_specs, check_vma=False)
```

```python
import functools

import jax
import jax.numpy as jnp
from jax import lax
from jax.experimental import pallas as pl
from jax.experimental.pallas import tpu as pltpu
from jax.sharding import PartitionSpec as P

D = 1024
FF = 4096
HEAD_DIM = 64
SEQ = 512


def gelu_pair(inner_pre):
    normal_cdf = 0.5 * (1.0 + jax.scipy.special.erf(inner_pre * 0.7071067811865476))
    density = jnp.exp(-0.5 * inner_pre * inner_pre) * 0.3989422804014327
    return (inner_pre * normal_cdf, normal_cdf + inner_pre * density)


def norm_forward(summed, gain, shift):
    centre = summed - jnp.mean(summed, axis=-1, keepdims=True)
    scaled = lax.rsqrt(jnp.mean(centre * centre, axis=-1, keepdims=True) + 1e-05)
    normed = centre * scaled
    return (normed * gain + shift, normed, scaled)


def norm_backward(upstream, gain, normed, scaled):
    grad_norm = upstream * gain
    return scaled * (
        grad_norm
        - jnp.mean(grad_norm, axis=-1, keepdims=True)
        - normed * jnp.mean(grad_norm * normed, axis=-1, keepdims=True)
    )


def attend_block(block):
    queries, key_rows, values = block
    scores = jnp.einsum(
        "qhd,khd->hqk", queries, key_rows, preferred_element_type=jnp.float32
    ) * HEAD_DIM ** (-0.5)
    peak_score = jnp.max(scores, axis=-1, keepdims=True)
    lifted = jnp.exp(scores - peak_score)
    totals = jnp.sum(lifted, axis=-1, keepdims=True)
    weights = (lifted / totals).astype(jnp.bfloat16)
    context = jnp.einsum("hqk,khd->qhd", weights, values, preferred_element_type=jnp.float32)
    return (context.astype(jnp.bfloat16), (peak_score + jnp.log(totals))[..., 0])


def attend_back(block):
    queries, key_rows, values, logsum, grad_ctx = block
    scale = HEAD_DIM ** (-0.5)
    scores = (
        jnp.einsum("qhd,khd->hqk", queries, key_rows, preferred_element_type=jnp.float32) * scale
    )
    weights = jnp.exp(scores - logsum[..., None])
    grad_weights = jnp.einsum("qhd,khd->hqk", grad_ctx, values, preferred_element_type=jnp.float32)
    grad_scores = weights * (grad_weights - jnp.sum(weights * grad_weights, axis=-1, keepdims=True))
    grad_low = grad_scores.astype(jnp.bfloat16)
    grad_v = jnp.einsum(
        "hqk,qhd->khd", weights.astype(jnp.bfloat16), grad_ctx, preferred_element_type=jnp.float32
    )
    grad_q = (
        jnp.einsum("hqk,khd->qhd", grad_low, key_rows, preferred_element_type=jnp.float32) * scale
    )
    grad_k = (
        jnp.einsum("hqk,qhd->khd", grad_low, queries, preferred_element_type=jnp.float32) * scale
    )
    return (grad_q.astype(jnp.bfloat16), grad_k.astype(jnp.bfloat16), grad_v.astype(jnp.bfloat16))


def body_tensor(
    tokens,
    cotangent,
    w_qkv,
    bias_q,
    bias_v,
    w_out,
    bias_o,
    gain_one,
    shift_one,
    w_up,
    bias_up,
    w_down,
    bias_down,
    gain_two,
    shift_two,
):
    rank = lax.axis_index("tensor")
    full_rows = lax.all_gather(tokens, "tensor", axis=0, tiled=True)
    group_rows = full_rows.shape[0]
    local_width = w_qkv.shape[2]
    head_shape = (group_rows // SEQ, SEQ, local_width // HEAD_DIM, HEAD_DIM)
    projected = jnp.einsum("td,kde->kte", full_rows, w_qkv, preferred_element_type=jnp.float32)
    queries = (projected[0] + bias_q).astype(jnp.bfloat16).reshape(head_shape)
    key_rows = projected[1].astype(jnp.bfloat16).reshape(head_shape)
    values = (projected[2] + bias_v).astype(jnp.bfloat16).reshape(head_shape)
    context, logsum = lax.map(attend_block, (queries, key_rows, values))
    context = context.reshape(group_rows, local_width)
    attended = (
        lax.psum_scatter(
            jnp.dot(context, w_out, preferred_element_type=jnp.float32),
            "tensor",
            scatter_dimension=0,
            tiled=True,
        )
        + bias_o
    )
    hidden_one, normed_one, scaled_one = norm_forward(
        tokens.astype(jnp.float32) + attended, gain_one, shift_one
    )
    hidden_rows = lax.all_gather(hidden_one.astype(jnp.bfloat16), "tensor", axis=0, tiled=True)
    inner_pre = jnp.dot(hidden_rows, w_up, preferred_element_type=jnp.float32) + bias_up
    activated, slope = gelu_pair(inner_pre)
    active_low = activated.astype(jnp.bfloat16)
    branch = (
        lax.psum_scatter(
            jnp.dot(active_low, w_down, preferred_element_type=jnp.float32),
            "tensor",
            scatter_dimension=0,
            tiled=True,
        )
        + bias_down
    )
    result, normed_two, scaled_two = norm_forward(hidden_one + branch, gain_two, shift_two)
    upstream = cotangent.astype(jnp.float32)
    grad_two = norm_backward(upstream, gain_two, normed_two, scaled_two)
    grad_branch = grad_two.astype(jnp.bfloat16)
    branch_rows = lax.all_gather(grad_branch, "tensor", axis=0, tiled=True)
    grad_down = jnp.einsum("tf,td->fd", active_low, branch_rows, preferred_element_type=jnp.float32)
    grad_inner = (
        jnp.einsum("td,fd->tf", branch_rows, w_down, preferred_element_type=jnp.float32) * slope
    ).astype(jnp.bfloat16)
    grad_up = jnp.einsum("td,tf->df", hidden_rows, grad_inner, preferred_element_type=jnp.float32)
    grad_hidden = grad_two + lax.psum_scatter(
        jnp.einsum("tf,df->td", grad_inner, w_up, preferred_element_type=jnp.float32),
        "tensor",
        scatter_dimension=0,
        tiled=True,
    )
    grad_one = norm_backward(grad_hidden, gain_one, normed_one, scaled_one)
    grad_attended = grad_one.astype(jnp.bfloat16)
    attended_rows = lax.all_gather(grad_attended, "tensor", axis=0, tiled=True)
    grad_out = jnp.einsum("te,td->ed", context, attended_rows, preferred_element_type=jnp.float32)
    grad_context = jnp.einsum(
        "td,ed->te", attended_rows, w_out, preferred_element_type=jnp.float32
    ).astype(jnp.bfloat16)
    grad_q, grad_k, grad_v = lax.map(
        attend_back, (queries, key_rows, values, logsum, grad_context.reshape(head_shape))
    )
    grad_stack = jnp.stack(
        [
            grad_q.reshape(group_rows, local_width),
            grad_k.reshape(group_rows, local_width),
            grad_v.reshape(group_rows, local_width),
        ]
    )
    weight_qkv = jnp.einsum(
        "td,kte->kde", full_rows, grad_stack, preferred_element_type=jnp.float32
    )
    grad_input = grad_one + lax.psum_scatter(
        jnp.einsum("kte,kde->td", grad_stack, w_qkv, preferred_element_type=jnp.float32).astype(
            jnp.bfloat16
        ),
        "tensor",
        scatter_dimension=0,
        tiled=True,
    ).astype(jnp.float32)

    def placed(piece, length):
        return lax.dynamic_update_slice_in_dim(
            jnp.zeros((length,), jnp.float32), piece, rank * piece.shape[0], 0
        )

    vectors = lax.psum(
        (
            placed(jnp.sum(grad_stack[0].astype(jnp.float32), axis=0), D),
            placed(jnp.sum(grad_stack[2].astype(jnp.float32), axis=0), D),
            jnp.sum(grad_attended.astype(jnp.float32), axis=0),
            jnp.sum(grad_hidden * normed_one, axis=0),
            jnp.sum(grad_hidden, axis=0),
            placed(jnp.sum(grad_inner.astype(jnp.float32), axis=0), FF),
            jnp.sum(grad_branch.astype(jnp.float32), axis=0),
            jnp.sum(upstream * normed_two, axis=0),
            jnp.sum(upstream, axis=0),
        ),
        ("dp", "tensor"),
    )
    weight_parts = (
        lax.psum_scatter(
            weight_qkv.astype(jnp.bfloat16), "dp", scatter_dimension=1, tiled=True
        ).astype(jnp.float32),
        lax.psum_scatter(
            grad_out.astype(jnp.bfloat16), "dp", scatter_dimension=1, tiled=True
        ).astype(jnp.float32),
        lax.psum_scatter(
            grad_up.astype(jnp.bfloat16), "dp", scatter_dimension=0, tiled=True
        ).astype(jnp.float32),
        lax.psum_scatter(
            grad_down.astype(jnp.bfloat16), "dp", scatter_dimension=1, tiled=True
        ).astype(jnp.float32),
    )
    return (
        result.astype(jnp.bfloat16),
        grad_input,
        weight_parts[0],
        vectors[0],
        vectors[1],
        weight_parts[1],
        vectors[2],
        vectors[3],
        vectors[4],
        weight_parts[2],
        vectors[5],
        weight_parts[3],
        vectors[6],
        vectors[7],
        vectors[8],
    )


AXES = ("dp", "tensor")
LOG2E = 1.4426950408889634
VMEM = 56 * 1024 * 1024
NT = (((1,), (1,)), ((), ()))


def dot(left, right):
    return jnp.dot(left, right, preferred_element_type=jnp.float32)


def dot_nt(left, right):
    return lax.dot_general(left, right, NT, preferred_element_type=jnp.float32)


def head_masks(width):
    lane = lax.broadcasted_iota(jnp.int32, (1, width), 1)
    return lane < HEAD_DIM


MESH = pl.DeviceIdType.MESH
CHUNKS = 8
SPAN = 256


def bit_of(index, bit):
    return lax.rem(lax.div(index, bit), 2)


def flip(index, bit):
    return index + bit - 2 * bit * bit_of(index, bit)


def mine():
    return lax.axis_index("dp"), lax.axis_index("tensor")


def greet():
    dp, t = mine()
    barrier = pltpu.get_barrier_semaphore()
    peers = [(flip(dp, 1), t), (dp, flip(t, 1)), (flip(dp, 2), t), (flip(dp, 4), t), (flip(dp, 8), t)]
    for peer in peers:
        pl.semaphore_signal(barrier, inc=1, device_id=peer, device_id_type=MESH)
    pl.semaphore_wait(barrier, len(peers))


def turn(left_ref, turned):
    dp, _ = mine()
    height = turned.shape[0] // 16
    whole = left_ref[...].T
    for piece in range(16):
        spot = 0
        for bit, weight in ((1, 8), (2, 4), (4, 2), (8, 1)):
            own = bit_of(dp, bit)
            spot = spot + weight * (own if piece & bit else 1 - own)
        turned[pl.ds(pl.multiple_of(spot * height, height), height), :] = whole[
            piece * height : (piece + 1) * height
        ]


class Scatter:
    def __init__(self, keep, lands, sems):
        self.keep = keep
        self.lands = lands
        self.sent, self.got = sems

    def copy(self, stage, m):
        dp, t = mine()
        odd = lax.rem(m, 2)
        rows = self.keep.shape[3]
        if stage == 1:
            src, peer = self.keep.at[m, 0], (dp + odd * (flip(dp, 2) - dp), t + (1 - odd) * (1 - 2 * t))
        elif stage == 2:
            src, peer = self.keep.at[m, 1, 0], (dp + (1 - odd) * (flip(dp, 2) - dp), t + odd * (1 - 2 * t))
        elif stage == 3:
            src, peer = self.keep.at[m, 1, 1, pl.ds(0, rows // 2)], (flip(dp, 4), t)
        else:
            src, peer = self.keep.at[m, 1, 1, pl.ds(rows // 2, rows // 4)], (flip(dp, 8), t)
        return pltpu.make_async_remote_copy(
            src_ref=src,
            dst_ref=self.lands[stage - 1].at[m],
            send_sem=self.sent.at[stage, m],
            recv_sem=self.got.at[stage, m],
            device_id=peer,
            device_id_type=MESH,
        )

    def step(self, stage, m):
        rows = self.keep.shape[3]
        self.copy(stage, m).wait_recv()
        land = self.lands[stage - 1]
        if stage == 1:
            @pl.loop(0, 2)
            def _(half):
                self.keep[m, 1, half] = plus(self.keep[m, 1, half], land[m, half])
        elif stage == 2:
            self.keep[m, 1, 1] = plus(self.keep[m, 1, 1], land[m])
        elif stage == 3:
            half = pl.ds(rows // 2, rows // 2)
            self.keep[m, 1, 1, half] = plus(self.keep[m, 1, 1, half], land[m])
        self.copy(stage + 1, m).start()

    def last(self, m):
        rows = self.keep.shape[3]
        self.copy(4, m).wait_recv()
        rest = pl.ds(3 * rows // 4, rows // 4)
        return self.keep[m, 1, 1, rest].astype(jnp.float32) + self.lands[3][m].astype(jnp.float32)

    def drain(self, m):
        for stage in (1, 2, 3, 4):
            self.copy(stage, m).wait_send()


class Pair:
    def __init__(self, keep, send, land, sems):
        self.keep, self.send, self.land = keep, send, land
        self.sent, self.got = sems
        self.slots = send.shape[0]

    def copy(self, m):
        dp, t = mine()
        return pltpu.make_async_remote_copy(
            src_ref=self.send.at[lax.rem(m, self.slots)],
            dst_ref=self.land.at[m],
            send_sem=self.sent.at[0, m],
            recv_sem=self.got.at[0, m],
            device_id=(flip(dp, 1), t),
            device_id_type=MESH,
        )

    def store(self, m, product, own):
        half = product.shape[0] // 2
        rows = half // 2
        odd = lax.rem(m, 2)
        slot = lax.rem(m, self.slots)
        for x in range(2):
            first = odd * x + (1 - odd) * own
            second = odd * own + (1 - odd) * x
            self.send[slot, first, second] = product[x * rows : (x + 1) * rows].astype(jnp.bfloat16)
            self.keep[m, first, second] = product[half + x * rows : half + (x + 1) * rows].astype(
                jnp.bfloat16
            )

    def free(self, m):
        @pl.when(m >= self.slots)
        def _():
            self.copy(m - self.slots).wait_send()

    def add(self, m):
        self.copy(m).wait_recv()

        @pl.loop(0, 4)
        def _(quarter):
            a, b = lax.div(quarter, 2), lax.rem(quarter, 2)
            self.keep[m, a, b] = plus(self.keep[m, a, b], self.land[m, a, b])


def plus(left, right):
    return (left.astype(jnp.float32) + right.astype(jnp.float32)).astype(jnp.bfloat16)


def low_buffer(*shape):
    return pltpu.VMEM(shape, jnp.bfloat16)


def land_scratch(chunks, rows, width):
    return [
        low_buffer(chunks, 2, rows, width),
        low_buffer(chunks, rows, width),
        low_buffer(chunks, rows // 2, width),
        low_buffer(chunks, rows // 4, width),
    ]


def due(n, table, action):
    chunk = -1
    for m, tick in enumerate(table):
        chunk = jnp.where(n == tick, m, chunk)

    @pl.when(chunk >= 0)
    def _():
        action(jnp.maximum(chunk, 0))


EARLY_UP = 2
FFN_TICKS, FFN_END = 40, 55
FFN_DOWN = (
    (4, 5, 10, 11, 15, 16, 21, 22),
    (11, 12, 18, 19, 23, 28, 29, 34),
    (16, 19, 30, 31, 36, 37, 38, 39),
    (19, 23, 34, 35, 41, 43, 44, 46),
    (23, 27, 38, 39, 48, 50, 52, 54),
)
FFN_UP = (
    (7, 12, 19, 25, 29, 33, 37, 42),
    (14, 23),
    (24, 31),
    (27, 35),
    (31, 39),
)
ATT_TICKS, ATT_END = 32, 59
ATT_UP = (
    (-1, -1, -1, -1, -1, -1),
    (2, 3, 4, 5, 9, 10),
    (10, 11, 12, 13, 14, 15),
    (12, 14, 17, 18, 19, 20),
    (16, 18, 19, 20, 22, 25),
)
ATT_OWN = (
    (2, 9, 10, 11, 12, 16, 17, 18, 19, 25, 26, 27, 28, 32, 33, 34),
    (10, 12, 15, 16, 17, 18, 19, 20, 23, 27, 28, 32, 33, 35, 36, 40),
    (13, 16, 17, 18, 19, 20, 22, 25, 26, 30, 32, 34, 36, 42, 44, 46),
    (17, 19, 20, 21, 23, 25, 26, 27, 28, 33, 34, 38, 42, 48, 50, 52),
    (20, 23, 25, 26, 27, 28, 29, 30, 32, 35, 36, 44, 46, 54, 56, 58),
)


def ffn_back_kernel(
    dm_hbm, hr_hbm, dz_hbm, n1_hbm, scale_ref, g1_ref, sums_ref,
    g_own, g_oth, s_own, s_oth, wd_own, wd_oth, wu_own, wu_oth,
    down_ref, up_ref, vec_ref, up_hbm, dz_out, da_out,
    dm, hr, n1, dm_turned, hr_turned, total,
    keep_d, send_d, land_d, d1, d2, d3, d4, keep_u, send_u, land_u, u1, u2, u3, u4,
    sent_d, got_d, sent_u, got_u, local_u, load_sems, out_sems,
):
    j = pl.program_id(0)
    steps = pl.num_programs(0)
    _, t = mine()
    width = keep_d.shape[4]
    early = u1.shape[0]
    pair_d = Pair(keep_d, send_d, land_d, (sent_d, got_d))
    pair_u = Pair(keep_u, send_u, land_u, (sent_u, got_u))
    scatter_d = Scatter(keep_d, (d1, d2, d3, d4), (sent_d, got_d))
    scatter_u = Scatter(keep_u, (u1, u2, u3, u4), (sent_u, got_u))
    loads = [
        pltpu.make_async_copy(source, target, load_sems.at[i])
        for i, (source, target) in enumerate(((dm_hbm, dm), (hr_hbm, hr), (dz_hbm, total), (n1_hbm, n1)))
    ]

    @pl.when(j == 0)
    def _():
        for copy in loads:
            copy.start()
        greet()
        vec_ref[...] = jnp.zeros_like(vec_ref)
        vec_ref[0:3, :] = sums_ref[0:3, :]
        loads[0].wait()
        turn(dm, dm_turned)
        loads[1].wait()
        turn(hr, hr_turned)

    def out_copy(m):
        return pltpu.make_async_copy(keep_u.at[m], up_hbm.at[m - early], local_u.at[m])

    def columns(m):
        return pl.ds(pl.multiple_of(m * width, width), width)

    def finish_d(m):
        down_ref[:, columns(m)] = scatter_d.last(m)

    def finish_u(m):
        up_ref[:, columns(m)] = scatter_u.last(m)

    def pair_down(m):
        pair_d.add(m)
        scatter_d.copy(1, m).start()

    def pair_up(m):
        pair_u.add(m)

        @pl.when(m < early)
        def _():
            scatter_u.copy(1, m).start()

        @pl.when(m >= early)
        def _():
            out_copy(m).start()

    def tick(n):
        due(n, FFN_DOWN[4], finish_d)
        for stage in (3, 2, 1):
            due(n, FFN_DOWN[stage], lambda m: scatter_d.step(stage, m))
        due(n, FFN_UP[4], finish_u)
        for stage in (3, 2, 1):
            due(n, FFN_UP[stage], lambda m: scatter_u.step(stage, m))
        due(n, FFN_DOWN[0], pair_down)
        due(n, FFN_UP[0], pair_up)

    fast = j < steps // 2
    base = jnp.where(fast, 6 * j, 2 * (steps // 2) + 4 * j)

    @pl.when(fast)
    def _():
        for part in range(2):
            m = 2 * j + part
            pair_d.free(m)
            for own, g_ref in ((0, g_oth), (1, g_own)):
                pair_d.store(m, dot(dm_turned[...], g_ref[:, part * width : (part + 1) * width]), own)
            pair_d.copy(m).start()
            tick(base + part)

    base = jnp.where(fast, base + 2, base)
    low = []
    for own, slope, weight in ((0, s_oth, wd_oth), (1, s_own, wd_own)):
        raised = dot_nt(dm[...], weight[...]) * slope[...].astype(jnp.float32)
        low.append(raised.astype(jnp.bfloat16))
        spot = t * own + (1 - t) * (1 - own)
        row = 6 + 2 * spot + lax.div(j, 4)
        vec_ref[pl.ds(row, 1), columns(lax.rem(j, 4))] = jnp.sum(
            low[-1].astype(jnp.float32), axis=0, keepdims=True
        )
        tick(base + own)
    pair_u.free(j)
    for own in range(2):
        pair_u.store(j, dot(hr_turned[...], low[own]), own)
    pair_u.copy(j).start()
    tick(base + 2)

    @pl.when(j == 0)
    def _():
        loads[2].wait()

    total[...] += dot_nt(low[0], wu_oth[...]) + dot_nt(low[1], wu_own[...])
    tick(base + 3)

    @pl.when(j == steps - 1)
    def _():
        loads[3].wait()
        tile = 128

        @pl.loop(0, total.shape[0] // tile)
        def _(r):
            here = pl.ds(pl.multiple_of(r * tile, tile), tile)
            upstream = total[here, :]
            normed = n1[here, :]
            grad = norm_backward(upstream, g1_ref[...], normed, scale_ref[here, 0:1])
            grad_low = grad.astype(jnp.bfloat16)
            total[here, :] = grad
            hr[here, :] = grad_low
            vec_ref[3:4, :] += jnp.sum(upstream, axis=0, keepdims=True)
            vec_ref[4:5, :] += jnp.sum(upstream * normed, axis=0, keepdims=True)
            vec_ref[5:6, :] += jnp.sum(grad_low.astype(jnp.float32), axis=0, keepdims=True)
            tick(FFN_TICKS + r)

        outs = [
            pltpu.make_async_copy(source, target, out_sems.at[i])
            for i, (source, target) in enumerate(((total, dz_out), (hr, da_out)))
        ]
        for copy in outs:
            copy.start()

        @pl.loop(FFN_TICKS + total.shape[0] // tile, FFN_END)
        def _(n):
            tick(n)

        for m in range(CHUNKS - 2, CHUNKS):
            pair_d.copy(m).wait_send()
            pair_u.copy(m).wait_send()

        @pl.loop(0, CHUNKS)
        def _(m):
            scatter_d.drain(m)

        @pl.loop(0, early)
        def _(m):
            scatter_u.drain(m)

        @pl.loop(early, CHUNKS)
        def _(m):
            out_copy(m).wait()

        for copy in outs:
            copy.wait()


def ffn_backward(
    grad_branch, hidden_rows, grad_two, normed_one, scaled_one, gain_one, sums,
    act, act2, slope, slope2, w_down, w_down2, w_up, w_up2,
):
    rows, depth = grad_branch.shape
    inner = act.shape[1]
    tile = inner // CHUNKS
    last = CHUNKS // 2 - 1
    fixed = lambda *shape: pl.BlockSpec(shape, lambda j: (0,) * len(shape))
    anywhere = pl.BlockSpec(memory_space=pl.ANY)
    double = pl.BlockSpec((rows, 2 * tile), lambda j: (0, jnp.minimum(j, last)))
    column = pl.BlockSpec((rows, tile), lambda j: (0, j))
    row = pl.BlockSpec((tile, depth), lambda j: (j, 0))
    weight_column = pl.BlockSpec((depth, tile), lambda j: (0, j))
    sems = pltpu.SemaphoreType.DMA((5, CHUNKS))
    low, f32 = jnp.bfloat16, jnp.float32
    early = EARLY_UP
    return pl.pallas_call(
        ffn_back_kernel,
        grid=(CHUNKS,),
        in_specs=[anywhere] * 4
        + [fixed(rows, 128), fixed(1, depth), fixed(8, depth)]
        + [double, double, column, column, row, row, weight_column, weight_column],
        out_specs=[
            fixed(depth // 16, inner), fixed(depth // 16, early * tile), fixed(16, depth),
            anywhere, anywhere, anywhere,
        ],
        out_shape=[
            jax.ShapeDtypeStruct((depth // 16, inner), f32),
            jax.ShapeDtypeStruct((depth // 16, early * tile), f32),
            jax.ShapeDtypeStruct((16, depth), f32),
            jax.ShapeDtypeStruct((CHUNKS - early, 2, 2, SPAN, tile), low),
            jax.ShapeDtypeStruct((rows, depth), f32),
            jax.ShapeDtypeStruct((rows, depth), low),
        ],
        scratch_shapes=[
            low_buffer(rows, depth),
            low_buffer(rows, depth),
            pltpu.VMEM((rows, depth), f32),
            low_buffer(depth, rows),
            low_buffer(depth, rows),
            pltpu.VMEM((rows, depth), f32),
            low_buffer(CHUNKS, 2, 2, SPAN, tile),
            low_buffer(2, 2, 2, SPAN, tile),
            low_buffer(CHUNKS, 2, 2, SPAN, tile),
            *land_scratch(CHUNKS, SPAN, tile),
            low_buffer(CHUNKS, 2, 2, SPAN, tile),
            low_buffer(2, 2, 2, SPAN, tile),
            low_buffer(CHUNKS, 2, 2, SPAN, tile),
            *land_scratch(early, SPAN, tile),
            sems, sems, sems, sems,
            pltpu.SemaphoreType.DMA((CHUNKS,)),
            pltpu.SemaphoreType.DMA((4,)),
            pltpu.SemaphoreType.DMA((2,)),
        ],
        compiler_params=pltpu.CompilerParams(
            vmem_limit_bytes=VMEM, collective_id=1, has_side_effects=True
        ),
        cost_estimate=pl.CostEstimate(
            flops=rows * depth * inner * 16, bytes_accessed=60 * 1024 * 1024, transcendentals=0
        ),
        name="ffn_backward",
    )(
        grad_branch, hidden_rows, grad_two, normed_one, scaled_one, gain_one.reshape(1, -1), sums,
        act, act2, slope, slope2, w_down, w_down2, w_up, w_up2,
    )


def attend_back_one(queries, key_rows, values, grad_ctx, levels):
    scale = HEAD_DIM**-0.5
    first = head_masks(128)
    keys_t = key_rows.T
    parts = []
    grad_k = grad_v = None
    for head in range(2):
        mask = first if head == 0 else jnp.logical_not(first)
        picked = jnp.where(mask, queries, jnp.zeros_like(queries))
        grad_picked = jnp.where(mask, grad_ctx, jnp.zeros_like(grad_ctx))
        weights = jnp.exp2(dot_nt(key_rows, picked) * (LOG2E * scale) - levels[head])
        grad_weights = dot_nt(values, grad_picked)
        rowsum = jnp.sum(weights * grad_weights, axis=0, keepdims=True)
        grad_low = (weights * (grad_weights - rowsum)).astype(jnp.bfloat16)
        piece_v = dot(weights.astype(jnp.bfloat16), grad_picked)
        piece_k = dot(grad_low, picked)
        grad_v = piece_v if grad_v is None else grad_v + piece_v
        grad_k = piece_k if grad_k is None else grad_k + piece_k
        parts.append(dot(keys_t[head * HEAD_DIM : (head + 1) * HEAD_DIM], grad_low))
    grad_q = jnp.concatenate(parts, axis=0).T
    return (
        (grad_q * scale).astype(jnp.bfloat16),
        (grad_k * scale).astype(jnp.bfloat16),
        grad_v.astype(jnp.bfloat16),
    )


class Total:
    def __init__(self, sums, lands, sems):
        self.sums, self.lands = sums, lands
        self.sent, self.got = sems

    def copy(self, stage):
        dp, t = mine()
        peer = ((flip(dp, 1), t), (dp, 1 - t), (flip(dp, 2), t), (flip(dp, 4), t), (flip(dp, 8), t))[stage]
        return pltpu.make_async_remote_copy(
            src_ref=self.sums.at[stage],
            dst_ref=self.lands.at[stage],
            send_sem=self.sent.at[stage],
            recv_sem=self.got.at[stage],
            device_id=peer,
            device_id_type=MESH,
        )

    def step(self, stage):
        self.copy(stage).wait_recv()
        self.sums[stage + 1] = self.sums[stage] + self.lands[stage]
        if stage < 4:
            self.copy(stage + 1).start()

    def drain(self):
        for stage in range(5):
            self.copy(stage).wait_send()


def attend_back_kernel(
    da_hbm, x_hbm, up_hbm, dz_hbm, wq_own_hbm, wq_oth_hbm, vec_ref, level_ref,
    qkv_own, c_own, wo_own, qkv_oth, c_oth, wo_oth,
    gin_hbm, gup_ref, gout_ref, gqkv_ref, vec_out, bias_out,
    da, xs, da_turned, x_turned, total, stack, wq,
    keep_u, u1, u2, u3, u4,
    keep_a, send_a, land_a, a1, a2, a3, a4,
    vec_sums, vec_lands, bias_sums, bias_lands,
    sent_u, got_u, sent_a, got_a, sent_v, got_v, sent_b, got_b, local_u, load_sems, out_sems,
):
    g = pl.program_id(0)
    steps = pl.num_programs(0)
    seqs = xs.shape[0] // SEQ
    late = keep_u.shape[0]
    n_chunks = keep_a.shape[0]
    pair = Pair(keep_a, send_a, land_a, (sent_a, got_a))
    scatter_a = Scatter(keep_a, (a1, a2, a3, a4), (sent_a, got_a))
    scatter_u = Scatter(keep_u, (u1, u2, u3, u4), (sent_u, got_u))
    vec_total = Total(vec_sums, vec_lands, (sent_v, got_v))
    bias_total = Total(bias_sums, bias_lands, (sent_b, got_b))
    _, t = mine()

    def load_up(m):
        return pltpu.make_async_copy(up_hbm.at[m], keep_u.at[m], local_u.at[m])

    pairs = ((x_hbm, xs), (da_hbm, da), (dz_hbm, total), (wq_oth_hbm, wq.at[0]), (wq_own_hbm, wq.at[1]))
    loads = [pltpu.make_async_copy(*ends, load_sems.at[i]) for i, ends in enumerate(pairs)]

    @pl.when(g == 0)
    def _():
        for m in range(late):
            load_up(m).start()
        for copy in loads:
            copy.start()
        greet()
        for m in range(late):
            load_up(m).wait()
            scatter_u.copy(1, jnp.int32(m)).start()
        vec_sums[0] = vec_ref[...]
        vec_total.copy(0).start()
        bias_sums[0] = jnp.zeros_like(bias_sums[0])
        loads[1].wait()
        turn(da, da_turned)
        loads[0].wait()
        turn(xs, x_turned)

    def finish_u(m):
        width = keep_u.shape[4]
        gup_ref[:, pl.ds(pl.multiple_of(m * width, width), width)] = scatter_u.last(m)

    def finish_a(m):
        done = scatter_a.last(m)
        kind = lax.rem(m, 4)
        cols = pl.ds(pl.multiple_of(lax.div(m, 4) * 128, 128), 128)

        @pl.when(kind == 0)
        def _():
            gout_ref[:, cols] = done

        @pl.when(kind > 0)
        def _():
            gqkv_ref[jnp.maximum(kind - 1, 0), :, cols] = done

    def pair_a(m):
        pair.add(m)
        scatter_a.copy(1, m).start()

    def tick(n):
        due(n, ATT_UP[4], finish_u)
        for stage in (3, 2, 1):
            due(n, ATT_UP[stage], lambda m: scatter_u.step(stage, m))
        due(n, ATT_OWN[4], finish_a)
        for stage in (3, 2, 1):
            due(n, ATT_OWN[stage], lambda m: scatter_a.step(stage, m))
        due(n, ATT_OWN[0], pair_a)

    base = 8 * g
    cols = pl.ds(pl.multiple_of(g * 128, 128), 128)

    def emit(kind, turned, other, own):
        m = 4 * g + kind
        pair.free(m)
        product = dot(turned[...], jnp.concatenate([other, own], axis=1))
        pair.store(m, product[:, :128], 0)
        pair.store(m, product[:, 128:], 1)
        pair.copy(m).start()

    emit(0, da_turned, c_oth[...], c_own[...])
    tick(base)
    for own, qkv_ref, wo_ref in ((0, qkv_oth, wo_oth), (1, qkv_own, wo_own)):
        grad_ctx = dot_nt(da[...], wo_ref[...]).astype(jnp.bfloat16)
        for s in range(seqs):
            rows = slice(s * SEQ, (s + 1) * SEQ)
            levels = [level_ref[own, s, pl.ds(2 * g + head, 1), :] for head in range(2)]
            grads = attend_back_one(
                qkv_ref[0, rows, :], qkv_ref[1, rows, :], qkv_ref[2, rows, :], grad_ctx[rows], levels
            )
            for kind in range(3):
                stack[own * 3 + kind, rows, cols] = grads[kind]
            if s == seqs - 1:
                spot = t * own + (1 - t) * (1 - own)
                where = pl.ds(pl.multiple_of(spot * 512 + g * 128, 128), 128)
                for row, kind in ((0, 0), (1, 2)):
                    bias_sums[0, row : row + 1, where] = jnp.sum(
                        stack[own * 3 + kind, :, cols].astype(jnp.float32), axis=0, keepdims=True
                    )
            tick(base + 1 + own * 2 + min(s, 1))

    @pl.when(g == steps - 1)
    def _():
        bias_total.copy(0).start()

    for kind in range(1, 4):
        emit(kind, x_turned, stack[kind - 1, :, cols], stack[kind + 2, :, cols])
        tick(base + 4 + kind)
    for stage in range(3):
        @pl.when(g == stage)
        def _():
            vec_total.step(stage)

    @pl.when(g == steps - 1)
    def _():
        for copy in loads[2:]:
            copy.wait()
        vec_total.step(3)
        tile = xs.shape[0] // 4
        outs = []
        for r in range(4):
            here = slice(r * tile, (r + 1) * tile)
            block = total[here, :]
            for own in range(2):
                for kind in range(3):
                    block = block + dot_nt(stack[own * 3 + kind, here, :], wq[own, kind])
            total[here, :] = block
            outs.append(pltpu.make_async_copy(total.at[here], gin_hbm.at[here], out_sems.at[r]))
            outs[-1].start()
            tick(jnp.int32(ATT_TICKS + r))
            bias_total.step(r)
            if r == 0:
                vec_total.step(4)
        bias_total.step(4)

        @pl.loop(ATT_TICKS + 4, ATT_END)
        def _(n):
            tick(n)

        vec_out[...] = vec_sums[5]
        bias_out[...] = bias_sums[5]
        for m in range(pair.slots):
            pair.copy(n_chunks - 1 - m).wait_send()

        @pl.loop(0, late)
        def _(m):
            scatter_u.drain(m)

        @pl.loop(0, n_chunks)
        def _(m):
            scatter_a.drain(m)

        vec_total.drain()
        bias_total.drain()
        for copy in outs:
            copy.wait()


def attend_backward(grad_attended, tokens, keep_up, grad_one, vectors, levels, w_qkv, w_qkv2, own, other):
    rows, depth = tokens.shape
    width = own[1].shape[1]
    steps = width // 128
    late, tile = keep_up.shape[0], keep_up.shape[4]
    n_chunks = 4 * steps
    fixed = lambda *shape: pl.BlockSpec(shape, lambda g: (0,) * len(shape))
    anywhere = pl.BlockSpec(memory_space=pl.ANY)
    side = [
        pl.BlockSpec((3, rows, 128), lambda g: (0, 0, g)),
        pl.BlockSpec((rows, 128), lambda g: (0, g)),
        pl.BlockSpec((128, depth), lambda g: (g, 0)),
    ]
    sems_u = pltpu.SemaphoreType.DMA((5, late))
    sems_a = pltpu.SemaphoreType.DMA((5, n_chunks))
    few = pltpu.SemaphoreType.DMA((5,))
    f32 = jnp.float32
    return pl.pallas_call(
        attend_back_kernel,
        grid=(steps,),
        in_specs=[anywhere] * 6 + [fixed(*vectors.shape), fixed(*levels.shape)] + side + side,
        out_specs=[
            anywhere, fixed(depth // 16, late * tile), fixed(depth // 16, width),
            fixed(3, depth // 16, width), fixed(*vectors.shape), fixed(8, depth),
        ],
        out_shape=[
            jax.ShapeDtypeStruct((rows, depth), f32),
            jax.ShapeDtypeStruct((depth // 16, late * tile), f32),
            jax.ShapeDtypeStruct((depth // 16, width), f32),
            jax.ShapeDtypeStruct((3, depth // 16, width), f32),
            jax.ShapeDtypeStruct(vectors.shape, f32),
            jax.ShapeDtypeStruct((8, depth), f32),
        ],
        scratch_shapes=[
            low_buffer(rows, depth),
            low_buffer(rows, depth),
            low_buffer(depth, rows),
            low_buffer(depth, rows),
            pltpu.VMEM((rows, depth), f32),
            low_buffer(6, rows, width),
            low_buffer(2, 3, depth, width),
            low_buffer(late, 2, 2, SPAN, tile),
            *land_scratch(late, SPAN, tile),
            low_buffer(n_chunks, 2, 2, SPAN, 128),
            low_buffer(4, 2, 2, SPAN, 128),
            low_buffer(n_chunks, 2, 2, SPAN, 128),
            *land_scratch(n_chunks, SPAN, 128),
            pltpu.VMEM((6, *vectors.shape), f32),
            pltpu.VMEM((5, *vectors.shape), f32),
            pltpu.VMEM((6, 8, depth), f32),
            pltpu.VMEM((5, 8, depth), f32),
            sems_u, sems_u, sems_a, sems_a, few, few, few, few,
            pltpu.SemaphoreType.DMA((late,)),
            pltpu.SemaphoreType.DMA((5,)),
            pltpu.SemaphoreType.DMA((4,)),
        ],
        compiler_params=pltpu.CompilerParams(
            vmem_limit_bytes=VMEM, collective_id=2, has_side_effects=True
        ),
        cost_estimate=pl.CostEstimate(
            flops=rows * depth * width * 40, bytes_accessed=60 * 1024 * 1024, transcendentals=0
        ),
        name="attend_backward",
    )(
        grad_attended, tokens, keep_up, grad_one, w_qkv, w_qkv2, vectors, levels, *own, *other,
    )


def deliver_kernel(
    gin, res, up_a, up_b, down, out, qkv, vec, bias,
    o_gin, o_res, o_up, o_down, o_out, o_qkv, *vectors,
):
    o_gin[...] = gin[...]
    o_res[...] = res[...]

    @pl.when(pl.program_id(0) == 0)
    def _():
        cols = up_a.shape[1]
        o_up[:, :cols] = up_a[...]
        o_up[:, cols:] = up_b[...]
        o_down[...] = down[...]
        o_out[...] = out[...]
        o_qkv[...] = qkv[...]
        for row in range(6):
            vectors[row][...] = vec[row : row + 1, :]
        wide = vec.shape[1]
        for row in range(4):
            vectors[6][:, row * wide : (row + 1) * wide] = vec[6 + row : 7 + row, :]
        vectors[7][...] = bias[0:1, :]
        vectors[8][...] = bias[1:2, :]


def deliver(gin, res, up_a, up_b, down, out, qkv, vec, bias):
    steps = 4
    wide = vec.shape[1]
    like = lambda array: jax.ShapeDtypeStruct(array.shape, array.dtype)
    flat = lambda size: jax.ShapeDtypeStruct((1, size), jnp.float32)
    fixed = lambda array: pl.BlockSpec(array.shape, lambda i: (0,) * len(array.shape))
    tall = pl.BlockSpec((gin.shape[0] // steps, gin.shape[1]), lambda i: (i, 0))
    up = jax.ShapeDtypeStruct((up_a.shape[0], up_a.shape[1] + up_b.shape[1]), jnp.float32)
    flats = [flat(wide)] * 6 + [flat(4 * wide)] + [flat(wide)] * 2
    small = [up, like(down), like(out), like(qkv)] + flats
    return pl.pallas_call(
        deliver_kernel,
        grid=(steps,),
        in_specs=[tall, tall] + [fixed(array) for array in (up_a, up_b, down, out, qkv, vec, bias)],
        out_specs=[tall, tall] + [fixed(array) for array in small],
        out_shape=[like(gin), like(res)] + small,
        compiler_params=pltpu.CompilerParams(vmem_limit_bytes=VMEM),
        name="deliver",
    )(gin, res, up_a, up_b, down, out, qkv, vec, bias)


def attend_one(queries, key_rows, values):
    first = head_masks(128)
    values_t = values.T
    parts, levels = [], []
    for head in range(2):
        mask = first if head == 0 else jnp.logical_not(first)
        picked = jnp.where(mask, queries, jnp.zeros_like(queries))
        scores = dot_nt(key_rows, picked) * (LOG2E * HEAD_DIM**-0.5)
        peak = jnp.max(scores, axis=0, keepdims=True)
        lifted = jnp.exp2(scores - peak)
        totals = jnp.sum(lifted, axis=0, keepdims=True)
        context = dot(values_t[head * HEAD_DIM : (head + 1) * HEAD_DIM], lifted.astype(jnp.bfloat16))
        parts.append(context * (1.0 / totals))
        levels.append(peak + jnp.log2(totals))
    return jnp.concatenate(parts, axis=0).T.astype(jnp.bfloat16), levels


class Fetch:
    HOPS = 9

    def __init__(self, source, target, unit, index, sems):
        self.source, self.target, self.unit, self.index = source, target, unit, index
        self.sent, self.got = sems

    def copy(self, hop):
        dp, t = mine()
        core, x, z = bit_of(dp, 1), bit_of(dp, 2), bit_of(dp, 4)
        quarter = {0: x * 2 + z, 1: (1 - x) * 2 + z, 2: x * 2 + 1 - z, 3: (1 - x) * 2 + 1 - z}
        if hop == 0:
            which, part, peer = 0, None, (dp, 1 - t)
        elif hop == 1:
            which, part, peer = 0, None, (flip(dp, 2), t)
        elif hop == 2:
            which, part, peer = 0, None, (flip(dp, 4), t)
        elif hop == 3:
            which, part, peer = 2, 0, (flip(dp, 2), t)
        elif hop == 4:
            which, part, peer = 1, 1, (flip(dp, 4), t)
        else:
            which, part, peer = hop - 5, None, (flip(dp, 1), t)
        place = self.unit(core, quarter[which], part)
        origin = self.source if hop == 0 else self.target
        return pltpu.make_async_remote_copy(
            src_ref=origin.at[place],
            dst_ref=self.target.at[place],
            send_sem=self.sent.at[self.index, hop],
            recv_sem=self.got.at[self.index, hop],
            device_id=peer,
            device_id_type=MESH,
        )

    def start(self, *hops):
        for hop in hops:
            self.copy(hop).start()

    def arrive(self, *hops):
        for hop in hops:
            self.copy(hop).wait_recv()

    def advance(self, stage):
        if stage == 1:
            self.arrive(0)
            self.start(1, 2, 5)
        elif stage == 2:
            self.arrive(1, 2)
            self.start(3, 4, 6, 7)
        elif stage == 3:
            self.arrive(3, 4)
            self.start(8)
        else:
            self.arrive(5, 6, 7, 8)

    def drain(self):
        for hop in range(self.HOPS):
            self.copy(hop).wait_send()


AHEAD = 3


def unit_of(total, lead=(), base=0, tail=()):
    def unit(core, quarter, part):
        size = total // 8
        start = base + core * (total // 2) + quarter * size
        if part is not None:
            size //= 2
            start = start + part * size
        return (*lead, pl.ds(pl.multiple_of(start, 16), size), *tail)

    return unit


def forward_kernel(
    x_hbm, cot_hbm, wq_hbm, wo_hbm, wu_hbm, wd_hbm,
    bq_ref, bv_ref, bu_ref, bo_ref, g1_ref, s1_ref, bd_ref, g2_ref, s2_ref,
    qkv_out1, qkv_out0, ctx_out1, ctx_out0, act_out1, act_out0, slope_out1, slope_out0,
    hr_out, n1_out, dm_out, dz_out, res_out, wq_out, wo_out, wu_out, wd_out,
    level_ref, scale_ref, sums_ref,
    x, cot, wq1, wq0, wo1, wo0, wu1, wu0, wd1, wd0, qkv1, qkv0, ctx1, ctx0, n1, hr, total, act, slope,
    bias_own, bias_oth, sent, got, bias_sent, bias_got, load_sems, out_sems,
):
    dp, t = mine()
    rows, depth = x.shape
    seqs = rows // SEQ
    width = ctx1.shape[1]
    inner = wu1.shape[1]
    tiles = 4
    span = inner // tiles

    chunks = []

    def chunk(source, target, unit):
        chunks.append(Fetch(source, target, unit, len(chunks), (sent, got)))
        return len(chunks) - 1

    c_qkv = [chunk(wq_hbm, wq0, unit_of(depth, lead=(kind,))) for kind in range(3)]
    c_out = chunk(wo_hbm, wo0, unit_of(width))
    c_up, c_down = [], []
    for j in range(tiles):
        c_up.append(chunk(wu_hbm, wu0, unit_of(depth, tail=(pl.ds(j * span, span),))))
        c_down.append(chunk(wd_hbm, wd0, unit_of(span, base=j * span)))

    loads, outs, done = {}, [], []

    def finish(copy):
        copy.wait()
        done.append(copy)

    def load(name, source, target):
        copy = pltpu.make_async_copy(source, target, load_sems.at[len(loads)])
        loads[name] = copy
        copy.start()

    def save(source, target):
        copy = pltpu.make_async_copy(source, target, out_sems.at[len(outs)])
        outs.append(copy)
        copy.start()
        return copy

    load("x", x_hbm, x)
    for kind in range(3):
        load(("q", kind), wq_hbm.at[kind], wq1.at[kind])
    greet()
    ahead = AHEAD
    for m in range(ahead):
        chunks[m].start(0)
    bias_own[:, :width] = bq_ref[...]
    bias_own[:, width : 2 * width] = bv_ref[...]
    bias_own[:, 2 * width :] = bu_ref[...]
    bias_copy = pltpu.make_async_remote_copy(
        src_ref=bias_own, dst_ref=bias_oth, send_sem=bias_sent, recv_sem=bias_got,
        device_id=(dp, 1 - t), device_id_type=MESH,
    )
    bias_copy.start()
    load("o", wo_hbm, wo1)
    load("u", wu_hbm, wu1)
    load("d", wd_hbm, wd1)
    load("cot", cot_hbm, cot)

    events = []
    for m in range(len(chunks)):
        for stage, lag in ((1, 7.0), (2, 13.0), (3, 17.0), (4, 20.0)):
            events.append((lag + 4.3 * m, stage, m))
    events.sort()
    saves = {}
    for kind in range(3):
        saves[c_qkv[kind]] = (wq0.at[kind], wq_out.at[kind])
    saves[c_out] = (wo0, wo_out)
    for j in range(tiles):
        cols = pl.ds(j * span, span)
        saves[c_up[j]] = (wu0.at[:, cols], wu_out.at[:, cols])
        saves[c_down[j]] = (wd0.at[cols], wd_out.at[cols])

    def event():
        _, stage, m = events.pop(0)
        chunks[m].advance(stage)
        if stage == 1 and m + ahead < len(chunks):
            chunks[m + ahead].start(0)
        if stage == 4:
            save(*saves[m])

    clock = [0.0]

    def spend(us):
        clock[0] += us
        while events and events[0][0] <= clock[0]:
            event()

    def need(m):
        while any(e[1] == 4 and e[2] == m for e in events):
            clock[0] = max(clock[0], events[0][0])
            event()

    def project(weights, kind, kept, biases):
        product = dot(x[...], weights[kind])
        if kind != 1:
            at = 0 if kind == 0 else width
            product = product + biases[:, at : at + width]
        kept[kind] = product.astype(jnp.bfloat16)

    def attend(side, kept, context, pair):
        cols = slice(pair * 128, pair * 128 + 128)

        @pl.loop(0, seqs)
        def _(s):
            here = pl.ds(pl.multiple_of(s * SEQ, SEQ), SEQ)
            out, levels = attend_one(kept[0, here, cols], kept[1, here, cols], kept[2, here, cols])
            context[here, cols] = out
            for head in range(2):
                spot = 2 * pair + head
                level_ref[side, s, spot : spot + 1, :] = levels[head]

    loads["x"].wait()
    for kind in range(3):
        loads[("q", kind)].wait()
        project(wq1, kind, qkv1, bias_own)
        spend(1.6)
    save(qkv1, qkv_out1)
    for pair in range(width // 128):
        attend(1, qkv1, ctx1, pair)
        spend(2.7)
    save(ctx1, ctx_out1)
    bias_copy.wait_recv()
    for kind in range(3):
        need(c_qkv[kind])
        project(wq0, kind, qkv0, bias_oth)
        spend(1.6)
    save(qkv0, qkv_out0)
    for pair in range(width // 128):
        attend(0, qkv0, ctx0, pair)
        spend(2.7)
    save(ctx0, ctx_out0)
    loads["o"].wait()
    need(c_out)
    step = 256

    @pl.loop(0, rows // step)
    def _(r):
        here = pl.ds(pl.multiple_of(r * step, step), step)
        attended = dot(ctx1[here, :], wo1[...]) + dot(ctx0[here, :], wo0[...])
        _, normed, scaled = norm_forward(
            x[here, :].astype(jnp.float32) + attended + bo_ref[...], g1_ref[...], s1_ref[...]
        )
        n1[here, :] = normed
        hr[here, :] = (normed * g1_ref[...] + s1_ref[...]).astype(jnp.bfloat16)
        scale_ref[here, :] = jnp.broadcast_to(scaled, (step, 128))

    save(n1, n1_out)
    hr_saved = save(hr, hr_out)
    spend(5.0)
    loads["u"].wait()
    loads["d"].wait()
    big = 512
    slots = []
    for side, up, down, biases, act_out, slope_out in (
        (1, wu1, wd1, bias_own, act_out1, slope_out1),
        (0, wu0, wd0, bias_oth, act_out0, slope_out0),
    ):
        for j in range(tiles):
            cols = pl.ds(j * span, span)
            slot = len(slots) % 2
            if len(slots) >= 2:
                for copy in slots[-2]:
                    finish(copy)
            if side == 0:
                need(c_up[j])
                need(c_down[j])
            bias = biases[:, 2 * width + j * span : 2 * width + (j + 1) * span]
            fresh = not slots

            @pl.loop(0, rows // big)
            def _(r):
                here = pl.ds(pl.multiple_of(r * big, big), big)
                activated, leaning = gelu_pair(dot(hr[here, :], up[:, cols]) + bias)
                activated = activated.astype(jnp.bfloat16)
                act[slot, here, :] = activated
                slope[slot, here, :] = leaning.astype(jnp.bfloat16)
                product = dot(activated, down[cols, :])
                total[here, :] = product if fresh else total[here, :] + product

            slots.append((
                save(act.at[slot], act_out.at[:, cols]),
                save(slope.at[slot], slope_out.at[:, cols]),
            ))
            spend(3.6)
    while events:
        event()
    finish(hr_saved)
    loads["cot"].wait()
    sums_ref[...] = jnp.zeros_like(sums_ref)

    @pl.loop(0, rows // step)
    def _(r):
        here = pl.ds(pl.multiple_of(r * step, step), step)
        hidden = n1[here, :] * g1_ref[...] + s1_ref[...]
        result, normed, scaled = norm_forward(hidden + total[here, :] + bd_ref[...], g2_ref[...], s2_ref[...])
        x[here, :] = result.astype(jnp.bfloat16)
        upstream = cot[here, :].astype(jnp.float32)
        grad = norm_backward(upstream, g2_ref[...], normed, scaled)
        total[here, :] = grad
        low = grad.astype(jnp.bfloat16)
        hr[here, :] = low
        sums_ref[0:1, :] += jnp.sum(upstream, axis=0, keepdims=True)
        sums_ref[1:2, :] += jnp.sum(upstream * normed, axis=0, keepdims=True)
        sums_ref[2:3, :] += jnp.sum(low.astype(jnp.float32), axis=0, keepdims=True)

    save(x, res_out)
    save(hr, dm_out)
    save(total, dz_out)
    bias_copy.wait_send()
    for fetch in chunks:
        fetch.drain()
    for copy in outs:
        if not any(copy is other for other in done):
            copy.wait()


def forward(tokens, cotangent, w_qkv, w_out, w_up, w_down, biases, bias_o, gain_one, shift_one, bias_down, gain_two, shift_two):
    rows, depth = tokens.shape
    width, inner = w_out.shape[0], w_up.shape[1]
    seqs, heads = rows // SEQ, width // HEAD_DIM
    low, f32 = jnp.bfloat16, jnp.float32
    any_space = pl.BlockSpec(memory_space=pl.ANY)
    near = pl.BlockSpec(memory_space=pltpu.VMEM)
    qkv = (3, rows, width)
    outs = [
        (qkv, low), (qkv, low), ((rows, width), low), ((rows, width), low),
        ((rows, inner), low), ((rows, inner), low), ((rows, inner), low), ((rows, inner), low),
        ((rows, depth), low), ((rows, depth), f32), ((rows, depth), low), ((rows, depth), f32), ((rows, depth), low),
        (w_qkv.shape, low), (w_out.shape, low), (w_up.shape, low), (w_down.shape, low),
        ((2, seqs, heads, SEQ), f32), ((rows, 128), f32), ((8, depth), f32),
    ]
    span = inner // 4
    flat = (1, 2 * width + inner)
    scratch = [
        ((rows, depth), low), ((rows, depth), low), (w_qkv.shape, low), (w_qkv.shape, low),
        (w_out.shape, low), (w_out.shape, low), (w_up.shape, low), (w_up.shape, low),
        (w_down.shape, low), (w_down.shape, low), (qkv, low), (qkv, low),
        ((rows, width), low), ((rows, width), low), ((rows, depth), f32), ((rows, depth), low),
        ((rows, depth), f32), ((2, rows, span), low), ((2, rows, span), low), (flat, f32), (flat, f32),
    ]
    sems = pltpu.SemaphoreType.DMA((12, Fetch.HOPS))
    one = pltpu.SemaphoreType.DMA
    return pl.pallas_call(
        forward_kernel,
        in_specs=[any_space] * 6 + [near] * 9,
        out_specs=[any_space] * 17 + [near] * 3,
        out_shape=[jax.ShapeDtypeStruct(*out) for out in outs],
        scratch_shapes=[pltpu.VMEM(*buffer) for buffer in scratch]
        + [sems, sems, one, one, pltpu.SemaphoreType.DMA((8,)), pltpu.SemaphoreType.DMA((40,))],
        compiler_params=pltpu.CompilerParams(
            vmem_limit_bytes=60 * 1024 * 1024, collective_id=3, has_side_effects=True
        ),
        cost_estimate=pl.CostEstimate(
            flops=rows * depth * (width * 16 + inner * 8), bytes_accessed=80 * 1024 * 1024, transcendentals=0
        ),
        name="forward",
    )(
        tokens, cotangent, w_qkv, w_out, w_up, w_down,
        *(v.reshape(1, -1) for v in (*biases, bias_o, gain_one, shift_one, bias_down, gain_two, shift_two)),
    )


def body(mesh, *args):
    tokens, w_qkv = args[0], args[2]
    n_dp, n_tensor = mesh.shape["dp"], mesh.shape["tensor"]
    local = (*tokens.shape, w_qkv.shape[2], args[9].shape[1])
    if (n_dp, n_tensor) == (16, 2) and local == (1024, 1024, 512, 2048):
        return body_tokens(*args)
    return body_tensor(*args)


def body_tokens(
    tokens,
    cotangent,
    w_qkv,
    bias_q,
    bias_v,
    w_out,
    bias_o,
    gain_one,
    shift_one,
    w_up,
    bias_up,
    w_down,
    bias_down,
    gain_two,
    shift_two,
):
    (
        qkv, qkv2, ctx, ctx2, active, active2, slope, slope2,
        hidden_rows, normed_one, grad_branch, grad_two, result,
        w_qkv2, w_out2, w_up2, w_down2, levels, scaled_one, sums,
    ) = forward(
        tokens, cotangent, w_qkv, w_out, w_up, w_down, (bias_q, bias_v, bias_up),
        bias_o, gain_one, shift_one, bias_down, gain_two, shift_two,
    )
    grad_down, up_early, vectors, keep_up, grad_one, grad_attended = ffn_backward(
        grad_branch, hidden_rows, grad_two, normed_one, scaled_one, gain_one, sums,
        active, active2, slope, slope2, w_down, w_down2, w_up, w_up2,
    )
    grad_input, up_late, grad_out, grad_qkv, vectors, biases = attend_backward(
        grad_attended, tokens, keep_up, grad_one, vectors, levels, w_qkv, w_qkv2,
        (qkv, ctx, w_out), (qkv2, ctx2, w_out2),
    )
    grad_input, result, grad_up, grad_down, grad_out, grad_qkv, *vectors = deliver(
        grad_input, result, up_early, up_late, grad_down, grad_out, grad_qkv, vectors, biases
    )
    g_shift_two, g_gain_two, g_bias_down, g_shift_one, g_gain_one, g_bias_o, g_bias_up, g_bias_q, g_bias_v = (
        vector.reshape(-1) for vector in vectors
    )
    return (
        result,
        grad_input,
        grad_qkv,
        g_bias_q,
        g_bias_v,
        grad_out.T,
        g_bias_o,
        g_gain_one,
        g_shift_one,
        grad_up,
        g_bias_up,
        grad_down.T,
        g_bias_down,
        g_gain_two,
        g_shift_two,
    )


def solution(mesh):
    in_specs = (
        P(("dp", "tensor"), None),
        P(("dp", "tensor"), None),
        P(None, None, "tensor"),
        P("tensor"),
        P("tensor"),
        P("tensor", None),
        P(),
        P(),
        P(),
        P(None, "tensor"),
        P("tensor"),
        P("tensor", None),
        P(),
        P(),
        P(),
    )
    out_specs = (
        P(("dp", "tensor"), None),
        P(("dp", "tensor"), None),
        P(None, "dp", "tensor"),
        P(),
        P(),
        P("tensor", "dp"),
        P(),
        P(),
        P(),
        P("dp", "tensor"),
        P(),
        P("tensor", "dp"),
        P(),
        P(),
        P(),
    )
    return jax.shard_map(functools.partial(body, mesh), mesh=mesh, in_specs=in_specs, out_specs=out_specs, check_vma=False)
```

```python
import functools

import jax
import jax.numpy as jnp
from jax import lax
from jax.experimental import pallas as pl
from jax.experimental.pallas import tpu as pltpu
from jax.sharding import PartitionSpec as P

D = 1024
FF = 4096
HEAD_DIM = 64
SEQ = 512


def gelu_pair(inner_pre):
    normal_cdf = 0.5 * (1.0 + jax.scipy.special.erf(inner_pre * 0.7071067811865476))
    density = jnp.exp(-0.5 * inner_pre * inner_pre) * 0.3989422804014327
    return (inner_pre * normal_cdf, normal_cdf + inner_pre * density)


def norm_forward(summed, gain, shift):
    centre = summed - jnp.mean(summed, axis=-1, keepdims=True)
    scaled = lax.rsqrt(jnp.mean(centre * centre, axis=-1, keepdims=True) + 1e-05)
    normed = centre * scaled
    return (normed * gain + shift, normed, scaled)


def norm_backward(upstream, gain, normed, scaled):
    grad_norm = upstream * gain
    return scaled * (
        grad_norm
        - jnp.mean(grad_norm, axis=-1, keepdims=True)
        - normed * jnp.mean(grad_norm * normed, axis=-1, keepdims=True)
    )


def attend_block(block):
    queries, key_rows, values = block
    scores = jnp.einsum(
        "qhd,khd->hqk", queries, key_rows, preferred_element_type=jnp.float32
    ) * HEAD_DIM ** (-0.5)
    peak_score = jnp.max(scores, axis=-1, keepdims=True)
    lifted = jnp.exp(scores - peak_score)
    totals = jnp.sum(lifted, axis=-1, keepdims=True)
    weights = (lifted / totals).astype(jnp.bfloat16)
    context = jnp.einsum("hqk,khd->qhd", weights, values, preferred_element_type=jnp.float32)
    return (context.astype(jnp.bfloat16), (peak_score + jnp.log(totals))[..., 0])


def attend_back(block):
    queries, key_rows, values, logsum, grad_ctx = block
    scale = HEAD_DIM ** (-0.5)
    scores = (
        jnp.einsum("qhd,khd->hqk", queries, key_rows, preferred_element_type=jnp.float32) * scale
    )
    weights = jnp.exp(scores - logsum[..., None])
    grad_weights = jnp.einsum("qhd,khd->hqk", grad_ctx, values, preferred_element_type=jnp.float32)
    grad_scores = weights * (grad_weights - jnp.sum(weights * grad_weights, axis=-1, keepdims=True))
    grad_low = grad_scores.astype(jnp.bfloat16)
    grad_v = jnp.einsum(
        "hqk,qhd->khd", weights.astype(jnp.bfloat16), grad_ctx, preferred_element_type=jnp.float32
    )
    grad_q = (
        jnp.einsum("hqk,khd->qhd", grad_low, key_rows, preferred_element_type=jnp.float32) * scale
    )
    grad_k = (
        jnp.einsum("hqk,qhd->khd", grad_low, queries, preferred_element_type=jnp.float32) * scale
    )
    return (grad_q.astype(jnp.bfloat16), grad_k.astype(jnp.bfloat16), grad_v.astype(jnp.bfloat16))


def body_tensor(
    tokens,
    cotangent,
    w_qkv,
    bias_q,
    bias_v,
    w_out,
    bias_o,
    gain_one,
    shift_one,
    w_up,
    bias_up,
    w_down,
    bias_down,
    gain_two,
    shift_two,
):
    rank = lax.axis_index("tensor")
    full_rows = lax.all_gather(tokens, "tensor", axis=0, tiled=True)
    group_rows = full_rows.shape[0]
    local_width = w_qkv.shape[2]
    head_shape = (group_rows // SEQ, SEQ, local_width // HEAD_DIM, HEAD_DIM)
    projected = jnp.einsum("td,kde->kte", full_rows, w_qkv, preferred_element_type=jnp.float32)
    queries = (projected[0] + bias_q).astype(jnp.bfloat16).reshape(head_shape)
    key_rows = projected[1].astype(jnp.bfloat16).reshape(head_shape)
    values = (projected[2] + bias_v).astype(jnp.bfloat16).reshape(head_shape)
    context, logsum = lax.map(attend_block, (queries, key_rows, values))
    context = context.reshape(group_rows, local_width)
    attended = (
        lax.psum_scatter(
            jnp.dot(context, w_out, preferred_element_type=jnp.float32),
            "tensor",
            scatter_dimension=0,
            tiled=True,
        )
        + bias_o
    )
    hidden_one, normed_one, scaled_one = norm_forward(
        tokens.astype(jnp.float32) + attended, gain_one, shift_one
    )
    hidden_rows = lax.all_gather(hidden_one.astype(jnp.bfloat16), "tensor", axis=0, tiled=True)
    inner_pre = jnp.dot(hidden_rows, w_up, preferred_element_type=jnp.float32) + bias_up
    activated, slope = gelu_pair(inner_pre)
    active_low = activated.astype(jnp.bfloat16)
    branch = (
        lax.psum_scatter(
            jnp.dot(active_low, w_down, preferred_element_type=jnp.float32),
            "tensor",
            scatter_dimension=0,
            tiled=True,
        )
        + bias_down
    )
    result, normed_two, scaled_two = norm_forward(hidden_one + branch, gain_two, shift_two)
    upstream = cotangent.astype(jnp.float32)
    grad_two = norm_backward(upstream, gain_two, normed_two, scaled_two)
    grad_branch = grad_two.astype(jnp.bfloat16)
    branch_rows = lax.all_gather(grad_branch, "tensor", axis=0, tiled=True)
    grad_down = jnp.einsum("tf,td->fd", active_low, branch_rows, preferred_element_type=jnp.float32)
    grad_inner = (
        jnp.einsum("td,fd->tf", branch_rows, w_down, preferred_element_type=jnp.float32) * slope
    ).astype(jnp.bfloat16)
    grad_up = jnp.einsum("td,tf->df", hidden_rows, grad_inner, preferred_element_type=jnp.float32)
    grad_hidden = grad_two + lax.psum_scatter(
        jnp.einsum("tf,df->td", grad_inner, w_up, preferred_element_type=jnp.float32),
        "tensor",
        scatter_dimension=0,
        tiled=True,
    )
    grad_one = norm_backward(grad_hidden, gain_one, normed_one, scaled_one)
    grad_attended = grad_one.astype(jnp.bfloat16)
    attended_rows = lax.all_gather(grad_attended, "tensor", axis=0, tiled=True)
    grad_out = jnp.einsum("te,td->ed", context, attended_rows, preferred_element_type=jnp.float32)
    grad_context = jnp.einsum(
        "td,ed->te", attended_rows, w_out, preferred_element_type=jnp.float32
    ).astype(jnp.bfloat16)
    grad_q, grad_k, grad_v = lax.map(
        attend_back, (queries, key_rows, values, logsum, grad_context.reshape(head_shape))
    )
    grad_stack = jnp.stack(
        [
            grad_q.reshape(group_rows, local_width),
            grad_k.reshape(group_rows, local_width),
            grad_v.reshape(group_rows, local_width),
        ]
    )
    weight_qkv = jnp.einsum(
        "td,kte->kde", full_rows, grad_stack, preferred_element_type=jnp.float32
    )
    grad_input = grad_one + lax.psum_scatter(
        jnp.einsum("kte,kde->td", grad_stack, w_qkv, preferred_element_type=jnp.float32).astype(
            jnp.bfloat16
        ),
        "tensor",
        scatter_dimension=0,
        tiled=True,
    ).astype(jnp.float32)

    def placed(piece, length):
        return lax.dynamic_update_slice_in_dim(
            jnp.zeros((length,), jnp.float32), piece, rank * piece.shape[0], 0
        )

    vectors = lax.psum(
        (
            placed(jnp.sum(grad_stack[0].astype(jnp.float32), axis=0), D),
            placed(jnp.sum(grad_stack[2].astype(jnp.float32), axis=0), D),
            jnp.sum(grad_attended.astype(jnp.float32), axis=0),
            jnp.sum(grad_hidden * normed_one, axis=0),
            jnp.sum(grad_hidden, axis=0),
            placed(jnp.sum(grad_inner.astype(jnp.float32), axis=0), FF),
            jnp.sum(grad_branch.astype(jnp.float32), axis=0),
            jnp.sum(upstream * normed_two, axis=0),
            jnp.sum(upstream, axis=0),
        ),
        ("dp", "tensor"),
    )
    weight_parts = (
        lax.psum_scatter(
            weight_qkv.astype(jnp.bfloat16), "dp", scatter_dimension=1, tiled=True
        ).astype(jnp.float32),
        lax.psum_scatter(
            grad_out.astype(jnp.bfloat16), "dp", scatter_dimension=1, tiled=True
        ).astype(jnp.float32),
        lax.psum_scatter(
            grad_up.astype(jnp.bfloat16), "dp", scatter_dimension=0, tiled=True
        ).astype(jnp.float32),
        lax.psum_scatter(
            grad_down.astype(jnp.bfloat16), "dp", scatter_dimension=1, tiled=True
        ).astype(jnp.float32),
    )
    return (
        result.astype(jnp.bfloat16),
        grad_input,
        weight_parts[0],
        vectors[0],
        vectors[1],
        weight_parts[1],
        vectors[2],
        vectors[3],
        vectors[4],
        weight_parts[2],
        vectors[5],
        weight_parts[3],
        vectors[6],
        vectors[7],
        vectors[8],
    )


AXES = ("dp", "tensor")
LOG2E = 1.4426950408889634
VMEM = 60 * 1024 * 1024
NT = (((1,), (1,)), ((), ()))


def dot(left, right):
    return jnp.dot(left, right, preferred_element_type=jnp.float32)


def dot_nt(left, right):
    return lax.dot_general(left, right, NT, preferred_element_type=jnp.float32)


def head_masks(width):
    lane = lax.broadcasted_iota(jnp.int32, (1, width), 1)
    return lane < HEAD_DIM


MESH = pl.DeviceIdType.MESH
CHUNKS = 8
SPAN = 256


def bit_of(index, bit):
    return lax.rem(lax.div(index, bit), 2)


def flip(index, bit):
    return index + bit - 2 * bit * bit_of(index, bit)


def mine():
    return lax.axis_index("dp"), lax.axis_index("tensor")


def greet():
    dp, t = mine()
    barrier = pltpu.get_barrier_semaphore()
    peers = [(flip(dp, 1), t), (dp, flip(t, 1)), (flip(dp, 2), t), (flip(dp, 4), t), (flip(dp, 8), t)]
    peers.append((flip(flip(dp, 4), 8), t))
    for peer in peers:
        pl.semaphore_signal(barrier, inc=1, device_id=peer, device_id_type=MESH)
    pl.semaphore_wait(barrier, len(peers))


def turn(left_ref, turned):
    dp, _ = mine()
    height = turned.shape[0] // 16
    whole = left_ref[...].T
    for piece in range(16):
        spot = 0
        for bit, weight in ((1, 8), (2, 4), (4, 2), (8, 1)):
            own = bit_of(dp, bit)
            spot = spot + weight * (own if piece & bit else 1 - own)
        turned[pl.ds(pl.multiple_of(spot * height, height), height), :] = whole[
            piece * height : (piece + 1) * height
        ]


class Scatter:
    def __init__(self, keep, lands, sems, shift=0):
        self.keep = keep
        self.lands = lands
        self.shift = shift
        self.sent, self.got = sems

    def copy(self, stage, m):
        dp, t = mine()
        odd = rem(m + self.shift, 2)
        rows = self.keep.shape[3]
        if stage == 1:
            src, peer = self.keep.at[m, 0], (dp + odd * (flip(dp, 2) - dp), t + (1 - odd) * (1 - 2 * t))
        elif stage == 2:
            src, peer = self.keep.at[m, 1, 0], (dp + (1 - odd) * (flip(dp, 2) - dp), t + odd * (1 - 2 * t))
        else:
            part = rows // 4
            start, peer = (
                (part, (flip(dp, 4), t)), (2 * part, (flip(dp, 8), t)), (0, (flip(flip(dp, 4), 8), t))
            )[stage - 3]
            src = self.keep.at[pl.ds(2 * m, 2), 1, 1, pl.ds(start, part)]
        return pltpu.make_async_remote_copy(
            src_ref=src,
            dst_ref=self.lands[stage - 1].at[m] if stage < 3 else self.lands[2].at[stage - 3, pl.ds(2 * m, 2)],
            send_sem=self.sent.at[stage, m],
            recv_sem=self.got.at[stage, m],
            device_id=peer,
            device_id_type=MESH,
        )

    def start(self, stage, m):
        self.copy(stage, m).start()

    def add(self, stage, m):
        self.copy(stage, m).wait_recv()
        land = self.lands[stage - 1]
        if stage == 1:
            @pl.loop(0, 2)
            def _(half):
                self.keep[m, 1, half] = plus(self.keep[m, 1, half], land[m, half])
        else:
            self.keep[m, 1, 1] = plus(self.keep[m, 1, 1], land[m])

    def step(self, stage, m):
        self.add(stage, m)
        self.start(stage + 1, m)

    def along_z(self, m):
        for stage in (3, 4, 5):
            self.copy(stage, m).start()

    def last(self, m, place):
        rows = self.keep.shape[3]
        for stage in (3, 4, 5):
            self.copy(stage, m).wait_recv()
        rest = pl.ds(3 * rows // 4, rows // 4)
        for chunk in (2 * m, 2 * m + 1):
            total = self.keep[chunk, 1, 1, rest].astype(jnp.float32)
            for other in range(3):
                total = total + self.lands[2][other, chunk].astype(jnp.float32)
            place(chunk, total)

    def actions(self, name, place):
        return {
            f"{name}1": functools.partial(self.step, 1),
            f"{name}2": functools.partial(self.add, 2),
            f"{name}z": self.along_z,
            f"{name}4": lambda m: self.last(m, place),
        }

    def drain(self, stage, m):
        self.copy(stage, m).wait_send()


class Pair:
    def __init__(self, keep, send, land, sems):
        self.keep, self.send, self.land = keep, send, land
        self.sent, self.got = sems
        self.slots = send.shape[0]

    def copy(self, m):
        dp, t = mine()
        return pltpu.make_async_remote_copy(
            src_ref=self.send.at[rem(m, self.slots)],
            dst_ref=self.land.at[m],
            send_sem=self.sent.at[0, m],
            recv_sem=self.got.at[0, m],
            device_id=(flip(dp, 1), t),
            device_id_type=MESH,
        )

    def store(self, m, product, own, odd, slot):
        half = product.shape[0] // 2
        rows = half // 2
        for x in range(2):
            first = odd * x + (1 - odd) * own
            second = odd * own + (1 - odd) * x
            self.send[slot, first, second] = product[x * rows : (x + 1) * rows].astype(jnp.bfloat16)
            self.keep[m, first, second] = product[half + x * rows : half + (x + 1) * rows].astype(
                jnp.bfloat16
            )

    def free(self, m):
        @pl.when(m >= self.slots)
        def _():
            self.copy(m - self.slots).wait_send()

    def add(self, m):
        self.copy(m).wait_recv()

        @pl.loop(0, 4)
        def _(quarter):
            a, b = lax.div(quarter, 2), lax.rem(quarter, 2)
            self.keep[m, a, b] = plus(self.keep[m, a, b], self.land[m, a, b])


def plus(left, right):
    return left + right


def low_buffer(*shape):
    return pltpu.VMEM(shape, jnp.bfloat16)


def land_scratch(chunks, rows, width):
    return [
        low_buffer(chunks, 2, rows, width),
        low_buffer(chunks, rows, width),
        low_buffer(3, chunks, rows // 4, width),
    ]


def rem(m, n):
    return m % n if isinstance(m, int) else lax.rem(m, n)


def run_events(table, actions, ticks, index=None):
    for spot, tick in enumerate(ticks):
        if tick not in table:
            continue

        def go(events=table[tick]):
            for name, m in events:
                actions[name](m)

        if index is None:
            go()
        else:
            pl.when(index == spot)(go)


EARLY_UP, MIDDLE_UP = 0, 0
FFN_TICKS, FFN_END = 16, 25
FFN_SITES = (
    (0, 2, 4, 6, 8, 10, 12, 14),
    (1, 3, 5, 7, 9, 11, 13, 15),
)
FFN_EVENTS = {
    2: (('d0', 0), ('d0', 1), ('u0', 0)),
    4: (('d0', 2), ('d0', 3), ('u0', 1)),
    5: (('d1', 0), ('d1', 1)),
    6: (('d0', 4), ('d0', 5), ('u0', 2)),
    7: (('d1', 2), ('d1', 3), ('d2', 1), ('d2', 0), ('dz', 0), ('d0', 6)),
    8: (('d0', 7),),
    9: (('u0', 3), ('d1', 4), ('d1', 5)),
    11: (('d2', 3), ('d2', 2), ('dz', 1), ('d4', 0), ('u0', 4)),
    13: (('d1', 6), ('d1', 7), ('u0', 5), ('d2', 5), ('d2', 4), ('dz', 2)),
    15: (('d4', 1), ('u0', 6)),
    16: (('d2', 6), ('d2', 7), ('dz', 3)),
    21: (('u0', 7), ('d4', 2)),
    24: (('d4', 3),),
}
ATT_TICKS, ATT_END = 12, 23
ATT_EVENTS = {
    1: (('u1', 0), ('u1', 1)),
    3: (('u1', 2), ('u1', 3), ('a0', 0), ('a0', 1)),
    4: (('u1', 4), ('u1', 5)),
    5: (('u1', 6), ('u1', 7), ('u2', 0), ('u2', 1), ('uz', 0)),
    6: (('u2', 2), ('u2', 3), ('uz', 1), ('a0', 2), ('a0', 3)),
    7: (('a1', 0), ('a1', 1), ('u4', 0), ('u2', 4), ('u2', 5), ('uz', 2)),
    8: (('u2', 6), ('u2', 7), ('uz', 3), ('u4', 1)),
    9: (('a0', 4), ('a1', 2), ('a1', 3), ('a0', 5), ('u4', 2)),
    10: (('a2', 0), ('a2', 1), ('az', 0), ('u4', 3)),
    11: (('a2', 2), ('a1', 4)),
    12: (('a2', 3), ('az', 1), ('a1', 5)),
    13: (('a0', 6), ('a0', 7), ('a4', 0)),
    14: (('a2', 4),),
    15: (('a2', 5), ('az', 2)),
    16: (('a4', 1),),
    17: (('a1', 7),),
    18: (('a1', 6),),
    19: (('a4', 2),),
    20: (('a2', 7),),
    21: (('a2', 6), ('az', 3)),
    22: (('a4', 3),),
}


def ffn_back_kernel(
    dm_hbm, hr_hbm, dz_hbm, n1_hbm, scale_ref, g1_ref, sums_ref,
    g_own, g_oth, s_own, s_oth, wd_own, wd_oth, wu_own, wu_oth,
    down_ref, up_ref, vec_ref, up_hbm, dz_out, da_out,
    dm, hr, n1, dm_turned, hr_turned, total,
    keep_d, send_d, land_d, d1, d2, d3, keep_u, send_u, land_u, u1, u2, u3,
    sent_d, got_d, sent_u, got_u, local_u, load_sems, out_sems,
):
    j = pl.program_id(0)
    steps = pl.num_programs(0)
    _, t = mine()
    width = keep_d.shape[4]
    early = EARLY_UP
    pair_d = Pair(keep_d, send_d, land_d, (sent_d, got_d))
    pair_u = Pair(keep_u, send_u, land_u, (sent_u, got_u))
    scatter_d = Scatter(keep_d, (d1, d2, d3), (sent_d, got_d))
    scatter_u = Scatter(keep_u, (u1, u2, u3), (sent_u, got_u))
    loads = [
        pltpu.make_async_copy(source, target, load_sems.at[i])
        for i, (source, target) in enumerate(((dm_hbm, dm), (hr_hbm, hr), (dz_hbm, total), (n1_hbm, n1)))
    ]

    @pl.when(j == 0)
    def _():
        for copy in loads:
            copy.start()
        greet()
        vec_ref[...] = jnp.zeros_like(vec_ref)
        vec_ref[0:3, :] = sums_ref[0:3, :]
        up_ref[...] = jnp.zeros_like(up_ref)
        loads[0].wait()
        turn(dm, dm_turned)
        loads[1].wait()
        turn(hr, hr_turned)

    def out_copy(m):
        return pltpu.make_async_copy(keep_u.at[m], up_hbm.at[m - early], local_u.at[m])

    def columns(m):
        return pl.ds(m * width if isinstance(m, int) else pl.multiple_of(m * width, width), width)

    def place_d(m, value):
        down_ref[:, columns(m)] = value

    def place_u(m, value):
        up_ref[:, columns(m)] = value

    def pair_down(m):
        pair_d.add(m)
        scatter_d.copy(1, m).start()

    def pair_up(m):
        pair_u.add(m)
        if m < early + MIDDLE_UP:
            scatter_u.start(1, m)
        else:
            out_copy(m).start()

    def half_up(m):
        scatter_u.add(1, m)
        out_copy(m).start()

    actions = {"d0": pair_down, "u0": pair_up, "uh": half_up}
    actions |= scatter_d.actions("d", place_d) | scatter_u.actions("u", place_u)

    def tick(site):
        run_events(FFN_EVENTS, actions, FFN_SITES[site], j)

    fast = j < steps // 2

    @pl.when(fast)
    def _():
        for part in range(2):
            m = 2 * j + part
            pair_d.free(m)
            for own, g_ref in ((0, g_oth), (1, g_own)):
                product = dot(dm_turned[...], g_ref[:, part * width : (part + 1) * width])
                pair_d.store(m, product, own, part, part)
            pair_d.copy(m).start()

    low = []
    for own, slope, weight in ((0, s_oth, wd_oth), (1, s_own, wd_own)):
        raised = dot_nt(dm[...], weight[...]) * slope[...].astype(jnp.float32)
        low.append(raised.astype(jnp.bfloat16))
        spot = t * own + (1 - t) * (1 - own)
        row = 6 + 2 * spot + lax.div(j, 4)
        vec_ref[pl.ds(row, 1), columns(lax.rem(j, 4))] = jnp.sum(
            low[-1].astype(jnp.float32), axis=0, keepdims=True
        )
    tick(0)
    pair_u.free(j)
    for own in range(2):
        pair_u.store(j, dot(hr_turned[...], low[own]), own, lax.rem(j, 2), lax.rem(j, 2))
    pair_u.copy(j).start()

    @pl.when(j == 0)
    def _():
        loads[2].wait()

    total[...] += dot_nt(low[0], wu_oth[...]) + dot_nt(low[1], wu_own[...])
    tick(1)

    @pl.when(j == steps - 1)
    def _():
        loads[3].wait()
        tile = 128

        @pl.loop(0, total.shape[0] // tile)
        def _(r):
            here = pl.ds(pl.multiple_of(r * tile, tile), tile)
            upstream = total[here, :]
            normed = n1[here, :]
            grad = norm_backward(upstream, g1_ref[...], normed, scale_ref[here, 0:1])
            grad_low = grad.astype(jnp.bfloat16)
            total[here, :] = grad
            hr[here, :] = grad_low
            vec_ref[3:4, :] += jnp.sum(upstream, axis=0, keepdims=True)
            vec_ref[4:5, :] += jnp.sum(upstream * normed, axis=0, keepdims=True)
            vec_ref[5:6, :] += jnp.sum(grad_low.astype(jnp.float32), axis=0, keepdims=True)
            run_events(FFN_EVENTS, actions, range(FFN_TICKS, FFN_TICKS + 8), r)

        outs = [
            pltpu.make_async_copy(source, target, out_sems.at[i])
            for i, (source, target) in enumerate(((total, dz_out), (hr, da_out)))
        ]
        for copy in outs:
            copy.start()

        run_events(FFN_EVENTS, actions, range(FFN_TICKS + 8, FFN_END))

        for m in range(CHUNKS - 2, CHUNKS):
            pair_d.copy(m).wait_send()
            pair_u.copy(m).wait_send()

        for m in range(CHUNKS):
            for stage in (1, 2):
                scatter_d.drain(stage, m)
                if m < early or (stage == 1 and m < early + MIDDLE_UP):
                    scatter_u.drain(stage, m)
        for m in range(CHUNKS // 2):
            for stage in (3, 4, 5):
                scatter_d.drain(stage, m)
                if m < early // 2:
                    scatter_u.drain(stage, m)

        @pl.loop(early, CHUNKS)
        def _(m):
            out_copy(m).wait()

        for copy in outs:
            copy.wait()


def ffn_backward(
    grad_branch, hidden_rows, grad_two, normed_one, scaled_one, gain_one, sums,
    act, act2, slope, slope2, w_down, w_down2, w_up, w_up2,
):
    rows, depth = grad_branch.shape
    inner = act.shape[1]
    tile = inner // CHUNKS
    last = CHUNKS // 2 - 1
    fixed = lambda *shape: pl.BlockSpec(shape, lambda j: (0,) * len(shape))
    anywhere = pl.BlockSpec(memory_space=pl.ANY)
    double = pl.BlockSpec((rows, 2 * tile), lambda j: (0, jnp.minimum(j, last)))
    column = pl.BlockSpec((rows, tile), lambda j: (0, j))
    row = pl.BlockSpec((tile, depth), lambda j: (j, 0))
    weight_column = pl.BlockSpec((depth, tile), lambda j: (0, j))
    sems = pltpu.SemaphoreType.DMA((6, CHUNKS))
    low, f32 = jnp.bfloat16, jnp.float32
    early = EARLY_UP
    return pl.pallas_call(
        ffn_back_kernel,
        grid=(CHUNKS,),
        in_specs=[anywhere] * 4
        + [fixed(rows, 128), fixed(1, depth), fixed(8, depth)]
        + [double, double, column, column, row, row, weight_column, weight_column],
        out_specs=[
            fixed(depth // 16, inner), fixed(depth // 16, max(early, 1) * tile), fixed(16, depth),
            anywhere, anywhere, anywhere,
        ],
        out_shape=[
            jax.ShapeDtypeStruct((depth // 16, inner), f32),
            jax.ShapeDtypeStruct((depth // 16, max(early, 1) * tile), f32),
            jax.ShapeDtypeStruct((16, depth), f32),
            jax.ShapeDtypeStruct((CHUNKS - early, 2, 2, SPAN, tile), low),
            jax.ShapeDtypeStruct((rows, depth), f32),
            jax.ShapeDtypeStruct((rows, depth), low),
        ],
        scratch_shapes=[
            low_buffer(rows, depth),
            low_buffer(rows, depth),
            pltpu.VMEM((rows, depth), f32),
            low_buffer(depth, rows),
            low_buffer(depth, rows),
            pltpu.VMEM((rows, depth), f32),
            low_buffer(CHUNKS, 2, 2, SPAN, tile),
            low_buffer(2, 2, 2, SPAN, tile),
            low_buffer(CHUNKS, 2, 2, SPAN, tile),
            *land_scratch(CHUNKS, SPAN, tile),
            low_buffer(CHUNKS, 2, 2, SPAN, tile),
            low_buffer(2, 2, 2, SPAN, tile),
            low_buffer(CHUNKS, 2, 2, SPAN, tile),
            low_buffer(max(early + MIDDLE_UP, 1), 2, SPAN, tile),
            *land_scratch(max(early, 2), SPAN, tile)[1:],
            sems, sems, sems, sems,
            pltpu.SemaphoreType.DMA((CHUNKS,)),
            pltpu.SemaphoreType.DMA((4,)),
            pltpu.SemaphoreType.DMA((2,)),
        ],
        compiler_params=pltpu.CompilerParams(
            vmem_limit_bytes=VMEM, collective_id=1, has_side_effects=True
        ),
        cost_estimate=pl.CostEstimate(
            flops=rows * depth * inner * 16, bytes_accessed=60 * 1024 * 1024, transcendentals=0
        ),
        name="ffn_backward",
    )(
        grad_branch, hidden_rows, grad_two, normed_one, scaled_one, gain_one.reshape(1, -1), sums,
        act, act2, slope, slope2, w_down, w_down2, w_up, w_up2,
    )


def attend_back_one(queries, key_rows, values, grad_ctx, levels):
    scale = HEAD_DIM**-0.5
    first = head_masks(128)
    keys_t = key_rows.T
    parts = []
    grad_k = grad_v = None
    for head in range(2):
        mask = first if head == 0 else jnp.logical_not(first)
        picked = jnp.where(mask, queries, jnp.zeros_like(queries))
        grad_picked = jnp.where(mask, grad_ctx, jnp.zeros_like(grad_ctx))
        weights = jnp.exp2(dot_nt(key_rows, picked) * (LOG2E * scale) - levels[head])
        grad_weights = dot_nt(values, grad_picked)
        rowsum = jnp.sum(weights * grad_weights, axis=0, keepdims=True)
        grad_low = (weights * (grad_weights - rowsum)).astype(jnp.bfloat16)
        piece_v = dot(weights.astype(jnp.bfloat16), grad_picked)
        piece_k = dot(grad_low, picked)
        grad_v = piece_v if grad_v is None else grad_v + piece_v
        grad_k = piece_k if grad_k is None else grad_k + piece_k
        parts.append(dot(keys_t[head * HEAD_DIM : (head + 1) * HEAD_DIM], grad_low))
    grad_q = jnp.concatenate(parts, axis=0).T
    return (
        (grad_q * scale).astype(jnp.bfloat16),
        (grad_k * scale).astype(jnp.bfloat16),
        grad_v.astype(jnp.bfloat16),
    )


class Total:
    def __init__(self, sums, lands, sems):
        self.sums, self.lands = sums, lands
        self.sent, self.got = sems

    def copy(self, stage):
        dp, t = mine()
        peer = ((flip(dp, 1), t), (dp, 1 - t), (flip(dp, 2), t), (flip(dp, 4), t), (flip(dp, 8), t))[stage]
        return pltpu.make_async_remote_copy(
            src_ref=self.sums.at[stage],
            dst_ref=self.lands.at[stage],
            send_sem=self.sent.at[stage],
            recv_sem=self.got.at[stage],
            device_id=peer,
            device_id_type=MESH,
        )

    def step(self, stage):
        self.copy(stage).wait_recv()
        self.sums[stage + 1] = self.sums[stage] + self.lands[stage]
        if stage < 4:
            self.copy(stage + 1).start()

    def drain(self):
        for stage in range(5):
            self.copy(stage).wait_send()


def attend_back_kernel(
    da_hbm, x_hbm, up_hbm, dz_hbm, wq_own_hbm, wq_oth_hbm, vec_ref, level_ref,
    qkv_own, c_own, wo_own, qkv_oth, c_oth, wo_oth,
    gin_hbm, gup_ref, gout_ref, gqkv_ref, vec_out, bias_out,
    da, xs, da_turned, x_turned, total, stack, wq,
    keep_u, u1, u2, u3,
    keep_a, send_a, land_a, a1, a2, a3,
    vec_sums, vec_lands, bias_sums, bias_lands,
    sent_u, got_u, sent_a, got_a, sent_v, got_v, sent_b, got_b, local_u, load_sems, out_sems,
):
    g = pl.program_id(0)
    steps = pl.num_programs(0)
    seqs = xs.shape[0] // SEQ
    late = keep_u.shape[0]
    n_chunks = keep_a.shape[0]
    pair = Pair(keep_a, send_a, land_a, (sent_a, got_a))
    scatter_a = Scatter(keep_a, (a1, a2, a3), (sent_a, got_a))
    scatter_u = Scatter(keep_u, (u1, u2, u3), (sent_u, got_u), EARLY_UP)
    vec_total = Total(vec_sums, vec_lands, (sent_v, got_v))
    bias_total = Total(bias_sums, bias_lands, (sent_b, got_b))
    _, t = mine()

    def load_up(m):
        return pltpu.make_async_copy(up_hbm.at[m], keep_u.at[m], local_u.at[m])

    pairs = ((x_hbm, xs), (da_hbm, da), (dz_hbm, total), (wq_oth_hbm, wq.at[0]), (wq_own_hbm, wq.at[1]))
    loads = [pltpu.make_async_copy(*ends, load_sems.at[i]) for i, ends in enumerate(pairs)]

    @pl.when(g == 0)
    def _():
        for m in range(late):
            load_up(m).start()
        for copy in loads:
            copy.start()
        greet()
        for m in range(late):
            load_up(m).wait()
            scatter_u.start(2 if m < MIDDLE_UP else 1, m)
        vec_sums[0] = vec_ref[...]
        vec_total.copy(0).start()
        bias_sums[0] = jnp.zeros_like(bias_sums[0])
        loads[1].wait()
        turn(da, da_turned)
        loads[0].wait()
        turn(xs, x_turned)

    def place_u(m, value):
        width = value.shape[1]
        gup_ref[:, m * width : (m + 1) * width] = value

    def place_a(m, value):
        cols = slice(m // 2 * 128, m // 2 * 128 + 128)
        left, right = value[:, :128], value[:, 128:]
        if m % 2 == 0:
            gout_ref[:, cols] = left
            gqkv_ref[1, :, cols] = right
        else:
            gqkv_ref[0, :, cols] = left
            gqkv_ref[2, :, cols] = right

    def pair_a(m):
        pair.add(m)
        scatter_a.copy(1, m).start()

    actions = {"a0": pair_a} | scatter_u.actions("u", place_u) | scatter_a.actions("a", place_a)

    def tick(site):
        run_events(ATT_EVENTS, actions, range(site, ATT_TICKS, 3), g)

    cols = pl.ds(pl.multiple_of(g * 128, 128), 128)

    def gradient(turned, other, own):
        product = dot(turned[...], jnp.concatenate([other, own], axis=1))
        return product[:, :128], product[:, 128:]

    def emit(part, first, second):
        m = 2 * g + part
        pair.free(m)
        for own in range(2):
            pair.store(m, jnp.concatenate([first[own], second[own]], axis=1), own, part, part)
        pair.copy(m).start()

    for own, qkv_ref, wo_ref in ((0, qkv_oth, wo_oth), (1, qkv_own, wo_own)):
        grad_ctx = dot_nt(da[...], wo_ref[...]).astype(jnp.bfloat16)
        for s in range(seqs):
            rows = slice(s * SEQ, (s + 1) * SEQ)
            levels = [level_ref[own, s, pl.ds(2 * g + head, 1), :] for head in range(2)]
            grads = attend_back_one(
                qkv_ref[0, rows, :], qkv_ref[1, rows, :], qkv_ref[2, rows, :], grad_ctx[rows], levels
            )
            for kind in range(3):
                stack[own * 3 + kind, rows, cols] = grads[kind]
            if s == seqs - 1:
                spot = t * own + (1 - t) * (1 - own)
                where = pl.ds(pl.multiple_of(spot * 512 + g * 128, 128), 128)
                for row, kind in ((0, 0), (1, 2)):
                    bias_sums[0, row : row + 1, where] = jnp.sum(
                        stack[own * 3 + kind, :, cols].astype(jnp.float32), axis=0, keepdims=True
                    )
        tick(own)

    @pl.when(g == steps - 1)
    def _():
        bias_total.copy(0).start()

    grads = [gradient(x_turned, stack[kind, :, cols], stack[kind + 3, :, cols]) for kind in range(3)]
    emit(1, grads[0], grads[2])
    emit(0, gradient(da_turned, c_oth[...], c_own[...]), grads[1])
    tick(2)
    for stage in range(3):
        @pl.when(g == stage)
        def _():
            vec_total.step(stage)

    @pl.when(g == steps - 1)
    def _():
        for copy in loads[2:]:
            copy.wait()
        vec_total.step(3)
        tile = xs.shape[0] // 4
        outs = []
        for r in range(4):
            here = slice(r * tile, (r + 1) * tile)
            block = total[here, :]
            for own in range(2):
                for kind in range(3):
                    block = block + dot_nt(stack[own * 3 + kind, here, :], wq[own, kind])
            total[here, :] = block
            outs.append(pltpu.make_async_copy(total.at[here], gin_hbm.at[here], out_sems.at[r]))
            outs[-1].start()
            run_events(ATT_EVENTS, actions, [ATT_TICKS + r])
            bias_total.step(r)
            if r == 0:
                vec_total.step(4)
        bias_total.step(4)

        run_events(ATT_EVENTS, actions, range(ATT_TICKS + 4, ATT_END))

        vec_out[...] = vec_sums[5]
        bias_out[...] = bias_sums[5]
        for m in range(pair.slots):
            pair.copy(n_chunks - 1 - m).wait_send()

        for m in range(late):
            scatter_u.drain(2, m)
            if m >= MIDDLE_UP:
                scatter_u.drain(1, m)
        for m in range(n_chunks):
            scatter_a.drain(1, m)
            scatter_a.drain(2, m)
        for stage in (3, 4, 5):
            for m in range(late // 2):
                scatter_u.drain(stage, m)
            for m in range(n_chunks // 2):
                scatter_a.drain(stage, m)
        vec_total.drain()
        bias_total.drain()
        for copy in outs:
            copy.wait()


def attend_backward(grad_attended, tokens, keep_up, grad_one, vectors, levels, w_qkv, w_qkv2, own, other):
    rows, depth = tokens.shape
    width = own[1].shape[1]
    steps = width // 128
    late, tile = keep_up.shape[0], keep_up.shape[4]
    n_chunks = 2 * steps
    fixed = lambda *shape: pl.BlockSpec(shape, lambda g: (0,) * len(shape))
    anywhere = pl.BlockSpec(memory_space=pl.ANY)
    side = [
        pl.BlockSpec((3, rows, 128), lambda g: (0, 0, g)),
        pl.BlockSpec((rows, 128), lambda g: (0, g)),
        pl.BlockSpec((128, depth), lambda g: (g, 0)),
    ]
    sems_u = pltpu.SemaphoreType.DMA((6, late))
    sems_a = pltpu.SemaphoreType.DMA((6, n_chunks))
    few = pltpu.SemaphoreType.DMA((5,))
    f32 = jnp.float32
    return pl.pallas_call(
        attend_back_kernel,
        grid=(steps,),
        in_specs=[anywhere] * 6 + [fixed(*vectors.shape), fixed(*levels.shape)] + side + side,
        out_specs=[
            anywhere, fixed(depth // 16, late * tile), fixed(depth // 16, width),
            fixed(3, depth // 16, width), fixed(*vectors.shape), fixed(8, depth),
        ],
        out_shape=[
            jax.ShapeDtypeStruct((rows, depth), f32),
            jax.ShapeDtypeStruct((depth // 16, late * tile), f32),
            jax.ShapeDtypeStruct((depth // 16, width), f32),
            jax.ShapeDtypeStruct((3, depth // 16, width), f32),
            jax.ShapeDtypeStruct(vectors.shape, f32),
            jax.ShapeDtypeStruct((8, depth), f32),
        ],
        scratch_shapes=[
            low_buffer(rows, depth),
            low_buffer(rows, depth),
            low_buffer(depth, rows),
            low_buffer(depth, rows),
            pltpu.VMEM((rows, depth), f32),
            low_buffer(6, rows, width),
            low_buffer(2, 3, depth, width),
            low_buffer(late, 2, 2, SPAN, tile),
            *land_scratch(late, SPAN, tile),
            low_buffer(n_chunks, 2, 2, SPAN, 256),
            low_buffer(2, 2, 2, SPAN, 256),
            low_buffer(n_chunks, 2, 2, SPAN, 256),
            *land_scratch(n_chunks, SPAN, 256),
            pltpu.VMEM((6, *vectors.shape), f32),
            pltpu.VMEM((5, *vectors.shape), f32),
            pltpu.VMEM((6, 8, depth), f32),
            pltpu.VMEM((5, 8, depth), f32),
            sems_u, sems_u, sems_a, sems_a, few, few, few, few,
            pltpu.SemaphoreType.DMA((late,)),
            pltpu.SemaphoreType.DMA((5,)),
            pltpu.SemaphoreType.DMA((4,)),
        ],
        compiler_params=pltpu.CompilerParams(
            vmem_limit_bytes=VMEM, collective_id=2, has_side_effects=True
        ),
        cost_estimate=pl.CostEstimate(
            flops=rows * depth * width * 40, bytes_accessed=60 * 1024 * 1024, transcendentals=0
        ),
        name="attend_backward",
    )(
        grad_attended, tokens, keep_up, grad_one, w_qkv, w_qkv2, vectors, levels, *own, *other,
    )


def deliver_kernel(
    gin, res, up_a, up_b, down, out, qkv, vec, bias,
    o_gin, o_res, o_up, o_down, o_out, o_qkv, *vectors,
):
    o_gin[...] = gin[...]
    o_res[...] = res[...]

    @pl.when(pl.program_id(0) == 0)
    def _():
        cols = o_up.shape[1] - up_b.shape[1]
        if cols:
            o_up[:, :cols] = up_a[:, :cols]
        o_up[:, cols:] = up_b[...]
        o_down[...] = down[...]
        o_out[...] = out[...]
        o_qkv[...] = qkv[...]
        for row in range(6):
            vectors[row][...] = vec[row : row + 1, :]
        wide = vec.shape[1]
        for row in range(4):
            vectors[6][:, row * wide : (row + 1) * wide] = vec[6 + row : 7 + row, :]
        vectors[7][...] = bias[0:1, :]
        vectors[8][...] = bias[1:2, :]


def deliver(gin, res, up_a, up_b, down, out, qkv, vec, bias):
    steps = 4
    wide = vec.shape[1]
    like = lambda array: jax.ShapeDtypeStruct(array.shape, array.dtype)
    flat = lambda size: jax.ShapeDtypeStruct((1, size), jnp.float32)
    fixed = lambda array: pl.BlockSpec(array.shape, lambda i: (0,) * len(array.shape))
    tall = pl.BlockSpec((gin.shape[0] // steps, gin.shape[1]), lambda i: (i, 0))
    up = like(down)
    flats = [flat(wide)] * 6 + [flat(4 * wide)] + [flat(wide)] * 2
    small = [up, like(down), like(out), like(qkv)] + flats
    return pl.pallas_call(
        deliver_kernel,
        grid=(steps,),
        in_specs=[tall, tall] + [fixed(array) for array in (up_a, up_b, down, out, qkv, vec, bias)],
        out_specs=[tall, tall] + [fixed(array) for array in small],
        out_shape=[like(gin), like(res)] + small,
        compiler_params=pltpu.CompilerParams(vmem_limit_bytes=VMEM),
        name="deliver",
    )(gin, res, up_a, up_b, down, out, qkv, vec, bias)


def attend_one(queries, key_rows, values):
    first = head_masks(128)
    values_t = values.T
    parts, levels = [], []
    for head in range(2):
        mask = first if head == 0 else jnp.logical_not(first)
        picked = jnp.where(mask, queries, jnp.zeros_like(queries))
        scores = dot_nt(key_rows, picked) * (LOG2E * HEAD_DIM**-0.5)
        peak = jnp.max(scores, axis=0, keepdims=True)
        lifted = jnp.exp2(scores - peak)
        totals = jnp.sum(lifted, axis=0, keepdims=True)
        context = dot(values_t[head * HEAD_DIM : (head + 1) * HEAD_DIM], lifted.astype(jnp.bfloat16))
        parts.append(context * (1.0 / totals))
        levels.append(peak + jnp.log2(totals))
    return jnp.concatenate(parts, axis=0).T.astype(jnp.bfloat16), levels


class Fetch:
    HOPS = 10

    def __init__(self, source, target, unit, index, sems):
        self.source, self.target, self.unit, self.index = source, target, unit, index
        self.sent, self.got = sems

    def copy(self, hop):
        dp, t = mine()
        core, x, z = bit_of(dp, 1), bit_of(dp, 2), bit_of(dp, 4)
        quarter = {0: x * 2 + z, 1: (1 - x) * 2 + z, 2: x * 2 + 1 - z, 3: (1 - x) * 2 + 1 - z}
        if hop == 0:
            which, part, peer = 0, None, (dp, 1 - t)
        elif hop == 1:
            which, part, peer = 0, None, (flip(dp, 2), t)
        elif hop == 2:
            which, part, peer = 0, None, (flip(dp, 4), t)
        elif hop == 3:
            which, part, peer = 2, 1, (flip(dp, 2), t)
        elif hop == 4:
            which, part, peer = 1, 2, (flip(dp, 4), t)
        elif hop == 9:
            which, part, peer = 3, 0, (dp, 1 - t)
        else:
            which, part, peer = hop - 5, None, (flip(dp, 1), t)
        place = self.unit(core, quarter[which], part, self.index)
        origin = self.source if hop in (0, 9) else self.target
        return pltpu.make_async_remote_copy(
            src_ref=origin.at[place],
            dst_ref=self.target.at[place],
            send_sem=self.sent.at[self.index, hop],
            recv_sem=self.got.at[self.index, hop],
            device_id=peer,
            device_id_type=MESH,
        )

    def start(self, *hops):
        for hop in hops:
            self.copy(hop).start()

    def arrive(self, *hops):
        for hop in hops:
            self.copy(hop).wait_recv()

    def advance(self, stage):
        if stage == 1:
            self.arrive(0)
            self.start(1, 2, 5)
        elif stage == 2:
            self.arrive(1, 2)
            self.start(3, 4, 6, 7)
        elif stage == 3:
            self.arrive(3, 4, 9)
            self.start(8)
        else:
            self.arrive(5, 6, 7, 8)

    def drain(self):
        for hop in range(self.HOPS):
            self.copy(hop).wait_send()


AHEAD = 3
BANDS = (0, 256, 512)
PACE = 4.0


def unit_of(total, lead=(), base=0, tail=()):
    def unit(core, quarter, part, index):
        size = total // 8
        start = base + core * (total // 2) + quarter * size
        if part is not None:
            sixteens = [size // 48] * 3
            for extra in range(size // 16 - sum(sixteens)):
                sixteens[(index + extra) % 3] += 1
            start = start + 16 * sum(sixteens[:part])
            size = 16 * sixteens[part]
        return (*lead, pl.ds(pl.multiple_of(start, 16), size), *tail)

    return unit


def forward_kernel(
    x_hbm, cot_hbm, wq_hbm, wo_hbm, wu_hbm, wd_hbm,
    bq_ref, bv_ref, bu_ref, bo_ref, g1_ref, s1_ref, bd_ref, g2_ref, s2_ref,
    qkv_out1, qkv_out0, ctx_out1, ctx_out0, act_out1, act_out0, slope_out1, slope_out0,
    hr_out, n1_out, dm_out, dz_out, res_out, wq_out, wo_out, wu_out, wd_out,
    level_ref, scale_ref, sums_ref,
    x, cot, wq1, wq0, wo1, wo0, wu1, wu0, wd1, wd0, qkv1, qkv0, ctx1, ctx0, n1, hr, total, act, slope,
    bias_own, bias_oth, sent, got, bias_sent, bias_got, load_sems, out_sems,
):
    dp, t = mine()
    rows, depth = x.shape
    seqs = rows // SEQ
    width = ctx1.shape[1]
    inner = wu1.shape[1]
    tiles = 4
    span = inner // tiles

    chunks = []

    def chunk(source, target, unit):
        chunks.append(Fetch(source, target, unit, len(chunks), (sent, got)))
        return len(chunks) - 1

    starts = BANDS
    bands = [pl.ds(a, b - a) for a, b in zip(starts, starts[1:])]
    c_qkv = [chunk(wq_hbm, wq0, unit_of(depth, lead=(slice(None),), tail=(cols,))) for cols in bands]
    sizes = [3 * cols.size / width for cols in bands] + [1.0] * (1 + 2 * tiles)
    c_out = chunk(wo_hbm, wo0, unit_of(width))
    c_up, c_down = [], []
    for j in range(tiles):
        c_up.append(chunk(wu_hbm, wu0, unit_of(depth, tail=(pl.ds(j * span, span),))))
        c_down.append(chunk(wd_hbm, wd0, unit_of(span, base=j * span)))

    loads, outs, done = {}, [], []

    def finish(copy):
        copy.wait()
        done.append(copy)

    def load(name, source, target):
        copy = pltpu.make_async_copy(source, target, load_sems.at[len(loads)])
        loads[name] = copy
        copy.start()

    def save(source, target):
        copy = pltpu.make_async_copy(source, target, out_sems.at[len(outs)])
        outs.append(copy)
        copy.start()
        return copy

    load("x", x_hbm, x)
    for kind in range(3):
        load(("q", kind), wq_hbm.at[kind], wq1.at[kind])
    greet()
    ahead = AHEAD
    for m in range(ahead):
        chunks[m].start(0, 9)
    bias_own[:, :width] = bq_ref[...]
    bias_own[:, width : 2 * width] = bv_ref[...]
    bias_own[:, 2 * width :] = bu_ref[...]
    bias_copy = pltpu.make_async_remote_copy(
        src_ref=bias_own, dst_ref=bias_oth, send_sem=bias_sent, recv_sem=bias_got,
        device_id=(dp, 1 - t), device_id_type=MESH,
    )
    bias_copy.start()
    load("o", wo_hbm, wo1)
    load("u", wu_hbm, wu1)
    load("d", wd_hbm, wd1)
    load("cot", cot_hbm, cot)

    events = []
    for m in range(len(chunks)):
        for stage, lag in ((1, 7.0), (2, 13.0), (3, 17.0), (4, 20.0)):
            events.append((lag + PACE * sum(sizes[:m + 1]) - PACE, stage, m))
    events.sort()
    saves = {}
    for i, cols in enumerate(bands):
        saves[c_qkv[i]] = (wq0.at[:, :, cols], wq_out.at[:, :, cols])
    saves[c_out] = (wo0, wo_out)
    for j in range(tiles):
        cols = pl.ds(j * span, span)
        saves[c_up[j]] = (wu0.at[:, cols], wu_out.at[:, cols])
        saves[c_down[j]] = (wd0.at[cols], wd_out.at[cols])

    def event():
        _, stage, m = events.pop(0)
        chunks[m].advance(stage)
        if stage == 1 and m + ahead < len(chunks):
            chunks[m + ahead].start(0, 9)
        if stage == 4:
            save(*saves[m])

    clock = [0.0]

    def spend(us):
        clock[0] += us
        while events and events[0][0] <= clock[0]:
            event()

    def need(m):
        while any(e[1] == 4 and e[2] == m for e in events):
            clock[0] = max(clock[0], events[0][0])
            event()

    def project(weights, kind, kept, biases, cols):
        product = dot(x[...], weights[kind, :, cols])
        if kind != 1:
            at = cols.start + (0 if kind == 0 else width)
            product = product + biases[:, at : at + cols.stop - cols.start]
        kept[kind, :, cols] = product.astype(jnp.bfloat16)

    def attend(side, kept, context, pair):
        cols = slice(pair * 128, pair * 128 + 128)

        for s in range(seqs):
            here = pl.ds(s * SEQ, SEQ)
            out, levels = attend_one(kept[0, here, cols], kept[1, here, cols], kept[2, here, cols])
            context[here, cols] = out
            for head in range(2):
                spot = 2 * pair + head
                level_ref[side, s, spot : spot + 1, :] = levels[head]

    loads["x"].wait()
    for kind in range(3):
        loads[("q", kind)].wait()
        project(wq1, kind, qkv1, bias_own, slice(0, width))
        spend(1.6)
    save(qkv1, qkv_out1)
    for pair in range(width // 128):
        attend(1, qkv1, ctx1, pair)
        spend(2.7)
    save(ctx1, ctx_out1)
    bias_copy.wait_recv()
    for i, (low, high) in enumerate(zip(starts, starts[1:])):
        need(c_qkv[i])
        for kind in range(3):
            project(wq0, kind, qkv0, bias_oth, slice(low, high))
            spend(0.8)
        for pair in range(low // 128, high // 128):
            attend(0, qkv0, ctx0, pair)
            spend(2.7)
    save(qkv0, qkv_out0)
    save(ctx0, ctx_out0)
    loads["o"].wait()
    need(c_out)
    step = 256

    @pl.loop(0, rows // step)
    def _(r):
        here = pl.ds(pl.multiple_of(r * step, step), step)
        attended = dot(ctx1[here, :], wo1[...]) + dot(ctx0[here, :], wo0[...])
        _, normed, scaled = norm_forward(
            x[here, :].astype(jnp.float32) + attended + bo_ref[...], g1_ref[...], s1_ref[...]
        )
        n1[here, :] = normed
        hr[here, :] = (normed * g1_ref[...] + s1_ref[...]).astype(jnp.bfloat16)
        scale_ref[here, :] = jnp.broadcast_to(scaled, (step, 128))

    save(n1, n1_out)
    hr_saved = save(hr, hr_out)
    spend(5.0)
    loads["u"].wait()
    loads["d"].wait()
    big = 512
    slots = []
    for side, up, down, biases, act_out, slope_out in (
        (1, wu1, wd1, bias_own, act_out1, slope_out1),
        (0, wu0, wd0, bias_oth, act_out0, slope_out0),
    ):
        for j in range(tiles):
            cols = pl.ds(j * span, span)
            slot = len(slots) % 2
            if len(slots) >= 2:
                for copy in slots[-2]:
                    finish(copy)
            if side == 0:
                need(c_up[j])
                need(c_down[j])
            bias = biases[:, 2 * width + j * span : 2 * width + (j + 1) * span]
            fresh = not slots

            for r in range(rows // big):
                here = pl.ds(r * big, big)
                activated, leaning = gelu_pair(dot(hr[here, :], up[:, cols]) + bias)
                activated = activated.astype(jnp.bfloat16)
                act[slot, here, :] = activated
                slope[slot, here, :] = leaning.astype(jnp.bfloat16)
                product = dot(activated, down[cols, :])
                total[here, :] = product if fresh else total[here, :] + product

            slots.append((
                save(act.at[slot], act_out.at[:, cols]),
                save(slope.at[slot], slope_out.at[:, cols]),
            ))
            spend(3.6)
    while events:
        event()
    finish(hr_saved)
    loads["cot"].wait()
    sums_ref[...] = jnp.zeros_like(sums_ref)

    for r in range(rows // step):
        here = pl.ds(r * step, step)
        hidden = n1[here, :] * g1_ref[...] + s1_ref[...]
        result, normed, scaled = norm_forward(hidden + total[here, :] + bd_ref[...], g2_ref[...], s2_ref[...])
        x[here, :] = result.astype(jnp.bfloat16)
        upstream = cot[here, :].astype(jnp.float32)
        grad = norm_backward(upstream, g2_ref[...], normed, scaled)
        total[here, :] = grad
        low = grad.astype(jnp.bfloat16)
        hr[here, :] = low
        sums_ref[0:1, :] += jnp.sum(upstream, axis=0, keepdims=True)
        sums_ref[1:2, :] += jnp.sum(upstream * normed, axis=0, keepdims=True)
        sums_ref[2:3, :] += jnp.sum(low.astype(jnp.float32), axis=0, keepdims=True)
        save(x.at[here], res_out.at[here])
        save(hr.at[here], dm_out.at[here])
        save(total.at[here], dz_out.at[here])

    bias_copy.wait_send()
    for fetch in chunks:
        fetch.drain()
    for copy in outs:
        if not any(copy is other for other in done):
            copy.wait()


def forward(tokens, cotangent, w_qkv, w_out, w_up, w_down, biases, bias_o, gain_one, shift_one, bias_down, gain_two, shift_two):
    rows, depth = tokens.shape
    width, inner = w_out.shape[0], w_up.shape[1]
    seqs, heads = rows // SEQ, width // HEAD_DIM
    low, f32 = jnp.bfloat16, jnp.float32
    any_space = pl.BlockSpec(memory_space=pl.ANY)
    near = pl.BlockSpec(memory_space=pltpu.VMEM)
    qkv = (3, rows, width)
    outs = [
        (qkv, low), (qkv, low), ((rows, width), low), ((rows, width), low),
        ((rows, inner), low), ((rows, inner), low), ((rows, inner), low), ((rows, inner), low),
        ((rows, depth), low), ((rows, depth), f32), ((rows, depth), low), ((rows, depth), f32), ((rows, depth), low),
        (w_qkv.shape, low), (w_out.shape, low), (w_up.shape, low), (w_down.shape, low),
        ((2, seqs, heads, SEQ), f32), ((rows, 128), f32), ((8, depth), f32),
    ]
    span = inner // 4
    flat = (1, 2 * width + inner)
    scratch = [
        ((rows, depth), low), ((rows, depth), low), (w_qkv.shape, low), (w_qkv.shape, low),
        (w_out.shape, low), (w_out.shape, low), (w_up.shape, low), (w_up.shape, low),
        (w_down.shape, low), (w_down.shape, low), (qkv, low), (qkv, low),
        ((rows, width), low), ((rows, width), low), ((rows, depth), f32), ((rows, depth), low),
        ((rows, depth), f32), ((2, rows, span), low), ((2, rows, span), low), (flat, f32), (flat, f32),
    ]
    sems = pltpu.SemaphoreType.DMA((len(BANDS) + 8, Fetch.HOPS))
    one = pltpu.SemaphoreType.DMA
    return pl.pallas_call(
        forward_kernel,
        in_specs=[any_space] * 6 + [near] * 9,
        out_specs=[any_space] * 17 + [near] * 3,
        out_shape=[jax.ShapeDtypeStruct(*out) for out in outs],
        scratch_shapes=[pltpu.VMEM(*buffer) for buffer in scratch]
        + [sems, sems, one, one, pltpu.SemaphoreType.DMA((8,)), pltpu.SemaphoreType.DMA((48,))],
        compiler_params=pltpu.CompilerParams(
            vmem_limit_bytes=60 * 1024 * 1024, collective_id=3, has_side_effects=True
        ),
        cost_estimate=pl.CostEstimate(
            flops=rows * depth * (width * 16 + inner * 8), bytes_accessed=80 * 1024 * 1024, transcendentals=0
        ),
        name="forward",
    )(
        tokens, cotangent, w_qkv, w_out, w_up, w_down,
        *(v.reshape(1, -1) for v in (*biases, bias_o, gain_one, shift_one, bias_down, gain_two, shift_two)),
    )


def body(mesh, *args):
    tokens, w_qkv = args[0], args[2]
    n_dp, n_tensor = mesh.shape["dp"], mesh.shape["tensor"]
    local = (*tokens.shape, w_qkv.shape[2], args[9].shape[1])
    if (n_dp, n_tensor) == (16, 2) and local == (1024, 1024, 512, 2048):
        return body_tokens(*args)
    return body_tensor(*args)


def body_tokens(
    tokens,
    cotangent,
    w_qkv,
    bias_q,
    bias_v,
    w_out,
    bias_o,
    gain_one,
    shift_one,
    w_up,
    bias_up,
    w_down,
    bias_down,
    gain_two,
    shift_two,
):
    (
        qkv, qkv2, ctx, ctx2, active, active2, slope, slope2,
        hidden_rows, normed_one, grad_branch, grad_two, result,
        w_qkv2, w_out2, w_up2, w_down2, levels, scaled_one, sums,
    ) = forward(
        tokens, cotangent, w_qkv, w_out, w_up, w_down, (bias_q, bias_v, bias_up),
        bias_o, gain_one, shift_one, bias_down, gain_two, shift_two,
    )
    grad_down, up_early, vectors, keep_up, grad_one, grad_attended = ffn_backward(
        grad_branch, hidden_rows, grad_two, normed_one, scaled_one, gain_one, sums,
        active, active2, slope, slope2, w_down, w_down2, w_up, w_up2,
    )
    grad_input, up_late, grad_out, grad_qkv, vectors, biases = attend_backward(
        grad_attended, tokens, keep_up, grad_one, vectors, levels, w_qkv, w_qkv2,
        (qkv, ctx, w_out), (qkv2, ctx2, w_out2),
    )
    grad_input, result, grad_up, grad_down, grad_out, grad_qkv, *vectors = deliver(
        grad_input, result, up_early, up_late, grad_down, grad_out, grad_qkv, vectors, biases
    )
    g_shift_two, g_gain_two, g_bias_down, g_shift_one, g_gain_one, g_bias_o, g_bias_up, g_bias_q, g_bias_v = (
        vector.reshape(-1) for vector in vectors
    )
    return (
        result,
        grad_input,
        grad_qkv,
        g_bias_q,
        g_bias_v,
        grad_out.T,
        g_bias_o,
        g_gain_one,
        g_shift_one,
        grad_up,
        g_bias_up,
        grad_down.T,
        g_bias_down,
        g_gain_two,
        g_shift_two,
    )


def solution(mesh):
    in_specs = (
        P(("dp", "tensor"), None),
        P(("dp", "tensor"), None),
        P(None, None, "tensor"),
        P("tensor"),
        P("tensor"),
        P("tensor", None),
        P(),
        P(),
        P(),
        P(None, "tensor"),
        P("tensor"),
        P("tensor", None),
        P(),
        P(),
        P(),
    )
    out_specs = (
        P(("dp", "tensor"), None),
        P(("dp", "tensor"), None),
        P(None, "dp", "tensor"),
        P(),
        P(),
        P("tensor", "dp"),
        P(),
        P(),
        P(),
        P("dp", "tensor"),
        P(),
        P("tensor", "dp"),
        P(),
        P(),
        P(),
    )
    return jax.shard_map(functools.partial(body, mesh), mesh=mesh, in_specs=in_specs, out_specs=out_specs, check_vma=False)
```

```python
import functools

import jax
import jax.numpy as jnp
from jax import lax
from jax.experimental import pallas as pl
from jax.experimental.pallas import tpu as pltpu
from jax.sharding import PartitionSpec as P

D = 1024
FF = 4096
HEAD_DIM = 64
SEQ = 512


def gelu_pair(inner_pre):
    normal_cdf = 0.5 * (1.0 + jax.scipy.special.erf(inner_pre * 0.7071067811865476))
    density = jnp.exp(-0.5 * inner_pre * inner_pre) * 0.3989422804014327
    return (inner_pre * normal_cdf, normal_cdf + inner_pre * density)


def norm_forward(summed, gain, shift):
    centre = summed - jnp.mean(summed, axis=-1, keepdims=True)
    scaled = lax.rsqrt(jnp.mean(centre * centre, axis=-1, keepdims=True) + 1e-05)
    normed = centre * scaled
    return (normed * gain + shift, normed, scaled)


def norm_backward(upstream, gain, normed, scaled):
    grad_norm = upstream * gain
    return scaled * (
        grad_norm
        - jnp.mean(grad_norm, axis=-1, keepdims=True)
        - normed * jnp.mean(grad_norm * normed, axis=-1, keepdims=True)
    )


def attend_block(block):
    queries, key_rows, values = block
    scores = jnp.einsum(
        "qhd,khd->hqk", queries, key_rows, preferred_element_type=jnp.float32
    ) * HEAD_DIM ** (-0.5)
    peak_score = jnp.max(scores, axis=-1, keepdims=True)
    lifted = jnp.exp(scores - peak_score)
    totals = jnp.sum(lifted, axis=-1, keepdims=True)
    weights = (lifted / totals).astype(jnp.bfloat16)
    context = jnp.einsum("hqk,khd->qhd", weights, values, preferred_element_type=jnp.float32)
    return (context.astype(jnp.bfloat16), (peak_score + jnp.log(totals))[..., 0])


def attend_back(block):
    queries, key_rows, values, logsum, grad_ctx = block
    scale = HEAD_DIM ** (-0.5)
    scores = (
        jnp.einsum("qhd,khd->hqk", queries, key_rows, preferred_element_type=jnp.float32) * scale
    )
    weights = jnp.exp(scores - logsum[..., None])
    grad_weights = jnp.einsum("qhd,khd->hqk", grad_ctx, values, preferred_element_type=jnp.float32)
    grad_scores = weights * (grad_weights - jnp.sum(weights * grad_weights, axis=-1, keepdims=True))
    grad_low = grad_scores.astype(jnp.bfloat16)
    grad_v = jnp.einsum(
        "hqk,qhd->khd", weights.astype(jnp.bfloat16), grad_ctx, preferred_element_type=jnp.float32
    )
    grad_q = (
        jnp.einsum("hqk,khd->qhd", grad_low, key_rows, preferred_element_type=jnp.float32) * scale
    )
    grad_k = (
        jnp.einsum("hqk,qhd->khd", grad_low, queries, preferred_element_type=jnp.float32) * scale
    )
    return (grad_q.astype(jnp.bfloat16), grad_k.astype(jnp.bfloat16), grad_v.astype(jnp.bfloat16))


def body_tensor(
    tokens,
    cotangent,
    w_qkv,
    bias_q,
    bias_v,
    w_out,
    bias_o,
    gain_one,
    shift_one,
    w_up,
    bias_up,
    w_down,
    bias_down,
    gain_two,
    shift_two,
):
    rank = lax.axis_index("tensor")
    full_rows = lax.all_gather(tokens, "tensor", axis=0, tiled=True)
    group_rows = full_rows.shape[0]
    local_width = w_qkv.shape[2]
    head_shape = (group_rows // SEQ, SEQ, local_width // HEAD_DIM, HEAD_DIM)
    projected = jnp.einsum("td,kde->kte", full_rows, w_qkv, preferred_element_type=jnp.float32)
    queries = (projected[0] + bias_q).astype(jnp.bfloat16).reshape(head_shape)
    key_rows = projected[1].astype(jnp.bfloat16).reshape(head_shape)
    values = (projected[2] + bias_v).astype(jnp.bfloat16).reshape(head_shape)
    context, logsum = lax.map(attend_block, (queries, key_rows, values))
    context = context.reshape(group_rows, local_width)
    attended = (
        lax.psum_scatter(
            jnp.dot(context, w_out, preferred_element_type=jnp.float32),
            "tensor",
            scatter_dimension=0,
            tiled=True,
        )
        + bias_o
    )
    hidden_one, normed_one, scaled_one = norm_forward(
        tokens.astype(jnp.float32) + attended, gain_one, shift_one
    )
    hidden_rows = lax.all_gather(hidden_one.astype(jnp.bfloat16), "tensor", axis=0, tiled=True)
    inner_pre = jnp.dot(hidden_rows, w_up, preferred_element_type=jnp.float32) + bias_up
    activated, slope = gelu_pair(inner_pre)
    active_low = activated.astype(jnp.bfloat16)
    branch = (
        lax.psum_scatter(
            jnp.dot(active_low, w_down, preferred_element_type=jnp.float32),
            "tensor",
            scatter_dimension=0,
            tiled=True,
        )
        + bias_down
    )
    result, normed_two, scaled_two = norm_forward(hidden_one + branch, gain_two, shift_two)
    upstream = cotangent.astype(jnp.float32)
    grad_two = norm_backward(upstream, gain_two, normed_two, scaled_two)
    grad_branch = grad_two.astype(jnp.bfloat16)
    branch_rows = lax.all_gather(grad_branch, "tensor", axis=0, tiled=True)
    grad_down = jnp.einsum("tf,td->fd", active_low, branch_rows, preferred_element_type=jnp.float32)
    grad_inner = (
        jnp.einsum("td,fd->tf", branch_rows, w_down, preferred_element_type=jnp.float32) * slope
    ).astype(jnp.bfloat16)
    grad_up = jnp.einsum("td,tf->df", hidden_rows, grad_inner, preferred_element_type=jnp.float32)
    grad_hidden = grad_two + lax.psum_scatter(
        jnp.einsum("tf,df->td", grad_inner, w_up, preferred_element_type=jnp.float32),
        "tensor",
        scatter_dimension=0,
        tiled=True,
    )
    grad_one = norm_backward(grad_hidden, gain_one, normed_one, scaled_one)
    grad_attended = grad_one.astype(jnp.bfloat16)
    attended_rows = lax.all_gather(grad_attended, "tensor", axis=0, tiled=True)
    grad_out = jnp.einsum("te,td->ed", context, attended_rows, preferred_element_type=jnp.float32)
    grad_context = jnp.einsum(
        "td,ed->te", attended_rows, w_out, preferred_element_type=jnp.float32
    ).astype(jnp.bfloat16)
    grad_q, grad_k, grad_v = lax.map(
        attend_back, (queries, key_rows, values, logsum, grad_context.reshape(head_shape))
    )
    grad_stack = jnp.stack(
        [
            grad_q.reshape(group_rows, local_width),
            grad_k.reshape(group_rows, local_width),
            grad_v.reshape(group_rows, local_width),
        ]
    )
    weight_qkv = jnp.einsum(
        "td,kte->kde", full_rows, grad_stack, preferred_element_type=jnp.float32
    )
    grad_input = grad_one + lax.psum_scatter(
        jnp.einsum("kte,kde->td", grad_stack, w_qkv, preferred_element_type=jnp.float32).astype(
            jnp.bfloat16
        ),
        "tensor",
        scatter_dimension=0,
        tiled=True,
    ).astype(jnp.float32)

    def placed(piece, length):
        return lax.dynamic_update_slice_in_dim(
            jnp.zeros((length,), jnp.float32), piece, rank * piece.shape[0], 0
        )

    vectors = lax.psum(
        (
            placed(jnp.sum(grad_stack[0].astype(jnp.float32), axis=0), D),
            placed(jnp.sum(grad_stack[2].astype(jnp.float32), axis=0), D),
            jnp.sum(grad_attended.astype(jnp.float32), axis=0),
            jnp.sum(grad_hidden * normed_one, axis=0),
            jnp.sum(grad_hidden, axis=0),
            placed(jnp.sum(grad_inner.astype(jnp.float32), axis=0), FF),
            jnp.sum(grad_branch.astype(jnp.float32), axis=0),
            jnp.sum(upstream * normed_two, axis=0),
            jnp.sum(upstream, axis=0),
        ),
        ("dp", "tensor"),
    )
    weight_parts = (
        lax.psum_scatter(
            weight_qkv.astype(jnp.bfloat16), "dp", scatter_dimension=1, tiled=True
        ).astype(jnp.float32),
        lax.psum_scatter(
            grad_out.astype(jnp.bfloat16), "dp", scatter_dimension=1, tiled=True
        ).astype(jnp.float32),
        lax.psum_scatter(
            grad_up.astype(jnp.bfloat16), "dp", scatter_dimension=0, tiled=True
        ).astype(jnp.float32),
        lax.psum_scatter(
            grad_down.astype(jnp.bfloat16), "dp", scatter_dimension=1, tiled=True
        ).astype(jnp.float32),
    )
    return (
        result.astype(jnp.bfloat16),
        grad_input,
        weight_parts[0],
        vectors[0],
        vectors[1],
        weight_parts[1],
        vectors[2],
        vectors[3],
        vectors[4],
        weight_parts[2],
        vectors[5],
        weight_parts[3],
        vectors[6],
        vectors[7],
        vectors[8],
    )


AXES = ("dp", "tensor")
LOG2E = 1.4426950408889634
VMEM = 60 * 1024 * 1024
NT = (((1,), (1,)), ((), ()))


def dot(left, right):
    return jnp.dot(left, right, preferred_element_type=jnp.float32)


def dot_nt(left, right):
    return lax.dot_general(left, right, NT, preferred_element_type=jnp.float32)


def head_masks(width):
    lane = lax.broadcasted_iota(jnp.int32, (1, width), 1)
    return lane < HEAD_DIM


MESH = pl.DeviceIdType.MESH
CHUNKS = 8
SPAN = 256


def bit_of(index, bit):
    return lax.rem(lax.div(index, bit), 2)


def flip(index, bit):
    return index + bit - 2 * bit * bit_of(index, bit)


def mine():
    return lax.axis_index("dp"), lax.axis_index("tensor")


def greet():
    dp, t = mine()
    barrier = pltpu.get_barrier_semaphore()
    peers = [(flip(dp, 1), t), (dp, flip(t, 1)), (flip(dp, 2), t), (flip(dp, 4), t), (flip(dp, 8), t)]
    peers.append((flip(flip(dp, 4), 8), t))
    for peer in peers:
        pl.semaphore_signal(barrier, inc=1, device_id=peer, device_id_type=MESH)
    pl.semaphore_wait(barrier, len(peers))


def turn(left_ref, turned):
    dp, _ = mine()
    height = turned.shape[0] // 16
    whole = left_ref[...].T
    for piece in range(16):
        spot = 0
        for bit, weight in ((1, 8), (2, 4), (4, 2), (8, 1)):
            own = bit_of(dp, bit)
            spot = spot + weight * (own if piece & bit else 1 - own)
        turned[pl.ds(pl.multiple_of(spot * height, height), height), :] = whole[
            piece * height : (piece + 1) * height
        ]


class Scatter:
    def __init__(self, keep, lands, sems, shift=0):
        self.keep = keep
        self.lands = lands
        self.shift = shift
        self.sent, self.got = sems

    def copy(self, stage, m):
        dp, t = mine()
        odd = rem(m + self.shift, 2)
        rows = self.keep.shape[3]
        if stage == 1:
            src, peer = self.keep.at[m, 0], (dp + odd * (flip(dp, 2) - dp), t + (1 - odd) * (1 - 2 * t))
        elif stage == 2:
            src, peer = self.keep.at[m, 1, 0], (dp + (1 - odd) * (flip(dp, 2) - dp), t + odd * (1 - 2 * t))
        else:
            part = rows // 4
            start, peer = (
                (part, (flip(dp, 4), t)), (2 * part, (flip(dp, 8), t)), (0, (flip(flip(dp, 4), 8), t))
            )[stage - 3]
            src = self.keep.at[pl.ds(2 * m, 2), 1, 1, pl.ds(start, part)]
        return pltpu.make_async_remote_copy(
            src_ref=src,
            dst_ref=self.lands[stage - 1].at[m] if stage < 3 else self.lands[2].at[stage - 3, pl.ds(2 * m, 2)],
            send_sem=self.sent.at[stage, m],
            recv_sem=self.got.at[stage, m],
            device_id=peer,
            device_id_type=MESH,
        )

    def start(self, stage, m):
        self.copy(stage, m).start()

    def add(self, stage, m):
        self.copy(stage, m).wait_recv()
        land = self.lands[stage - 1]
        if stage == 1:
            @pl.loop(0, 2)
            def _(half):
                self.keep[m, 1, half] = plus(self.keep[m, 1, half], land[m, half])
        else:
            self.keep[m, 1, 1] = plus(self.keep[m, 1, 1], land[m])

    def step(self, stage, m):
        self.add(stage, m)
        self.start(stage + 1, m)

    def along_z(self, m):
        for stage in (3, 4, 5):
            self.copy(stage, m).start()

    def last(self, m, place):
        rows = self.keep.shape[3]
        for stage in (3, 4, 5):
            self.copy(stage, m).wait_recv()
        rest = pl.ds(3 * rows // 4, rows // 4)
        for chunk in (2 * m, 2 * m + 1):
            total = self.keep[chunk, 1, 1, rest].astype(jnp.float32)
            for other in range(3):
                total = total + self.lands[2][other, chunk].astype(jnp.float32)
            place(chunk, total)

    def actions(self, name, place):
        return {
            f"{name}1": functools.partial(self.step, 1),
            f"{name}2": functools.partial(self.add, 2),
            f"{name}z": self.along_z,
            f"{name}4": lambda m: self.last(m, place),
        }

    def drain(self, stage, m):
        self.copy(stage, m).wait_send()


class Pair:
    def __init__(self, keep, send, land, sems):
        self.keep, self.send, self.land = keep, send, land
        self.sent, self.got = sems
        self.slots = send.shape[0]

    def copy(self, m):
        dp, t = mine()
        return pltpu.make_async_remote_copy(
            src_ref=self.send.at[rem(m, self.slots)],
            dst_ref=self.land.at[m],
            send_sem=self.sent.at[0, m],
            recv_sem=self.got.at[0, m],
            device_id=(flip(dp, 1), t),
            device_id_type=MESH,
        )

    def store(self, m, product, own, odd, slot):
        half = product.shape[0] // 2
        rows = half // 2
        for x in range(2):
            first = odd * x + (1 - odd) * own
            second = odd * own + (1 - odd) * x
            self.send[slot, first, second] = product[x * rows : (x + 1) * rows].astype(jnp.bfloat16)
            self.keep[m, first, second] = product[half + x * rows : half + (x + 1) * rows].astype(
                jnp.bfloat16
            )

    def free(self, m):
        @pl.when(m >= self.slots)
        def _():
            self.copy(m - self.slots).wait_send()

    def add(self, m):
        self.copy(m).wait_recv()

        @pl.loop(0, 4)
        def _(quarter):
            a, b = lax.div(quarter, 2), lax.rem(quarter, 2)
            self.keep[m, a, b] = plus(self.keep[m, a, b], self.land[m, a, b])


def plus(left, right):
    return left + right


def low_buffer(*shape):
    return pltpu.VMEM(shape, jnp.bfloat16)


def land_scratch(chunks, rows, width):
    return [
        low_buffer(chunks, 2, rows, width),
        low_buffer(chunks, rows, width),
        low_buffer(3, chunks, rows // 4, width),
    ]


def rem(m, n):
    return m % n if isinstance(m, int) else lax.rem(m, n)


def run_events(table, actions, ticks, index=None):
    for spot, tick in enumerate(ticks):
        if tick not in table:
            continue

        def go(events=table[tick]):
            for name, m in events:
                actions[name](m)

        if index is None:
            go()
        else:
            pl.when(index == spot)(go)


EARLY_UP, MIDDLE_UP = 0, 2
FFN_TICKS, FFN_END = 16, 27
FFN_SITES = (
    (0, 2, 4, 6, 8, 10, 12, 14),
    (1, 3, 5, 7, 9, 11, 13, 15),
)
FFN_EVENTS = {
    2: (('d0', 0), ('d0', 1), ('u0', 0)),
    4: (('d0', 2), ('d0', 3), ('u0', 1)),
    5: (('d1', 0), ('d1', 1)),
    6: (('d0', 4), ('d0', 5), ('uh', 0), ('u0', 2)),
    7: (('d1', 3),),
    8: (('d0', 6), ('d1', 2), ('d0', 7)),
    9: (('uh', 1), ('d2', 1), ('u0', 3), ('d2', 0), ('dz', 0)),
    11: (('d1', 4), ('u0', 4)),
    12: (('d1', 5), ('d2', 3)),
    13: (('d2', 2), ('dz', 1), ('u0', 5), ('d4', 0)),
    14: (('d1', 6),),
    15: (('d1', 7), ('d2', 5), ('u0', 6)),
    16: (('d2', 4), ('dz', 2)),
    20: (('d4', 1), ('d2', 6), ('u0', 7)),
    24: (('d2', 7), ('dz', 3)),
    25: (('d4', 2),),
    26: (('d4', 3),),
}
ATT_TICKS, ATT_END = 12, 25
ATT_EVENTS = {
    1: (('u2', 0), ('u2', 1), ('uz', 0)),
    2: (('u1', 2), ('u1', 3)),
    4: (('a0', 0), ('u1', 4), ('u1', 5), ('a0', 1), ('u4', 0)),
    5: (('u1', 6), ('u1', 7), ('u2', 2), ('u2', 3), ('uz', 1)),
    6: (('u2', 4), ('a0', 2)),
    7: (('a0', 3), ('a1', 0), ('a1', 1), ('u2', 5), ('uz', 2)),
    8: (('u4', 1), ('u2', 6), ('u2', 7), ('uz', 3)),
    9: (('a1', 2), ('a0', 4)),
    10: (('a1', 3), ('a0', 5), ('u4', 2), ('a2', 1), ('a2', 0), ('az', 0)),
    11: (('a2', 2), ('u4', 3)),
    12: (('a1', 4),),
    13: (('a2', 3), ('az', 1)),
    14: (('a0', 6), ('a1', 5), ('a0', 7), ('a4', 0)),
    16: (('a2', 4),),
    17: (('a4', 1),),
    18: (('a1', 6),),
    19: (('a1', 7),),
    20: (('a2', 5), ('az', 2)),
    21: (('a2', 6),),
    22: (('a2', 7), ('az', 3)),
    23: (('a4', 2),),
    24: (('a4', 3),),
}


def ffn_back_kernel(
    dm_hbm, hr_hbm, dz_hbm, n1_hbm, scale_ref, g1_ref, sums_ref,
    g_own, g_oth, s_own, s_oth, wd_own, wd_oth, wu_own, wu_oth,
    down_ref, up_ref, vec_ref, up_hbm, dz_out, da_out,
    dm, hr, n1, dm_turned, hr_turned, total,
    keep_d, send_d, land_d, d1, d2, d3, keep_u, send_u, land_u, u1, u2, u3,
    sent_d, got_d, sent_u, got_u, local_u, load_sems, out_sems,
):
    j = pl.program_id(0)
    steps = pl.num_programs(0)
    _, t = mine()
    width = keep_d.shape[4]
    early = EARLY_UP
    pair_d = Pair(keep_d, send_d, land_d, (sent_d, got_d))
    pair_u = Pair(keep_u, send_u, land_u, (sent_u, got_u))
    scatter_d = Scatter(keep_d, (d1, d2, d3), (sent_d, got_d))
    scatter_u = Scatter(keep_u, (u1, u2, u3), (sent_u, got_u))
    loads = [
        pltpu.make_async_copy(source, target, load_sems.at[i])
        for i, (source, target) in enumerate(((dm_hbm, dm), (hr_hbm, hr), (dz_hbm, total), (n1_hbm, n1)))
    ]

    @pl.when(j == 0)
    def _():
        for copy in loads:
            copy.start()
        greet()
        vec_ref[...] = jnp.zeros_like(vec_ref)
        vec_ref[0:3, :] = sums_ref[0:3, :]
        up_ref[...] = jnp.zeros_like(up_ref)
        loads[0].wait()
        turn(dm, dm_turned)
        loads[1].wait()
        turn(hr, hr_turned)

    def out_copy(m):
        return pltpu.make_async_copy(keep_u.at[m], up_hbm.at[m - early], local_u.at[m])

    def columns(m):
        return pl.ds(m * width if isinstance(m, int) else pl.multiple_of(m * width, width), width)

    def place_d(m, value):
        down_ref[:, columns(m)] = value

    def place_u(m, value):
        up_ref[:, columns(m)] = value

    def pair_down(m):
        pair_d.add(m)
        scatter_d.copy(1, m).start()

    def pair_up(m):
        pair_u.add(m)
        if m < early + MIDDLE_UP:
            scatter_u.start(1, m)
        else:
            out_copy(m).start()

    def half_up(m):
        scatter_u.add(1, m)
        out_copy(m).start()

    actions = {"d0": pair_down, "u0": pair_up, "uh": half_up}
    actions |= scatter_d.actions("d", place_d) | scatter_u.actions("u", place_u)

    def tick(site):
        run_events(FFN_EVENTS, actions, FFN_SITES[site], j)

    fast = j < steps // 2

    @pl.when(fast)
    def _():
        for part in range(2):
            m = 2 * j + part
            pair_d.free(m)
            for own, g_ref in ((0, g_oth), (1, g_own)):
                product = dot(dm_turned[...], g_ref[:, part * width : (part + 1) * width])
                pair_d.store(m, product, own, part, part)
            pair_d.copy(m).start()

    low = []
    for own, slope, weight in ((0, s_oth, wd_oth), (1, s_own, wd_own)):
        raised = dot_nt(dm[...], weight[...]) * slope[...].astype(jnp.float32)
        low.append(raised.astype(jnp.bfloat16))
        spot = t * own + (1 - t) * (1 - own)
        row = 6 + 2 * spot + lax.div(j, 4)
        vec_ref[pl.ds(row, 1), columns(lax.rem(j, 4))] = jnp.sum(
            low[-1].astype(jnp.float32), axis=0, keepdims=True
        )
    tick(0)
    pair_u.free(j)
    for own in range(2):
        pair_u.store(j, dot(hr_turned[...], low[own]), own, lax.rem(j, 2), lax.rem(j, 2))
    pair_u.copy(j).start()

    @pl.when(j == 0)
    def _():
        loads[2].wait()

    total[...] += dot_nt(low[0], wu_oth[...]) + dot_nt(low[1], wu_own[...])
    tick(1)

    @pl.when(j == steps - 1)
    def _():
        loads[3].wait()
        tile = 128

        @pl.loop(0, total.shape[0] // tile)
        def _(r):
            here = pl.ds(pl.multiple_of(r * tile, tile), tile)
            upstream = total[here, :]
            normed = n1[here, :]
            grad = norm_backward(upstream, g1_ref[...], normed, scale_ref[here, 0:1])
            grad_low = grad.astype(jnp.bfloat16)
            total[here, :] = grad
            hr[here, :] = grad_low
            vec_ref[3:4, :] += jnp.sum(upstream, axis=0, keepdims=True)
            vec_ref[4:5, :] += jnp.sum(upstream * normed, axis=0, keepdims=True)
            vec_ref[5:6, :] += jnp.sum(grad_low.astype(jnp.float32), axis=0, keepdims=True)
            run_events(FFN_EVENTS, actions, range(FFN_TICKS, FFN_TICKS + 8), r)

        outs = [
            pltpu.make_async_copy(source, target, out_sems.at[i])
            for i, (source, target) in enumerate(((total, dz_out), (hr, da_out)))
        ]
        for copy in outs:
            copy.start()

        run_events(FFN_EVENTS, actions, range(FFN_TICKS + 8, FFN_END))

        for m in range(CHUNKS - 2, CHUNKS):
            pair_d.copy(m).wait_send()
            pair_u.copy(m).wait_send()

        for m in range(CHUNKS):
            for stage in (1, 2):
                scatter_d.drain(stage, m)
                if m < early or (stage == 1 and m < early + MIDDLE_UP):
                    scatter_u.drain(stage, m)
        for m in range(CHUNKS // 2):
            for stage in (3, 4, 5):
                scatter_d.drain(stage, m)
                if m < early // 2:
                    scatter_u.drain(stage, m)

        @pl.loop(early, CHUNKS)
        def _(m):
            out_copy(m).wait()

        for copy in outs:
            copy.wait()


def ffn_backward(
    grad_branch, hidden_rows, grad_two, normed_one, scaled_one, gain_one, sums,
    act, act2, slope, slope2, w_down, w_down2, w_up, w_up2,
):
    rows, depth = grad_branch.shape
    inner = act.shape[1]
    tile = inner // CHUNKS
    last = CHUNKS // 2 - 1
    fixed = lambda *shape: pl.BlockSpec(shape, lambda j: (0,) * len(shape))
    anywhere = pl.BlockSpec(memory_space=pl.ANY)
    double = pl.BlockSpec((rows, 2 * tile), lambda j: (0, jnp.minimum(j, last)))
    column = pl.BlockSpec((rows, tile), lambda j: (0, j))
    row = pl.BlockSpec((tile, depth), lambda j: (j, 0))
    weight_column = pl.BlockSpec((depth, tile), lambda j: (0, j))
    sems = pltpu.SemaphoreType.DMA((6, CHUNKS))
    low, f32 = jnp.bfloat16, jnp.float32
    early = EARLY_UP
    return pl.pallas_call(
        ffn_back_kernel,
        grid=(CHUNKS,),
        in_specs=[anywhere] * 4
        + [fixed(rows, 128), fixed(1, depth), fixed(8, depth)]
        + [double, double, column, column, row, row, weight_column, weight_column],
        out_specs=[
            fixed(depth // 16, inner), fixed(depth // 16, max(early, 1) * tile), fixed(16, depth),
            anywhere, anywhere, anywhere,
        ],
        out_shape=[
            jax.ShapeDtypeStruct((depth // 16, inner), f32),
            jax.ShapeDtypeStruct((depth // 16, max(early, 1) * tile), f32),
            jax.ShapeDtypeStruct((16, depth), f32),
            jax.ShapeDtypeStruct((CHUNKS - early, 2, 2, SPAN, tile), low),
            jax.ShapeDtypeStruct((rows, depth), f32),
            jax.ShapeDtypeStruct((rows, depth), low),
        ],
        scratch_shapes=[
            low_buffer(rows, depth),
            low_buffer(rows, depth),
            pltpu.VMEM((rows, depth), f32),
            low_buffer(depth, rows),
            low_buffer(depth, rows),
            pltpu.VMEM((rows, depth), f32),
            low_buffer(CHUNKS, 2, 2, SPAN, tile),
            low_buffer(2, 2, 2, SPAN, tile),
            low_buffer(CHUNKS, 2, 2, SPAN, tile),
            *land_scratch(CHUNKS, SPAN, tile),
            low_buffer(CHUNKS, 2, 2, SPAN, tile),
            low_buffer(2, 2, 2, SPAN, tile),
            low_buffer(CHUNKS, 2, 2, SPAN, tile),
            low_buffer(max(early + MIDDLE_UP, 1), 2, SPAN, tile),
            *land_scratch(max(early, 2), SPAN, tile)[1:],
            sems, sems, sems, sems,
            pltpu.SemaphoreType.DMA((CHUNKS,)),
            pltpu.SemaphoreType.DMA((4,)),
            pltpu.SemaphoreType.DMA((2,)),
        ],
        compiler_params=pltpu.CompilerParams(
            vmem_limit_bytes=VMEM, collective_id=1, has_side_effects=True
        ),
        cost_estimate=pl.CostEstimate(
            flops=rows * depth * inner * 16, bytes_accessed=60 * 1024 * 1024, transcendentals=0
        ),
        name="ffn_backward",
    )(
        grad_branch, hidden_rows, grad_two, normed_one, scaled_one, gain_one.reshape(1, -1), sums,
        act, act2, slope, slope2, w_down, w_down2, w_up, w_up2,
    )


def attend_back_one(queries, key_rows, values, grad_ctx, levels):
    scale = HEAD_DIM**-0.5
    first = head_masks(128)
    masks = (first, jnp.logical_not(first))
    keys_t = key_rows.T
    picked = [jnp.where(mask, queries, jnp.zeros_like(queries)) for mask in masks]
    grad_picked = [jnp.where(mask, grad_ctx, jnp.zeros_like(grad_ctx)) for mask in masks]
    scores = [dot_nt(key_rows, rows) for rows in picked]
    grad_weights = [dot_nt(values, rows) for rows in grad_picked]
    parts = []
    grad_k = grad_v = None
    for head in range(2):
        weights = jnp.exp2(scores[head] * (LOG2E * scale) - levels[head])
        piece_v = dot(weights.astype(jnp.bfloat16), grad_picked[head])
        rowsum = jnp.sum(weights * grad_weights[head], axis=0, keepdims=True)
        grad_low = (weights * (grad_weights[head] - rowsum)).astype(jnp.bfloat16)
        piece_k = dot(grad_low, picked[head])
        grad_v = piece_v if grad_v is None else grad_v + piece_v
        grad_k = piece_k if grad_k is None else grad_k + piece_k
        parts.append(dot(keys_t[head * HEAD_DIM : (head + 1) * HEAD_DIM], grad_low))
    grad_q = jnp.concatenate(parts, axis=0).T
    return (
        (grad_q * scale).astype(jnp.bfloat16),
        (grad_k * scale).astype(jnp.bfloat16),
        grad_v.astype(jnp.bfloat16),
    )


class Total:
    def __init__(self, sums, lands, sems):
        self.sums, self.lands = sums, lands
        self.sent, self.got = sems

    def copy(self, stage):
        dp, t = mine()
        peer = ((flip(dp, 1), t), (dp, 1 - t), (flip(dp, 2), t), (flip(dp, 4), t), (flip(dp, 8), t))[stage]
        return pltpu.make_async_remote_copy(
            src_ref=self.sums.at[stage],
            dst_ref=self.lands.at[stage],
            send_sem=self.sent.at[stage],
            recv_sem=self.got.at[stage],
            device_id=peer,
            device_id_type=MESH,
        )

    def step(self, stage):
        self.copy(stage).wait_recv()
        self.sums[stage + 1] = self.sums[stage] + self.lands[stage]
        if stage < 4:
            self.copy(stage + 1).start()

    def drain(self):
        for stage in range(5):
            self.copy(stage).wait_send()


def attend_back_kernel(
    da_hbm, x_hbm, up_hbm, dz_hbm, wq_own_hbm, wq_oth_hbm, vec_ref, level_ref,
    qkv_own, c_own, wo_own, qkv_oth, c_oth, wo_oth,
    gin_hbm, gup_ref, gout_ref, gqkv_ref, vec_out, bias_out,
    da, xs, da_turned, x_turned, total, stack, wq,
    keep_u, u1, u2, u3,
    keep_a, send_a, land_a, a1, a2, a3,
    vec_sums, vec_lands, bias_sums, bias_lands,
    sent_u, got_u, sent_a, got_a, sent_v, got_v, sent_b, got_b, local_u, load_sems, out_sems,
):
    g = pl.program_id(0)
    steps = pl.num_programs(0)
    seqs = xs.shape[0] // SEQ
    late = keep_u.shape[0]
    n_chunks = keep_a.shape[0]
    pair = Pair(keep_a, send_a, land_a, (sent_a, got_a))
    scatter_a = Scatter(keep_a, (a1, a2, a3), (sent_a, got_a))
    scatter_u = Scatter(keep_u, (u1, u2, u3), (sent_u, got_u), EARLY_UP)
    vec_total = Total(vec_sums, vec_lands, (sent_v, got_v))
    bias_total = Total(bias_sums, bias_lands, (sent_b, got_b))
    _, t = mine()

    def load_up(m):
        return pltpu.make_async_copy(up_hbm.at[m], keep_u.at[m], local_u.at[m])

    pairs = ((x_hbm, xs), (da_hbm, da), (dz_hbm, total), (wq_oth_hbm, wq.at[0]), (wq_own_hbm, wq.at[1]))
    loads = [pltpu.make_async_copy(*ends, load_sems.at[i]) for i, ends in enumerate(pairs)]

    @pl.when(g == 0)
    def _():
        for m in range(late):
            load_up(m).start()
        for copy in loads:
            copy.start()
        greet()
        for m in range(late):
            load_up(m).wait()
            scatter_u.start(2 if m < MIDDLE_UP else 1, m)
        vec_sums[0] = vec_ref[...]
        vec_total.copy(0).start()
        bias_sums[0] = jnp.zeros_like(bias_sums[0])
        loads[1].wait()
        turn(da, da_turned)
        loads[0].wait()
        turn(xs, x_turned)

    def place_u(m, value):
        width = value.shape[1]
        gup_ref[:, m * width : (m + 1) * width] = value

    def place_a(m, value):
        cols = slice(m // 2 * 128, m // 2 * 128 + 128)
        left, right = value[:, :128], value[:, 128:]
        if m % 2 == 0:
            gout_ref[:, cols] = left
            gqkv_ref[1, :, cols] = right
        else:
            gqkv_ref[0, :, cols] = left
            gqkv_ref[2, :, cols] = right

    def pair_a(m):
        pair.add(m)
        scatter_a.copy(1, m).start()

    actions = {"a0": pair_a} | scatter_u.actions("u", place_u) | scatter_a.actions("a", place_a)

    def tick(site):
        run_events(ATT_EVENTS, actions, range(site, ATT_TICKS, 3), g)

    cols = pl.ds(pl.multiple_of(g * 128, 128), 128)

    def gradient(turned, other, own):
        product = dot(turned[...], jnp.concatenate([other, own], axis=1))
        return product[:, :128], product[:, 128:]

    def emit(part, first, second):
        m = 2 * g + part
        pair.free(m)
        for own in range(2):
            pair.store(m, jnp.concatenate([first[own], second[own]], axis=1), own, part, part)
        pair.copy(m).start()

    for own, qkv_ref, wo_ref in ((0, qkv_oth, wo_oth), (1, qkv_own, wo_own)):
        grad_ctx = dot_nt(da[...], wo_ref[...]).astype(jnp.bfloat16)
        for s in range(seqs):
            rows = slice(s * SEQ, (s + 1) * SEQ)
            levels = [level_ref[own, s, pl.ds(2 * g + head, 1), :] for head in range(2)]
            grads = attend_back_one(
                qkv_ref[0, rows, :], qkv_ref[1, rows, :], qkv_ref[2, rows, :], grad_ctx[rows], levels
            )
            for kind in range(3):
                stack[own * 3 + kind, rows, cols] = grads[kind]
            if s == seqs - 1:
                spot = t * own + (1 - t) * (1 - own)
                where = pl.ds(pl.multiple_of(spot * 512 + g * 128, 128), 128)
                for row, kind in ((0, 0), (1, 2)):
                    bias_sums[0, row : row + 1, where] = jnp.sum(
                        stack[own * 3 + kind, :, cols].astype(jnp.float32), axis=0, keepdims=True
                    )
        tick(own)

    @pl.when(g == steps - 1)
    def _():
        bias_total.copy(0).start()

    grads = [gradient(x_turned, stack[kind, :, cols], stack[kind + 3, :, cols]) for kind in range(3)]
    emit(1, grads[0], grads[2])
    emit(0, gradient(da_turned, c_oth[...], c_own[...]), grads[1])
    tick(2)
    for stage in range(3):
        @pl.when(g == stage)
        def _():
            vec_total.step(stage)

    @pl.when(g == steps - 1)
    def _():
        for copy in loads[2:]:
            copy.wait()
        vec_total.step(3)
        tile = xs.shape[0] // 4
        outs = []
        for r in range(4):
            here = slice(r * tile, (r + 1) * tile)
            block = total[here, :]
            for own in range(2):
                for kind in range(3):
                    block = block + dot_nt(stack[own * 3 + kind, here, :], wq[own, kind])
            total[here, :] = block
            outs.append(pltpu.make_async_copy(total.at[here], gin_hbm.at[here], out_sems.at[r]))
            outs[-1].start()
            run_events(ATT_EVENTS, actions, [ATT_TICKS + r])
            bias_total.step(r)
            if r == 0:
                vec_total.step(4)
        bias_total.step(4)

        run_events(ATT_EVENTS, actions, range(ATT_TICKS + 4, ATT_END))

        vec_out[...] = vec_sums[5]
        bias_out[...] = bias_sums[5]
        for m in range(pair.slots):
            pair.copy(n_chunks - 1 - m).wait_send()

        for m in range(late):
            scatter_u.drain(2, m)
            if m >= MIDDLE_UP:
                scatter_u.drain(1, m)
        for m in range(n_chunks):
            scatter_a.drain(1, m)
            scatter_a.drain(2, m)
        for stage in (3, 4, 5):
            for m in range(late // 2):
                scatter_u.drain(stage, m)
            for m in range(n_chunks // 2):
                scatter_a.drain(stage, m)
        vec_total.drain()
        bias_total.drain()
        for copy in outs:
            copy.wait()


def attend_backward(grad_attended, tokens, keep_up, grad_one, vectors, levels, w_qkv, w_qkv2, own, other):
    rows, depth = tokens.shape
    width = own[1].shape[1]
    steps = width // 128
    late, tile = keep_up.shape[0], keep_up.shape[4]
    n_chunks = 2 * steps
    fixed = lambda *shape: pl.BlockSpec(shape, lambda g: (0,) * len(shape))
    anywhere = pl.BlockSpec(memory_space=pl.ANY)
    side = [
        pl.BlockSpec((3, rows, 128), lambda g: (0, 0, g)),
        pl.BlockSpec((rows, 128), lambda g: (0, g)),
        pl.BlockSpec((128, depth), lambda g: (g, 0)),
    ]
    sems_u = pltpu.SemaphoreType.DMA((6, late))
    sems_a = pltpu.SemaphoreType.DMA((6, n_chunks))
    few = pltpu.SemaphoreType.DMA((5,))
    f32 = jnp.float32
    return pl.pallas_call(
        attend_back_kernel,
        grid=(steps,),
        in_specs=[anywhere] * 6 + [fixed(*vectors.shape), fixed(*levels.shape)] + side + side,
        out_specs=[
            anywhere, fixed(depth // 16, late * tile), fixed(depth // 16, width),
            fixed(3, depth // 16, width), fixed(*vectors.shape), fixed(8, depth),
        ],
        out_shape=[
            jax.ShapeDtypeStruct((rows, depth), f32),
            jax.ShapeDtypeStruct((depth // 16, late * tile), f32),
            jax.ShapeDtypeStruct((depth // 16, width), f32),
            jax.ShapeDtypeStruct((3, depth // 16, width), f32),
            jax.ShapeDtypeStruct(vectors.shape, f32),
            jax.ShapeDtypeStruct((8, depth), f32),
        ],
        scratch_shapes=[
            low_buffer(rows, depth),
            low_buffer(rows, depth),
            low_buffer(depth, rows),
            low_buffer(depth, rows),
            pltpu.VMEM((rows, depth), f32),
            low_buffer(6, rows, width),
            low_buffer(2, 3, depth, width),
            low_buffer(late, 2, 2, SPAN, tile),
            *land_scratch(late, SPAN, tile),
            low_buffer(n_chunks, 2, 2, SPAN, 256),
            low_buffer(2, 2, 2, SPAN, 256),
            low_buffer(n_chunks, 2, 2, SPAN, 256),
            *land_scratch(n_chunks, SPAN, 256),
            pltpu.VMEM((6, *vectors.shape), f32),
            pltpu.VMEM((5, *vectors.shape), f32),
            pltpu.VMEM((6, 8, depth), f32),
            pltpu.VMEM((5, 8, depth), f32),
            sems_u, sems_u, sems_a, sems_a, few, few, few, few,
            pltpu.SemaphoreType.DMA((late,)),
            pltpu.SemaphoreType.DMA((5,)),
            pltpu.SemaphoreType.DMA((4,)),
        ],
        compiler_params=pltpu.CompilerParams(
            vmem_limit_bytes=VMEM, collective_id=2, has_side_effects=True
        ),
        cost_estimate=pl.CostEstimate(
            flops=rows * depth * width * 40, bytes_accessed=60 * 1024 * 1024, transcendentals=0
        ),
        name="attend_backward",
    )(
        grad_attended, tokens, keep_up, grad_one, w_qkv, w_qkv2, vectors, levels, *own, *other,
    )


def deliver_kernel(
    gin, res, up_a, up_b, down, out, qkv, vec, bias,
    o_gin, o_res, o_up, o_down, o_out, o_qkv, *vectors,
):
    o_gin[...] = gin[...]
    o_res[...] = res[...]

    @pl.when(pl.program_id(0) == 0)
    def _():
        cols = o_up.shape[1] - up_b.shape[1]
        if cols:
            o_up[:, :cols] = up_a[:, :cols]
        o_up[:, cols:] = up_b[...]
        o_down[...] = down[...]
        o_out[...] = out[...]
        o_qkv[...] = qkv[...]
        for row in range(6):
            vectors[row][...] = vec[row : row + 1, :]
        wide = vec.shape[1]
        for row in range(4):
            vectors[6][:, row * wide : (row + 1) * wide] = vec[6 + row : 7 + row, :]
        vectors[7][...] = bias[0:1, :]
        vectors[8][...] = bias[1:2, :]


def deliver(gin, res, up_a, up_b, down, out, qkv, vec, bias):
    steps = 2
    wide = vec.shape[1]
    like = lambda array: jax.ShapeDtypeStruct(array.shape, array.dtype)
    flat = lambda size: jax.ShapeDtypeStruct((1, size), jnp.float32)
    fixed = lambda array: pl.BlockSpec(array.shape, lambda i: (0,) * len(array.shape))
    tall = pl.BlockSpec((gin.shape[0] // steps, gin.shape[1]), lambda i: (i, 0))
    up = like(down)
    flats = [flat(wide)] * 6 + [flat(4 * wide)] + [flat(wide)] * 2
    small = [up, like(down), like(out), like(qkv)] + flats
    return pl.pallas_call(
        deliver_kernel,
        grid=(steps,),
        in_specs=[tall, tall] + [fixed(array) for array in (up_a, up_b, down, out, qkv, vec, bias)],
        out_specs=[tall, tall] + [fixed(array) for array in small],
        out_shape=[like(gin), like(res)] + small,
        compiler_params=pltpu.CompilerParams(vmem_limit_bytes=VMEM),
        name="deliver",
    )(gin, res, up_a, up_b, down, out, qkv, vec, bias)


def attend_one(queries, key_rows, values):
    first = head_masks(128)
    values_t = values.T
    parts, levels = [], []
    for head in range(2):
        mask = first if head == 0 else jnp.logical_not(first)
        picked = jnp.where(mask, queries, jnp.zeros_like(queries))
        scores = dot_nt(key_rows, picked) * (LOG2E * HEAD_DIM**-0.5)
        peak = jnp.max(scores, axis=0, keepdims=True)
        lifted = jnp.exp2(scores - peak)
        totals = jnp.sum(lifted, axis=0, keepdims=True)
        context = dot(values_t[head * HEAD_DIM : (head + 1) * HEAD_DIM], lifted.astype(jnp.bfloat16))
        parts.append(context * (1.0 / totals))
        levels.append(peak + jnp.log2(totals))
    return jnp.concatenate(parts, axis=0).T.astype(jnp.bfloat16), levels


class Fetch:
    HOPS = 10

    def __init__(self, source, target, unit, index, sems):
        self.source, self.target, self.unit, self.index = source, target, unit, index
        self.sent, self.got = sems

    def copy(self, hop):
        dp, t = mine()
        core, x, z = bit_of(dp, 1), bit_of(dp, 2), bit_of(dp, 4)
        quarter = {0: x * 2 + z, 1: (1 - x) * 2 + z, 2: x * 2 + 1 - z, 3: (1 - x) * 2 + 1 - z}
        if hop == 0:
            which, part, peer = 0, None, (dp, 1 - t)
        elif hop == 1:
            which, part, peer = 0, None, (flip(dp, 2), t)
        elif hop == 2:
            which, part, peer = 0, None, (flip(dp, 4), t)
        elif hop == 3:
            which, part, peer = 2, 1, (flip(dp, 2), t)
        elif hop == 4:
            which, part, peer = 1, 2, (flip(dp, 4), t)
        elif hop == 9:
            which, part, peer = 3, 0, (dp, 1 - t)
        else:
            which, part, peer = hop - 5, None, (flip(dp, 1), t)
        place = self.unit(core, quarter[which], part, self.index)
        origin = self.source if hop in (0, 9) else self.target
        return pltpu.make_async_remote_copy(
            src_ref=origin.at[place],
            dst_ref=self.target.at[place],
            send_sem=self.sent.at[self.index, hop],
            recv_sem=self.got.at[self.index, hop],
            device_id=peer,
            device_id_type=MESH,
        )

    def start(self, *hops):
        for hop in hops:
            self.copy(hop).start()

    def arrive(self, *hops):
        for hop in hops:
            self.copy(hop).wait_recv()

    def advance(self, stage):
        if stage == 1:
            self.arrive(0)
            self.start(1, 2, 5)
        elif stage == 2:
            self.arrive(1, 2)
            self.start(3, 4, 6, 7)
        elif stage == 3:
            self.arrive(3, 4, 9)
            self.start(8)
        else:
            self.arrive(5, 6, 7, 8)

    def drain(self):
        for hop in range(self.HOPS):
            self.copy(hop).wait_send()


AHEAD = 2
BANDS = (0, 256, 512)
FORWARD_EVENTS = (
    (),
    (),
    (),
    (),
    (),
    ((1, 0),),
    (),
    ((1, 1), (1, 2), (2, 0), (1, 3), (2, 1), (1, 4), (2, 2), (3, 0), (1, 5), (2, 3), (4, 0)),
    (),
    (),
    (),
    ((3, 1),),
    ((1, 6), (2, 4), (3, 2), (1, 7), (4, 1)),
    (),
    (),
    ((2, 5),),
    ((3, 3),),
    ((4, 2), (2, 6), (1, 8), (3, 4)),
    ((4, 3), (2, 7), (1, 9), (3, 5), (3, 6)),
    ((4, 4), (1, 10)),
    ((2, 8),),
    ((3, 7), (4, 5)),
    ((4, 6),),
    ((2, 9),),
    ((4, 7), (2, 10)),
    ((3, 8),),
    ((3, 9),),
    ((3, 10),),
    ((4, 8),),
    ((4, 9),),
    ((4, 10),),
    (),
    (),
    (),
    (),
)
BANDS = (0, 256, 512)
PACE = 4.0


def unit_of(total, lead=(), base=0, tail=()):
    def unit(core, quarter, part, index):
        size = total // 8
        start = base + core * (total // 2) + quarter * size
        if part is not None:
            sixteens = [size // 48] * 3
            for extra in range(size // 16 - sum(sixteens)):
                sixteens[(index + extra) % 3] += 1
            start = start + 16 * sum(sixteens[:part])
            size = 16 * sixteens[part]
        return (*lead, pl.ds(pl.multiple_of(start, 16), size), *tail)

    return unit


def forward_kernel(
    x_hbm, cot_hbm, wq_hbm, wo_hbm, wu_hbm, wd_hbm,
    bq_ref, bv_ref, bu_ref, bo_ref, g1_ref, s1_ref, bd_ref, g2_ref, s2_ref,
    qkv_out1, qkv_out0, ctx_out1, ctx_out0, act_out1, act_out0, slope_out1, slope_out0,
    hr_out, n1_out, dm_out, dz_out, res_out, wq_out, wo_out, wu_out, wd_out,
    level_ref, scale_ref, sums_ref,
    x, cot, wq1, wq0, wo1, wo0, wu1, wu0, wd1, wd0, qkv1, qkv0, ctx1, ctx0, n1, hr, total, act, slope,
    bias_own, bias_oth, sent, got, bias_sent, bias_got, load_sems, out_sems,
):
    dp, t = mine()
    rows, depth = x.shape
    seqs = rows // SEQ
    width = ctx1.shape[1]
    inner = wu1.shape[1]
    tiles = 4
    span = inner // tiles

    chunks = []

    def chunk(source, target, unit):
        chunks.append(Fetch(source, target, unit, len(chunks), (sent, got)))
        return len(chunks) - 1

    starts = BANDS
    bands = [pl.ds(a, b - a) for a, b in zip(starts, starts[1:])]
    c_qkv = [chunk(wq1, wq0, unit_of(depth, lead=(slice(None),), tail=(cols,))) for cols in bands]
    c_out = chunk(wo1, wo0, unit_of(width))
    c_up, c_down = [], []
    for j in range(tiles):
        c_up.append(chunk(wu1, wu0, unit_of(depth, tail=(pl.ds(j * span, span),))))
        c_down.append(chunk(wd1, wd0, unit_of(span, base=j * span)))

    loads, outs, done = {}, [], []
    here_names = {id(wq1): "q", id(wo1): "o", id(wu1): "u", id(wd1): "d"}
    loaded = set()

    def ensure(name):
        if name not in loaded:
            loaded.add(name)
            loads[name].wait()

    def begin(m):
        ensure(here_names[id(chunks[m].source)])
        chunks[m].start(0, 9)

    def finish(copy):
        copy.wait()
        done.append(copy)

    def load(name, source, target):
        copy = pltpu.make_async_copy(source, target, load_sems.at[len(loads)])
        loads[name] = copy
        copy.start()

    def save(source, target):
        copy = pltpu.make_async_copy(source, target, out_sems.at[len(outs)])
        outs.append(copy)
        copy.start()
        return copy

    load("x", x_hbm, x)
    load("q", wq_hbm, wq1)
    greet()
    ahead = AHEAD
    for m in range(ahead):
        begin(m)
    bias_own[:, :width] = bq_ref[...]
    bias_own[:, width : 2 * width] = bv_ref[...]
    bias_own[:, 2 * width :] = bu_ref[...]
    bias_copy = pltpu.make_async_remote_copy(
        src_ref=bias_own, dst_ref=bias_oth, send_sem=bias_sent, recv_sem=bias_got,
        device_id=(dp, 1 - t), device_id_type=MESH,
    )
    bias_copy.start()
    load("o", wo_hbm, wo1)
    load("u", wu_hbm, wu1)
    load("d", wd_hbm, wd1)
    load("cot", cot_hbm, cot)

    saves = {}
    for i, cols in enumerate(bands):
        saves[c_qkv[i]] = (wq0.at[:, :, cols], wq_out.at[:, :, cols])
    saves[c_out] = (wo0, wo_out)
    for j in range(tiles):
        cols = pl.ds(j * span, span)
        saves[c_up[j]] = (wu0.at[:, cols], wu_out.at[:, cols])
        saves[c_down[j]] = (wd0.at[cols], wd_out.at[cols])

    points = iter(FORWARD_EVENTS)

    def point():
        for stage, m in next(points):
            chunks[m].advance(stage)
            if stage == 1 and m + ahead < len(chunks):
                begin(m + ahead)
            if stage == 4:
                save(*saves[m])

    def project(weights, kind, kept, biases, cols):
        product = dot(x[...], weights[kind, :, cols])
        if kind != 1:
            at = cols.start + (0 if kind == 0 else width)
            product = product + biases[:, at : at + cols.stop - cols.start]
        kept[kind, :, cols] = product.astype(jnp.bfloat16)

    def attend(side, kept, context, pair):
        cols = slice(pair * 128, pair * 128 + 128)

        for s in range(seqs):
            here = pl.ds(s * SEQ, SEQ)
            out, levels = attend_one(kept[0, here, cols], kept[1, here, cols], kept[2, here, cols])
            context[here, cols] = out
            for head in range(2):
                spot = 2 * pair + head
                level_ref[side, s, spot : spot + 1, :] = levels[head]

    loads["x"].wait()
    for kind in range(3):
        point()
        project(wq1, kind, qkv1, bias_own, slice(0, width))
    save(qkv1, qkv_out1)
    for pair in range(width // 128):
        point()
        attend(1, qkv1, ctx1, pair)
    save(ctx1, ctx_out1)
    bias_copy.wait_recv()
    for i, (low, high) in enumerate(zip(starts, starts[1:])):
        for kind in range(3):
            point()
            project(wq0, kind, qkv0, bias_oth, slice(low, high))
        for pair in range(low // 128, high // 128):
            point()
            attend(0, qkv0, ctx0, pair)
    save(qkv0, qkv_out0)
    save(ctx0, ctx_out0)
    ensure("o")
    point()
    step = 256

    @pl.loop(0, rows // step)
    def _(r):
        here = pl.ds(pl.multiple_of(r * step, step), step)
        attended = dot(ctx1[here, :], wo1[...]) + dot(ctx0[here, :], wo0[...])
        _, normed, scaled = norm_forward(
            x[here, :].astype(jnp.float32) + attended + bo_ref[...], g1_ref[...], s1_ref[...]
        )
        n1[here, :] = normed
        hr[here, :] = (normed * g1_ref[...] + s1_ref[...]).astype(jnp.bfloat16)
        scale_ref[here, :] = jnp.broadcast_to(scaled, (step, 128))

    save(n1, n1_out)
    hr_saved = save(hr, hr_out)
    ensure("u")
    ensure("d")
    big = 512
    slots = []
    for side, up, down, biases, act_out, slope_out in (
        (1, wu1, wd1, bias_own, act_out1, slope_out1),
        (0, wu0, wd0, bias_oth, act_out0, slope_out0),
    ):
        for j in range(tiles):
            cols = pl.ds(j * span, span)
            slot = len(slots) % 2
            if len(slots) >= 2:
                for copy in slots[-2]:
                    finish(copy)
            bias = biases[:, 2 * width + j * span : 2 * width + (j + 1) * span]
            fresh = not slots

            for r in range(rows // big):
                point()
                here = pl.ds(r * big, big)
                activated, leaning = gelu_pair(dot(hr[here, :], up[:, cols]) + bias)
                activated = activated.astype(jnp.bfloat16)
                act[slot, here, :] = activated
                slope[slot, here, :] = leaning.astype(jnp.bfloat16)
                product = dot(activated, down[cols, :])
                total[here, :] = product if fresh else total[here, :] + product

            slots.append((
                save(act.at[slot], act_out.at[:, cols]),
                save(slope.at[slot], slope_out.at[:, cols]),
            ))
    point()
    finish(hr_saved)
    loads["cot"].wait()
    sums_ref[...] = jnp.zeros_like(sums_ref)

    for r in range(rows // step):
        here = pl.ds(r * step, step)
        hidden = n1[here, :] * g1_ref[...] + s1_ref[...]
        result, normed, scaled = norm_forward(hidden + total[here, :] + bd_ref[...], g2_ref[...], s2_ref[...])
        x[here, :] = result.astype(jnp.bfloat16)
        upstream = cot[here, :].astype(jnp.float32)
        grad = norm_backward(upstream, g2_ref[...], normed, scaled)
        total[here, :] = grad
        low = grad.astype(jnp.bfloat16)
        hr[here, :] = low
        sums_ref[0:1, :] += jnp.sum(upstream, axis=0, keepdims=True)
        sums_ref[1:2, :] += jnp.sum(upstream * normed, axis=0, keepdims=True)
        sums_ref[2:3, :] += jnp.sum(low.astype(jnp.float32), axis=0, keepdims=True)
        save(x.at[here], res_out.at[here])
        save(hr.at[here], dm_out.at[here])
        save(total.at[here], dz_out.at[here])

    bias_copy.wait_send()
    for fetch in chunks:
        fetch.drain()
    for copy in outs:
        if not any(copy is other for other in done):
            copy.wait()


def forward(tokens, cotangent, w_qkv, w_out, w_up, w_down, biases, bias_o, gain_one, shift_one, bias_down, gain_two, shift_two):
    rows, depth = tokens.shape
    width, inner = w_out.shape[0], w_up.shape[1]
    seqs, heads = rows // SEQ, width // HEAD_DIM
    low, f32 = jnp.bfloat16, jnp.float32
    any_space = pl.BlockSpec(memory_space=pl.ANY)
    near = pl.BlockSpec(memory_space=pltpu.VMEM)
    qkv = (3, rows, width)
    outs = [
        (qkv, low), (qkv, low), ((rows, width), low), ((rows, width), low),
        ((rows, inner), low), ((rows, inner), low), ((rows, inner), low), ((rows, inner), low),
        ((rows, depth), low), ((rows, depth), f32), ((rows, depth), low), ((rows, depth), f32), ((rows, depth), low),
        (w_qkv.shape, low), (w_out.shape, low), (w_up.shape, low), (w_down.shape, low),
        ((2, seqs, heads, SEQ), f32), ((rows, 128), f32), ((8, depth), f32),
    ]
    span = inner // 4
    flat = (1, 2 * width + inner)
    scratch = [
        ((rows, depth), low), ((rows, depth), low), (w_qkv.shape, low), (w_qkv.shape, low),
        (w_out.shape, low), (w_out.shape, low), (w_up.shape, low), (w_up.shape, low),
        (w_down.shape, low), (w_down.shape, low), (qkv, low), (qkv, low),
        ((rows, width), low), ((rows, width), low), ((rows, depth), f32), ((rows, depth), low),
        ((rows, depth), f32), ((2, rows, span), low), ((2, rows, span), low), (flat, f32), (flat, f32),
    ]
    sems = pltpu.SemaphoreType.DMA((len(BANDS) + 8, Fetch.HOPS))
    one = pltpu.SemaphoreType.DMA
    return pl.pallas_call(
        forward_kernel,
        in_specs=[any_space] * 6 + [near] * 9,
        out_specs=[any_space] * 17 + [near] * 3,
        out_shape=[jax.ShapeDtypeStruct(*out) for out in outs],
        scratch_shapes=[pltpu.VMEM(*buffer) for buffer in scratch]
        + [sems, sems, one, one, pltpu.SemaphoreType.DMA((8,)), pltpu.SemaphoreType.DMA((48,))],
        compiler_params=pltpu.CompilerParams(
            vmem_limit_bytes=60 * 1024 * 1024, collective_id=3, has_side_effects=True
        ),
        cost_estimate=pl.CostEstimate(
            flops=rows * depth * (width * 16 + inner * 8), bytes_accessed=80 * 1024 * 1024, transcendentals=0
        ),
        name="forward",
    )(
        tokens, cotangent, w_qkv, w_out, w_up, w_down,
        *(v.reshape(1, -1) for v in (*biases, bias_o, gain_one, shift_one, bias_down, gain_two, shift_two)),
    )


def body(mesh, *args):
    tokens, w_qkv = args[0], args[2]
    n_dp, n_tensor = mesh.shape["dp"], mesh.shape["tensor"]
    local = (*tokens.shape, w_qkv.shape[2], args[9].shape[1])
    if (n_dp, n_tensor) == (16, 2) and local == (1024, 1024, 512, 2048):
        return body_tokens(*args)
    return body_tensor(*args)


def body_tokens(
    tokens,
    cotangent,
    w_qkv,
    bias_q,
    bias_v,
    w_out,
    bias_o,
    gain_one,
    shift_one,
    w_up,
    bias_up,
    w_down,
    bias_down,
    gain_two,
    shift_two,
):
    (
        qkv, qkv2, ctx, ctx2, active, active2, slope, slope2,
        hidden_rows, normed_one, grad_branch, grad_two, result,
        w_qkv2, w_out2, w_up2, w_down2, levels, scaled_one, sums,
    ) = forward(
        tokens, cotangent, w_qkv, w_out, w_up, w_down, (bias_q, bias_v, bias_up),
        bias_o, gain_one, shift_one, bias_down, gain_two, shift_two,
    )
    grad_down, up_early, vectors, keep_up, grad_one, grad_attended = ffn_backward(
        grad_branch, hidden_rows, grad_two, normed_one, scaled_one, gain_one, sums,
        active, active2, slope, slope2, w_down, w_down2, w_up, w_up2,
    )
    grad_input, up_late, grad_out, grad_qkv, vectors, biases = attend_backward(
        grad_attended, tokens, keep_up, grad_one, vectors, levels, w_qkv, w_qkv2,
        (qkv, ctx, w_out), (qkv2, ctx2, w_out2),
    )
    grad_input, result, grad_up, grad_down, grad_out, grad_qkv, *vectors = deliver(
        grad_input, result, up_early, up_late, grad_down, grad_out, grad_qkv, vectors, biases
    )
    g_shift_two, g_gain_two, g_bias_down, g_shift_one, g_gain_one, g_bias_o, g_bias_up, g_bias_q, g_bias_v = (
        vector.reshape(-1) for vector in vectors
    )
    return (
        result,
        grad_input,
        grad_qkv,
        g_bias_q,
        g_bias_v,
        grad_out.T,
        g_bias_o,
        g_gain_one,
        g_shift_one,
        grad_up,
        g_bias_up,
        grad_down.T,
        g_bias_down,
        g_gain_two,
        g_shift_two,
    )


def solution(mesh):
    in_specs = (
        P(("dp", "tensor"), None),
        P(("dp", "tensor"), None),
        P(None, None, "tensor"),
        P("tensor"),
        P("tensor"),
        P("tensor", None),
        P(),
        P(),
        P(),
        P(None, "tensor"),
        P("tensor"),
        P("tensor", None),
        P(),
        P(),
        P(),
    )
    out_specs = (
        P(("dp", "tensor"), None),
        P(("dp", "tensor"), None),
        P(None, "dp", "tensor"),
        P(),
        P(),
        P("tensor", "dp"),
        P(),
        P(),
        P(),
        P("dp", "tensor"),
        P(),
        P("tensor", "dp"),
        P(),
        P(),
        P(),
    )
    return jax.shard_map(functools.partial(body, mesh), mesh=mesh, in_specs=in_specs, out_specs=out_specs, check_vma=False)
```

```python
import functools

import jax
import jax.numpy as jnp
from jax import lax
from jax.experimental import pallas as pl
from jax.experimental.pallas import tpu as pltpu
from jax.sharding import PartitionSpec as P

D = 1024
FF = 4096
HEAD_DIM = 64
SEQ = 512


def gelu_pair(inner_pre):
    normal_cdf = 0.5 * (1.0 + jax.scipy.special.erf(inner_pre * 0.7071067811865476))
    density = jnp.exp(-0.5 * inner_pre * inner_pre) * 0.3989422804014327
    return (inner_pre * normal_cdf, normal_cdf + inner_pre * density)


def norm_forward(summed, gain, shift):
    centre = summed - jnp.mean(summed, axis=-1, keepdims=True)
    scaled = lax.rsqrt(jnp.mean(centre * centre, axis=-1, keepdims=True) + 1e-05)
    normed = centre * scaled
    return (normed * gain + shift, normed, scaled)


def norm_backward(upstream, gain, normed, scaled):
    grad_norm = upstream * gain
    return scaled * (
        grad_norm
        - jnp.mean(grad_norm, axis=-1, keepdims=True)
        - normed * jnp.mean(grad_norm * normed, axis=-1, keepdims=True)
    )


def attend_block(block):
    queries, key_rows, values = block
    scores = jnp.einsum(
        "qhd,khd->hqk", queries, key_rows, preferred_element_type=jnp.float32
    ) * HEAD_DIM ** (-0.5)
    peak_score = jnp.max(scores, axis=-1, keepdims=True)
    lifted = jnp.exp(scores - peak_score)
    totals = jnp.sum(lifted, axis=-1, keepdims=True)
    weights = (lifted / totals).astype(jnp.bfloat16)
    context = jnp.einsum("hqk,khd->qhd", weights, values, preferred_element_type=jnp.float32)
    return (context.astype(jnp.bfloat16), (peak_score + jnp.log(totals))[..., 0])


def attend_back(block):
    queries, key_rows, values, logsum, grad_ctx = block
    scale = HEAD_DIM ** (-0.5)
    scores = (
        jnp.einsum("qhd,khd->hqk", queries, key_rows, preferred_element_type=jnp.float32) * scale
    )
    weights = jnp.exp(scores - logsum[..., None])
    grad_weights = jnp.einsum("qhd,khd->hqk", grad_ctx, values, preferred_element_type=jnp.float32)
    grad_scores = weights * (grad_weights - jnp.sum(weights * grad_weights, axis=-1, keepdims=True))
    grad_low = grad_scores.astype(jnp.bfloat16)
    grad_v = jnp.einsum(
        "hqk,qhd->khd", weights.astype(jnp.bfloat16), grad_ctx, preferred_element_type=jnp.float32
    )
    grad_q = (
        jnp.einsum("hqk,khd->qhd", grad_low, key_rows, preferred_element_type=jnp.float32) * scale
    )
    grad_k = (
        jnp.einsum("hqk,qhd->khd", grad_low, queries, preferred_element_type=jnp.float32) * scale
    )
    return (grad_q.astype(jnp.bfloat16), grad_k.astype(jnp.bfloat16), grad_v.astype(jnp.bfloat16))


def body_tensor(
    tokens,
    cotangent,
    w_qkv,
    bias_q,
    bias_v,
    w_out,
    bias_o,
    gain_one,
    shift_one,
    w_up,
    bias_up,
    w_down,
    bias_down,
    gain_two,
    shift_two,
):
    rank = lax.axis_index("tensor")
    full_rows = lax.all_gather(tokens, "tensor", axis=0, tiled=True)
    group_rows = full_rows.shape[0]
    local_width = w_qkv.shape[2]
    head_shape = (group_rows // SEQ, SEQ, local_width // HEAD_DIM, HEAD_DIM)
    projected = jnp.einsum("td,kde->kte", full_rows, w_qkv, preferred_element_type=jnp.float32)
    queries = (projected[0] + bias_q).astype(jnp.bfloat16).reshape(head_shape)
    key_rows = projected[1].astype(jnp.bfloat16).reshape(head_shape)
    values = (projected[2] + bias_v).astype(jnp.bfloat16).reshape(head_shape)
    context, logsum = lax.map(attend_block, (queries, key_rows, values))
    context = context.reshape(group_rows, local_width)
    attended = (
        lax.psum_scatter(
            jnp.dot(context, w_out, preferred_element_type=jnp.float32),
            "tensor",
            scatter_dimension=0,
            tiled=True,
        )
        + bias_o
    )
    hidden_one, normed_one, scaled_one = norm_forward(
        tokens.astype(jnp.float32) + attended, gain_one, shift_one
    )
    hidden_rows = lax.all_gather(hidden_one.astype(jnp.bfloat16), "tensor", axis=0, tiled=True)
    inner_pre = jnp.dot(hidden_rows, w_up, preferred_element_type=jnp.float32) + bias_up
    activated, slope = gelu_pair(inner_pre)
    active_low = activated.astype(jnp.bfloat16)
    branch = (
        lax.psum_scatter(
            jnp.dot(active_low, w_down, preferred_element_type=jnp.float32),
            "tensor",
            scatter_dimension=0,
            tiled=True,
        )
        + bias_down
    )
    result, normed_two, scaled_two = norm_forward(hidden_one + branch, gain_two, shift_two)
    upstream = cotangent.astype(jnp.float32)
    grad_two = norm_backward(upstream, gain_two, normed_two, scaled_two)
    grad_branch = grad_two.astype(jnp.bfloat16)
    branch_rows = lax.all_gather(grad_branch, "tensor", axis=0, tiled=True)
    grad_down = jnp.einsum("tf,td->fd", active_low, branch_rows, preferred_element_type=jnp.float32)
    grad_inner = (
        jnp.einsum("td,fd->tf", branch_rows, w_down, preferred_element_type=jnp.float32) * slope
    ).astype(jnp.bfloat16)
    grad_up = jnp.einsum("td,tf->df", hidden_rows, grad_inner, preferred_element_type=jnp.float32)
    grad_hidden = grad_two + lax.psum_scatter(
        jnp.einsum("tf,df->td", grad_inner, w_up, preferred_element_type=jnp.float32),
        "tensor",
        scatter_dimension=0,
        tiled=True,
    )
    grad_one = norm_backward(grad_hidden, gain_one, normed_one, scaled_one)
    grad_attended = grad_one.astype(jnp.bfloat16)
    attended_rows = lax.all_gather(grad_attended, "tensor", axis=0, tiled=True)
    grad_out = jnp.einsum("te,td->ed", context, attended_rows, preferred_element_type=jnp.float32)
    grad_context = jnp.einsum(
        "td,ed->te", attended_rows, w_out, preferred_element_type=jnp.float32
    ).astype(jnp.bfloat16)
    grad_q, grad_k, grad_v = lax.map(
        attend_back, (queries, key_rows, values, logsum, grad_context.reshape(head_shape))
    )
    grad_stack = jnp.stack(
        [
            grad_q.reshape(group_rows, local_width),
            grad_k.reshape(group_rows, local_width),
            grad_v.reshape(group_rows, local_width),
        ]
    )
    weight_qkv = jnp.einsum(
        "td,kte->kde", full_rows, grad_stack, preferred_element_type=jnp.float32
    )
    grad_input = grad_one + lax.psum_scatter(
        jnp.einsum("kte,kde->td", grad_stack, w_qkv, preferred_element_type=jnp.float32).astype(
            jnp.bfloat16
        ),
        "tensor",
        scatter_dimension=0,
        tiled=True,
    ).astype(jnp.float32)

    def placed(piece, length):
        return lax.dynamic_update_slice_in_dim(
            jnp.zeros((length,), jnp.float32), piece, rank * piece.shape[0], 0
        )

    vectors = lax.psum(
        (
            placed(jnp.sum(grad_stack[0].astype(jnp.float32), axis=0), D),
            placed(jnp.sum(grad_stack[2].astype(jnp.float32), axis=0), D),
            jnp.sum(grad_attended.astype(jnp.float32), axis=0),
            jnp.sum(grad_hidden * normed_one, axis=0),
            jnp.sum(grad_hidden, axis=0),
            placed(jnp.sum(grad_inner.astype(jnp.float32), axis=0), FF),
            jnp.sum(grad_branch.astype(jnp.float32), axis=0),
            jnp.sum(upstream * normed_two, axis=0),
            jnp.sum(upstream, axis=0),
        ),
        ("dp", "tensor"),
    )
    weight_parts = (
        lax.psum_scatter(
            weight_qkv.astype(jnp.bfloat16), "dp", scatter_dimension=1, tiled=True
        ).astype(jnp.float32),
        lax.psum_scatter(
            grad_out.astype(jnp.bfloat16), "dp", scatter_dimension=1, tiled=True
        ).astype(jnp.float32),
        lax.psum_scatter(
            grad_up.astype(jnp.bfloat16), "dp", scatter_dimension=0, tiled=True
        ).astype(jnp.float32),
        lax.psum_scatter(
            grad_down.astype(jnp.bfloat16), "dp", scatter_dimension=1, tiled=True
        ).astype(jnp.float32),
    )
    return (
        result.astype(jnp.bfloat16),
        grad_input,
        weight_parts[0],
        vectors[0],
        vectors[1],
        weight_parts[1],
        vectors[2],
        vectors[3],
        vectors[4],
        weight_parts[2],
        vectors[5],
        weight_parts[3],
        vectors[6],
        vectors[7],
        vectors[8],
    )


AXES = ("dp", "tensor")
LOG2E = 1.4426950408889634
VMEM = 60 * 1024 * 1024
NT = (((1,), (1,)), ((), ()))


def dot(left, right):
    return jnp.dot(left, right, preferred_element_type=jnp.float32)


def dot_nt(left, right):
    return lax.dot_general(left, right, NT, preferred_element_type=jnp.float32)


def head_masks(width):
    lane = lax.broadcasted_iota(jnp.int32, (1, width), 1)
    return lane < HEAD_DIM


MESH = pl.DeviceIdType.MESH
CHUNKS = 8
SPAN = 256


def bit_of(index, bit):
    return lax.rem(lax.div(index, bit), 2)


def flip(index, bit):
    return index + bit - 2 * bit * bit_of(index, bit)


def mine():
    return lax.axis_index("dp"), lax.axis_index("tensor")


def greet():
    dp, t = mine()
    barrier = pltpu.get_barrier_semaphore()
    peers = [(flip(dp, 1), t), (dp, flip(t, 1)), (flip(dp, 2), t), (flip(dp, 4), t), (flip(dp, 8), t)]
    peers.append((flip(flip(dp, 4), 8), t))
    for peer in peers:
        pl.semaphore_signal(barrier, inc=1, device_id=peer, device_id_type=MESH)
    pl.semaphore_wait(barrier, len(peers))


def turn(left_ref, turned):
    dp, _ = mine()
    height = turned.shape[0] // 16
    whole = left_ref[...].T
    for piece in range(16):
        spot = 0
        for bit, weight in ((1, 8), (2, 4), (4, 2), (8, 1)):
            own = bit_of(dp, bit)
            spot = spot + weight * (own if piece & bit else 1 - own)
        turned[pl.ds(pl.multiple_of(spot * height, height), height), :] = whole[
            piece * height : (piece + 1) * height
        ]


class Scatter:
    def __init__(self, keep, lands, sems, shift=0):
        self.keep = keep
        self.lands = lands
        self.shift = shift
        self.sent, self.got = sems

    def copy(self, stage, m):
        dp, t = mine()
        odd = rem(m + self.shift, 2)
        rows = self.keep.shape[3]
        if stage == 1:
            src, peer = self.keep.at[m, 0], (dp + odd * (flip(dp, 2) - dp), t + (1 - odd) * (1 - 2 * t))
        elif stage == 2:
            src, peer = self.keep.at[m, 1, 0], (dp + (1 - odd) * (flip(dp, 2) - dp), t + odd * (1 - 2 * t))
        else:
            part = rows // 4
            start, peer = (
                (part, (flip(dp, 4), t)), (2 * part, (flip(dp, 8), t)), (0, (flip(flip(dp, 4), 8), t))
            )[stage - 3]
            src = self.keep.at[pl.ds(2 * m, 2), 1, 1, pl.ds(start, part)]
        return pltpu.make_async_remote_copy(
            src_ref=src,
            dst_ref=self.lands[stage - 1].at[m] if stage < 3 else self.lands[2].at[stage - 3, pl.ds(2 * m, 2)],
            send_sem=self.sent.at[stage, m],
            recv_sem=self.got.at[stage, m],
            device_id=peer,
            device_id_type=MESH,
        )

    def start(self, stage, m):
        self.copy(stage, m).start()

    def add(self, stage, m):
        self.copy(stage, m).wait_recv()
        land = self.lands[stage - 1]
        if stage == 1:
            @pl.loop(0, 2)
            def _(half):
                self.keep[m, 1, half] = plus(self.keep[m, 1, half], land[m, half])
        else:
            self.keep[m, 1, 1] = plus(self.keep[m, 1, 1], land[m])

    def step(self, stage, m):
        self.add(stage, m)
        self.start(stage + 1, m)

    def along_z(self, m):
        for stage in (3, 4, 5):
            self.copy(stage, m).start()

    def last(self, m, place):
        rows = self.keep.shape[3]
        for stage in (3, 4, 5):
            self.copy(stage, m).wait_recv()
        rest = pl.ds(3 * rows // 4, rows // 4)
        for chunk in (2 * m, 2 * m + 1):
            total = self.keep[chunk, 1, 1, rest].astype(jnp.float32)
            for other in range(3):
                total = total + self.lands[2][other, chunk].astype(jnp.float32)
            place(chunk, total)

    def actions(self, name, place):
        return {
            f"{name}1": functools.partial(self.step, 1),
            f"{name}2": functools.partial(self.add, 2),
            f"{name}z": self.along_z,
            f"{name}4": lambda m: self.last(m, place),
        }

    def drain(self, stage, m):
        self.copy(stage, m).wait_send()


class Pair:
    def __init__(self, keep, send, land, sems):
        self.keep, self.send, self.land = keep, send, land
        self.sent, self.got = sems
        self.slots = send.shape[0]

    def copy(self, m):
        dp, t = mine()
        return pltpu.make_async_remote_copy(
            src_ref=self.send.at[rem(m, self.slots)],
            dst_ref=self.land.at[m],
            send_sem=self.sent.at[0, m],
            recv_sem=self.got.at[0, m],
            device_id=(flip(dp, 1), t),
            device_id_type=MESH,
        )

    def store(self, m, product, own, odd, slot):
        half = product.shape[0] // 2
        rows = half // 2
        for x in range(2):
            first = odd * x + (1 - odd) * own
            second = odd * own + (1 - odd) * x
            self.send[slot, first, second] = product[x * rows : (x + 1) * rows].astype(jnp.bfloat16)
            self.keep[m, first, second] = product[half + x * rows : half + (x + 1) * rows].astype(
                jnp.bfloat16
            )

    def free(self, m):
        @pl.when(m >= self.slots)
        def _():
            self.copy(m - self.slots).wait_send()

    def add(self, m):
        self.copy(m).wait_recv()

        @pl.loop(0, 4)
        def _(quarter):
            a, b = lax.div(quarter, 2), lax.rem(quarter, 2)
            self.keep[m, a, b] = plus(self.keep[m, a, b], self.land[m, a, b])


def plus(left, right):
    return left + right


def low_buffer(*shape):
    return pltpu.VMEM(shape, jnp.bfloat16)


def land_scratch(chunks, rows, width):
    return [
        low_buffer(chunks, 2, rows, width),
        low_buffer(chunks, rows, width),
        low_buffer(3, chunks, rows // 4, width),
    ]


def rem(m, n):
    return m % n if isinstance(m, int) else lax.rem(m, n)


def run_events(table, actions, ticks, index=None):
    for spot, tick in enumerate(ticks):
        if tick not in table:
            continue

        def go(events=table[tick]):
            for name, m in events:
                actions[name](m)

        if index is None:
            go()
        else:
            pl.when(index == spot)(go)


EARLY_UP, MIDDLE_UP = 0, 2
FFN_TICKS, FFN_END = 16, 27
FFN_SITES = (
    (0, 2, 4, 6, 8, 10, 12, 14),
    (1, 3, 5, 7, 9, 11, 13, 15),
)
FFN_EVENTS = {
    2: (('d0', 0), ('d0', 1), ('u0', 0)),
    4: (('d0', 2), ('d0', 3), ('u0', 1)),
    5: (('d1', 0), ('d1', 1)),
    6: (('d0', 4), ('d0', 5), ('uh', 0), ('u0', 2)),
    7: (('d1', 3),),
    8: (('d0', 6), ('d1', 2), ('d0', 7)),
    9: (('uh', 1), ('d2', 1), ('u0', 3), ('d2', 0), ('dz', 0)),
    11: (('d1', 4), ('u0', 4)),
    12: (('d1', 5), ('d2', 3)),
    13: (('d2', 2), ('dz', 1), ('u0', 5), ('d4', 0)),
    14: (('d1', 6),),
    15: (('d1', 7), ('d2', 5), ('u0', 6)),
    16: (('d2', 4), ('dz', 2)),
    20: (('d4', 1), ('d2', 6), ('u0', 7)),
    24: (('d2', 7), ('dz', 3)),
    25: (('d4', 2),),
    26: (('d4', 3),),
}
ATT_TICKS, ATT_END = 12, 25
ATT_EVENTS = {
    1: (('u2', 0), ('u2', 1), ('uz', 0)),
    2: (('u1', 2), ('u1', 3)),
    4: (('a0', 0), ('u1', 4), ('u1', 5), ('a0', 1), ('u4', 0)),
    5: (('u1', 6), ('u1', 7), ('u2', 2), ('u2', 3), ('uz', 1)),
    6: (('u2', 4), ('a0', 2)),
    7: (('a0', 3), ('a1', 0), ('a1', 1), ('u2', 5), ('uz', 2)),
    8: (('u4', 1), ('u2', 6), ('u2', 7), ('uz', 3)),
    9: (('a1', 2), ('a0', 4)),
    10: (('a1', 3), ('a0', 5), ('u4', 2), ('a2', 1), ('a2', 0), ('az', 0)),
    11: (('a2', 2), ('u4', 3)),
    12: (('a1', 4),),
    13: (('a2', 3), ('az', 1)),
    14: (('a0', 6), ('a1', 5), ('a0', 7), ('a4', 0)),
    16: (('a2', 4),),
    17: (('a4', 1),),
    18: (('a1', 6),),
    19: (('a1', 7),),
    20: (('a2', 5), ('az', 2)),
    21: (('a2', 6),),
    22: (('a2', 7), ('az', 3)),
    23: (('a4', 2),),
    24: (('a4', 3),),
}


def ffn_back_kernel(
    dm_hbm, hr_hbm, dz_hbm, n1_hbm, scale_ref, g1_ref, sums_ref,
    g_own, g_oth, s_own, s_oth, wd_own, wd_oth, wu_own, wu_oth,
    down_ref, up_ref, vec_ref, up_hbm, dz_out, da_out,
    dm, hr, n1, dm_turned, hr_turned, total,
    keep_d, send_d, land_d, d1, d2, d3, keep_u, send_u, land_u, u1, u2, u3,
    sent_d, got_d, sent_u, got_u, local_u, load_sems, out_sems,
):
    j = pl.program_id(0)
    steps = pl.num_programs(0)
    _, t = mine()
    width = keep_d.shape[4]
    early = EARLY_UP
    pair_d = Pair(keep_d, send_d, land_d, (sent_d, got_d))
    pair_u = Pair(keep_u, send_u, land_u, (sent_u, got_u))
    scatter_d = Scatter(keep_d, (d1, d2, d3), (sent_d, got_d))
    scatter_u = Scatter(keep_u, (u1, u2, u3), (sent_u, got_u))
    loads = [
        pltpu.make_async_copy(source, target, load_sems.at[i])
        for i, (source, target) in enumerate(((dm_hbm, dm), (hr_hbm, hr), (dz_hbm, total), (n1_hbm, n1)))
    ]

    @pl.when(j == 0)
    def _():
        for copy in loads:
            copy.start()
        greet()
        vec_ref[...] = jnp.zeros_like(vec_ref)
        vec_ref[0:3, :] = sums_ref[0:3, :]
        up_ref[...] = jnp.zeros_like(up_ref)
        loads[0].wait()
        turn(dm, dm_turned)
        loads[1].wait()
        turn(hr, hr_turned)

    def out_copy(m):
        return pltpu.make_async_copy(keep_u.at[m], up_hbm.at[m - early], local_u.at[m])

    def columns(m):
        return pl.ds(m * width if isinstance(m, int) else pl.multiple_of(m * width, width), width)

    def place_d(m, value):
        down_ref[:, columns(m)] = value

    def place_u(m, value):
        up_ref[:, columns(m)] = value

    def pair_down(m):
        pair_d.add(m)
        scatter_d.copy(1, m).start()

    def pair_up(m):
        pair_u.add(m)
        if m < early + MIDDLE_UP:
            scatter_u.start(1, m)
        else:
            out_copy(m).start()

    def half_up(m):
        scatter_u.add(1, m)
        out_copy(m).start()

    actions = {"d0": pair_down, "u0": pair_up, "uh": half_up}
    actions |= scatter_d.actions("d", place_d) | scatter_u.actions("u", place_u)

    def tick(site):
        run_events(FFN_EVENTS, actions, FFN_SITES[site], j)

    fast = j < steps // 2

    @pl.when(fast)
    def _():
        for part in range(2):
            m = 2 * j + part
            pair_d.free(m)
            for own, g_ref in ((0, g_oth), (1, g_own)):
                product = dot(dm_turned[...], g_ref[:, part * width : (part + 1) * width])
                pair_d.store(m, product, own, part, part)
            pair_d.copy(m).start()

    low = []
    raised = [dot_nt(dm[...], weight[...]) for weight in (wd_oth, wd_own)]
    for own, slope in ((0, s_oth), (1, s_own)):
        low.append((raised[own] * slope[...].astype(jnp.float32)).astype(jnp.bfloat16))
        spot = t * own + (1 - t) * (1 - own)
        row = 6 + 2 * spot + lax.div(j, 4)
        vec_ref[pl.ds(row, 1), columns(lax.rem(j, 4))] = jnp.sum(
            low[-1].astype(jnp.float32), axis=0, keepdims=True
        )
    tick(0)
    pair_u.free(j)
    for own in range(2):
        pair_u.store(j, dot(hr_turned[...], low[own]), own, lax.rem(j, 2), lax.rem(j, 2))
    pair_u.copy(j).start()

    @pl.when(j == 0)
    def _():
        loads[2].wait()

    total[...] += dot_nt(low[0], wu_oth[...]) + dot_nt(low[1], wu_own[...])
    tick(1)

    @pl.when(j == steps - 1)
    def _():
        loads[3].wait()
        tile = 128

        @pl.loop(0, total.shape[0] // tile)
        def _(r):
            here = pl.ds(pl.multiple_of(r * tile, tile), tile)
            upstream = total[here, :]
            normed = n1[here, :]
            grad = norm_backward(upstream, g1_ref[...], normed, scale_ref[here, 0:1])
            grad_low = grad.astype(jnp.bfloat16)
            total[here, :] = grad
            hr[here, :] = grad_low
            vec_ref[3:4, :] += jnp.sum(upstream, axis=0, keepdims=True)
            vec_ref[4:5, :] += jnp.sum(upstream * normed, axis=0, keepdims=True)
            vec_ref[5:6, :] += jnp.sum(grad_low.astype(jnp.float32), axis=0, keepdims=True)
            run_events(FFN_EVENTS, actions, range(FFN_TICKS, FFN_TICKS + 8), r)

        outs = [
            pltpu.make_async_copy(source, target, out_sems.at[i])
            for i, (source, target) in enumerate(((total, dz_out), (hr, da_out)))
        ]
        for copy in outs:
            copy.start()

        run_events(FFN_EVENTS, actions, range(FFN_TICKS + 8, FFN_END))

        for m in range(CHUNKS - 2, CHUNKS):
            pair_d.copy(m).wait_send()
            pair_u.copy(m).wait_send()

        for m in range(CHUNKS):
            for stage in (1, 2):
                scatter_d.drain(stage, m)
                if m < early or (stage == 1 and m < early + MIDDLE_UP):
                    scatter_u.drain(stage, m)
        for m in range(CHUNKS // 2):
            for stage in (3, 4, 5):
                scatter_d.drain(stage, m)
                if m < early // 2:
                    scatter_u.drain(stage, m)

        @pl.loop(early, CHUNKS)
        def _(m):
            out_copy(m).wait()

        for copy in outs:
            copy.wait()


def ffn_backward(
    grad_branch, hidden_rows, grad_two, normed_one, scaled_one, gain_one, sums,
    act, act2, slope, slope2, w_down, w_down2, w_up, w_up2,
):
    rows, depth = grad_branch.shape
    inner = act.shape[1]
    tile = inner // CHUNKS
    last = CHUNKS // 2 - 1
    fixed = lambda *shape: pl.BlockSpec(shape, lambda j: (0,) * len(shape))
    anywhere = pl.BlockSpec(memory_space=pl.ANY)
    double = pl.BlockSpec((rows, 2 * tile), lambda j: (0, jnp.minimum(j, last)))
    column = pl.BlockSpec((rows, tile), lambda j: (0, j))
    row = pl.BlockSpec((tile, depth), lambda j: (j, 0))
    weight_column = pl.BlockSpec((depth, tile), lambda j: (0, j))
    sems = pltpu.SemaphoreType.DMA((6, CHUNKS))
    low, f32 = jnp.bfloat16, jnp.float32
    early = EARLY_UP
    return pl.pallas_call(
        ffn_back_kernel,
        grid=(CHUNKS,),
        in_specs=[anywhere] * 4
        + [fixed(rows, 128), fixed(1, depth), fixed(8, depth)]
        + [double, double, column, column, row, row, weight_column, weight_column],
        out_specs=[
            fixed(depth // 16, inner), fixed(depth // 16, max(early, 1) * tile), fixed(16, depth),
            anywhere, anywhere, anywhere,
        ],
        out_shape=[
            jax.ShapeDtypeStruct((depth // 16, inner), f32),
            jax.ShapeDtypeStruct((depth // 16, max(early, 1) * tile), f32),
            jax.ShapeDtypeStruct((16, depth), f32),
            jax.ShapeDtypeStruct((CHUNKS - early, 2, 2, SPAN, tile), low),
            jax.ShapeDtypeStruct((rows, depth), f32),
            jax.ShapeDtypeStruct((rows, depth), low),
        ],
        scratch_shapes=[
            low_buffer(rows, depth),
            low_buffer(rows, depth),
            pltpu.VMEM((rows, depth), f32),
            low_buffer(depth, rows),
            low_buffer(depth, rows),
            pltpu.VMEM((rows, depth), f32),
            low_buffer(CHUNKS, 2, 2, SPAN, tile),
            low_buffer(2, 2, 2, SPAN, tile),
            low_buffer(CHUNKS, 2, 2, SPAN, tile),
            *land_scratch(CHUNKS, SPAN, tile),
            low_buffer(CHUNKS, 2, 2, SPAN, tile),
            low_buffer(2, 2, 2, SPAN, tile),
            low_buffer(CHUNKS, 2, 2, SPAN, tile),
            low_buffer(max(early + MIDDLE_UP, 1), 2, SPAN, tile),
            *land_scratch(max(early, 2), SPAN, tile)[1:],
            sems, sems, sems, sems,
            pltpu.SemaphoreType.DMA((CHUNKS,)),
            pltpu.SemaphoreType.DMA((4,)),
            pltpu.SemaphoreType.DMA((2,)),
        ],
        compiler_params=pltpu.CompilerParams(
            vmem_limit_bytes=VMEM, collective_id=1, has_side_effects=True
        ),
        cost_estimate=pl.CostEstimate(
            flops=rows * depth * inner * 16, bytes_accessed=60 * 1024 * 1024, transcendentals=0
        ),
        name="ffn_backward",
    )(
        grad_branch, hidden_rows, grad_two, normed_one, scaled_one, gain_one.reshape(1, -1), sums,
        act, act2, slope, slope2, w_down, w_down2, w_up, w_up2,
    )


def attend_back_one(queries, key_rows, values, grad_ctx, levels):
    scale = HEAD_DIM**-0.5
    first = head_masks(128)
    masks = (first, jnp.logical_not(first))
    keys_t = key_rows.T
    picked = [jnp.where(mask, queries, jnp.zeros_like(queries)) for mask in masks]
    grad_picked = [jnp.where(mask, grad_ctx, jnp.zeros_like(grad_ctx)) for mask in masks]
    scores = [dot_nt(key_rows, rows) for rows in picked]
    grad_weights = [dot_nt(values, rows) for rows in grad_picked]
    parts = []
    grad_k = grad_v = None
    for head in range(2):
        weights = jnp.exp2(scores[head] * (LOG2E * scale) - levels[head])
        piece_v = dot(weights.astype(jnp.bfloat16), grad_picked[head])
        rowsum = jnp.sum(weights * grad_weights[head], axis=0, keepdims=True)
        grad_low = (weights * (grad_weights[head] - rowsum)).astype(jnp.bfloat16)
        piece_k = dot(grad_low, picked[head])
        grad_v = piece_v if grad_v is None else grad_v + piece_v
        grad_k = piece_k if grad_k is None else grad_k + piece_k
        parts.append(dot(keys_t[head * HEAD_DIM : (head + 1) * HEAD_DIM], grad_low))
    grad_q = jnp.concatenate(parts, axis=0).T
    return (
        (grad_q * scale).astype(jnp.bfloat16),
        (grad_k * scale).astype(jnp.bfloat16),
        grad_v.astype(jnp.bfloat16),
    )


class Total:
    def __init__(self, sums, lands, sems):
        self.sums, self.lands = sums, lands
        self.sent, self.got = sems

    def copy(self, stage):
        dp, t = mine()
        peer = ((flip(dp, 1), t), (dp, 1 - t), (flip(dp, 2), t), (flip(dp, 4), t), (flip(dp, 8), t))[stage]
        return pltpu.make_async_remote_copy(
            src_ref=self.sums.at[stage],
            dst_ref=self.lands.at[stage],
            send_sem=self.sent.at[stage],
            recv_sem=self.got.at[stage],
            device_id=peer,
            device_id_type=MESH,
        )

    def step(self, stage):
        self.copy(stage).wait_recv()
        self.sums[stage + 1] = self.sums[stage] + self.lands[stage]
        if stage < 4:
            self.copy(stage + 1).start()

    def drain(self):
        for stage in range(5):
            self.copy(stage).wait_send()


def attend_back_kernel(
    da_hbm, x_hbm, up_hbm, dz_hbm, wq_own_hbm, wq_oth_hbm, vec_ref, level_ref,
    qkv_own, c_own, wo_own, qkv_oth, c_oth, wo_oth,
    gin_hbm, gup_ref, gout_ref, gqkv_ref, vec_out, bias_out,
    da, xs, da_turned, x_turned, total, stack, wq,
    keep_u, u1, u2, u3,
    keep_a, send_a, land_a, a1, a2, a3,
    vec_sums, vec_lands, bias_sums, bias_lands,
    sent_u, got_u, sent_a, got_a, sent_v, got_v, sent_b, got_b, local_u, load_sems, out_sems,
):
    g = pl.program_id(0)
    steps = pl.num_programs(0)
    seqs = xs.shape[0] // SEQ
    late = keep_u.shape[0]
    n_chunks = keep_a.shape[0]
    pair = Pair(keep_a, send_a, land_a, (sent_a, got_a))
    scatter_a = Scatter(keep_a, (a1, a2, a3), (sent_a, got_a))
    scatter_u = Scatter(keep_u, (u1, u2, u3), (sent_u, got_u), EARLY_UP)
    vec_total = Total(vec_sums, vec_lands, (sent_v, got_v))
    bias_total = Total(bias_sums, bias_lands, (sent_b, got_b))
    _, t = mine()

    def load_up(m):
        return pltpu.make_async_copy(up_hbm.at[m], keep_u.at[m], local_u.at[m])

    pairs = ((x_hbm, xs), (da_hbm, da), (dz_hbm, total), (wq_oth_hbm, wq.at[0]), (wq_own_hbm, wq.at[1]))
    loads = [pltpu.make_async_copy(*ends, load_sems.at[i]) for i, ends in enumerate(pairs)]

    @pl.when(g == 0)
    def _():
        for m in range(late):
            load_up(m).start()
        for copy in loads:
            copy.start()
        greet()
        for m in range(late):
            load_up(m).wait()
            scatter_u.start(2 if m < MIDDLE_UP else 1, m)
        vec_sums[0] = vec_ref[...]
        vec_total.copy(0).start()
        bias_sums[0] = jnp.zeros_like(bias_sums[0])
        loads[1].wait()
        turn(da, da_turned)
        loads[0].wait()
        turn(xs, x_turned)

    def place_u(m, value):
        width = value.shape[1]
        gup_ref[:, m * width : (m + 1) * width] = value

    def place_a(m, value):
        cols = slice(m // 2 * 128, m // 2 * 128 + 128)
        left, right = value[:, :128], value[:, 128:]
        if m % 2 == 0:
            gout_ref[:, cols] = left
            gqkv_ref[1, :, cols] = right
        else:
            gqkv_ref[0, :, cols] = left
            gqkv_ref[2, :, cols] = right

    def pair_a(m):
        pair.add(m)
        scatter_a.copy(1, m).start()

    actions = {"a0": pair_a} | scatter_u.actions("u", place_u) | scatter_a.actions("a", place_a)

    def tick(site):
        run_events(ATT_EVENTS, actions, range(site, ATT_TICKS, 3), g)

    cols = pl.ds(pl.multiple_of(g * 128, 128), 128)

    def gradient(turned, other, own):
        product = dot(turned[...], jnp.concatenate([other, own], axis=1))
        return product[:, :128], product[:, 128:]

    def emit(part, first, second):
        m = 2 * g + part
        pair.free(m)
        for own in range(2):
            pair.store(m, jnp.concatenate([first[own], second[own]], axis=1), own, part, part)
        pair.copy(m).start()

    for own, qkv_ref, wo_ref in ((0, qkv_oth, wo_oth), (1, qkv_own, wo_own)):
        grad_ctx = dot_nt(da[...], wo_ref[...]).astype(jnp.bfloat16)
        for s in range(seqs):
            rows = slice(s * SEQ, (s + 1) * SEQ)
            levels = [level_ref[own, s, pl.ds(2 * g + head, 1), :] for head in range(2)]
            grads = attend_back_one(
                qkv_ref[0, rows, :], qkv_ref[1, rows, :], qkv_ref[2, rows, :], grad_ctx[rows], levels
            )
            for kind in range(3):
                stack[own * 3 + kind, rows, cols] = grads[kind]
            if s == seqs - 1:
                spot = t * own + (1 - t) * (1 - own)
                where = pl.ds(pl.multiple_of(spot * 512 + g * 128, 128), 128)
                for row, kind in ((0, 0), (1, 2)):
                    bias_sums[0, row : row + 1, where] = jnp.sum(
                        stack[own * 3 + kind, :, cols].astype(jnp.float32), axis=0, keepdims=True
                    )
        tick(own)

    @pl.when(g == steps - 1)
    def _():
        bias_total.copy(0).start()

    grads = [gradient(x_turned, stack[kind, :, cols], stack[kind + 3, :, cols]) for kind in range(3)]
    emit(1, grads[0], grads[2])
    emit(0, gradient(da_turned, c_oth[...], c_own[...]), grads[1])
    tick(2)
    for stage in range(3):
        @pl.when(g == stage)
        def _():
            vec_total.step(stage)

    @pl.when(g == steps - 1)
    def _():
        for copy in loads[2:]:
            copy.wait()
        vec_total.step(3)
        tile = xs.shape[0] // 4
        outs = []
        for r in range(4):
            here = slice(r * tile, (r + 1) * tile)
            block = total[here, :]
            for own in range(2):
                for kind in range(3):
                    block = block + dot_nt(stack[own * 3 + kind, here, :], wq[own, kind])
            total[here, :] = block
            outs.append(pltpu.make_async_copy(total.at[here], gin_hbm.at[here], out_sems.at[r]))
            outs[-1].start()
            run_events(ATT_EVENTS, actions, [ATT_TICKS + r])
            bias_total.step(r)
            if r == 0:
                vec_total.step(4)
        bias_total.step(4)

        run_events(ATT_EVENTS, actions, range(ATT_TICKS + 4, ATT_END))

        vec_out[...] = vec_sums[5]
        bias_out[...] = bias_sums[5]
        for m in range(pair.slots):
            pair.copy(n_chunks - 1 - m).wait_send()

        for m in range(late):
            scatter_u.drain(2, m)
            if m >= MIDDLE_UP:
                scatter_u.drain(1, m)
        for m in range(n_chunks):
            scatter_a.drain(1, m)
            scatter_a.drain(2, m)
        for stage in (3, 4, 5):
            for m in range(late // 2):
                scatter_u.drain(stage, m)
            for m in range(n_chunks // 2):
                scatter_a.drain(stage, m)
        vec_total.drain()
        bias_total.drain()
        for copy in outs:
            copy.wait()


def attend_backward(grad_attended, tokens, keep_up, grad_one, vectors, levels, w_qkv, w_qkv2, own, other):
    rows, depth = tokens.shape
    width = own[1].shape[1]
    steps = width // 128
    late, tile = keep_up.shape[0], keep_up.shape[4]
    n_chunks = 2 * steps
    fixed = lambda *shape: pl.BlockSpec(shape, lambda g: (0,) * len(shape))
    anywhere = pl.BlockSpec(memory_space=pl.ANY)
    side = [
        pl.BlockSpec((3, rows, 128), lambda g: (0, 0, g)),
        pl.BlockSpec((rows, 128), lambda g: (0, g)),
        pl.BlockSpec((128, depth), lambda g: (g, 0)),
    ]
    sems_u = pltpu.SemaphoreType.DMA((6, late))
    sems_a = pltpu.SemaphoreType.DMA((6, n_chunks))
    few = pltpu.SemaphoreType.DMA((5,))
    f32 = jnp.float32
    return pl.pallas_call(
        attend_back_kernel,
        grid=(steps,),
        in_specs=[anywhere] * 6 + [fixed(*vectors.shape), fixed(*levels.shape)] + side + side,
        out_specs=[
            anywhere, fixed(depth // 16, late * tile), fixed(depth // 16, width),
            fixed(3, depth // 16, width), fixed(*vectors.shape), fixed(8, depth),
        ],
        out_shape=[
            jax.ShapeDtypeStruct((rows, depth), f32),
            jax.ShapeDtypeStruct((depth // 16, late * tile), f32),
            jax.ShapeDtypeStruct((depth // 16, width), f32),
            jax.ShapeDtypeStruct((3, depth // 16, width), f32),
            jax.ShapeDtypeStruct(vectors.shape, f32),
            jax.ShapeDtypeStruct((8, depth), f32),
        ],
        scratch_shapes=[
            low_buffer(rows, depth),
            low_buffer(rows, depth),
            low_buffer(depth, rows),
            low_buffer(depth, rows),
            pltpu.VMEM((rows, depth), f32),
            low_buffer(6, rows, width),
            low_buffer(2, 3, depth, width),
            low_buffer(late, 2, 2, SPAN, tile),
            *land_scratch(late, SPAN, tile),
            low_buffer(n_chunks, 2, 2, SPAN, 256),
            low_buffer(2, 2, 2, SPAN, 256),
            low_buffer(n_chunks, 2, 2, SPAN, 256),
            *land_scratch(n_chunks, SPAN, 256),
            pltpu.VMEM((6, *vectors.shape), f32),
            pltpu.VMEM((5, *vectors.shape), f32),
            pltpu.VMEM((6, 8, depth), f32),
            pltpu.VMEM((5, 8, depth), f32),
            sems_u, sems_u, sems_a, sems_a, few, few, few, few,
            pltpu.SemaphoreType.DMA((late,)),
            pltpu.SemaphoreType.DMA((5,)),
            pltpu.SemaphoreType.DMA((4,)),
        ],
        compiler_params=pltpu.CompilerParams(
            vmem_limit_bytes=VMEM, collective_id=2, has_side_effects=True
        ),
        cost_estimate=pl.CostEstimate(
            flops=rows * depth * width * 40, bytes_accessed=60 * 1024 * 1024, transcendentals=0
        ),
        name="attend_backward",
    )(
        grad_attended, tokens, keep_up, grad_one, w_qkv, w_qkv2, vectors, levels, *own, *other,
    )


def deliver_kernel(
    gin, res, up_a, up_b, down, out, qkv, vec, bias,
    o_gin, o_res, o_up, o_down, o_out, o_qkv, *vectors,
):
    o_gin[...] = gin[...]
    o_res[...] = res[...]

    @pl.when(pl.program_id(0) == 0)
    def _():
        cols = o_up.shape[1] - up_b.shape[1]
        if cols:
            o_up[:, :cols] = up_a[:, :cols]
        o_up[:, cols:] = up_b[...]
        o_down[...] = down[...]
        o_out[...] = out[...]
        o_qkv[...] = qkv[...]
        for row in range(6):
            vectors[row][...] = vec[row : row + 1, :]
        wide = vec.shape[1]
        for row in range(4):
            vectors[6][:, row * wide : (row + 1) * wide] = vec[6 + row : 7 + row, :]
        vectors[7][...] = bias[0:1, :]
        vectors[8][...] = bias[1:2, :]


def deliver(gin, res, up_a, up_b, down, out, qkv, vec, bias):
    steps = 2
    wide = vec.shape[1]
    like = lambda array: jax.ShapeDtypeStruct(array.shape, array.dtype)
    flat = lambda size: jax.ShapeDtypeStruct((1, size), jnp.float32)
    fixed = lambda array: pl.BlockSpec(array.shape, lambda i: (0,) * len(array.shape))
    tall = pl.BlockSpec((gin.shape[0] // steps, gin.shape[1]), lambda i: (i, 0))
    up = like(down)
    flats = [flat(wide)] * 6 + [flat(4 * wide)] + [flat(wide)] * 2
    small = [up, like(down), like(out), like(qkv)] + flats
    return pl.pallas_call(
        deliver_kernel,
        grid=(steps,),
        in_specs=[tall, tall] + [fixed(array) for array in (up_a, up_b, down, out, qkv, vec, bias)],
        out_specs=[tall, tall] + [fixed(array) for array in small],
        out_shape=[like(gin), like(res)] + small,
        compiler_params=pltpu.CompilerParams(vmem_limit_bytes=VMEM),
        name="deliver",
    )(gin, res, up_a, up_b, down, out, qkv, vec, bias)


def attend_one(queries, key_rows, values):
    first = head_masks(128)
    values_t = values.T
    parts, levels = [], []
    for head in range(2):
        mask = first if head == 0 else jnp.logical_not(first)
        picked = jnp.where(mask, queries, jnp.zeros_like(queries))
        scores = dot_nt(key_rows, picked) * (LOG2E * HEAD_DIM**-0.5)
        peak = jnp.max(scores, axis=0, keepdims=True)
        lifted = jnp.exp2(scores - peak)
        totals = jnp.sum(lifted, axis=0, keepdims=True)
        context = dot(values_t[head * HEAD_DIM : (head + 1) * HEAD_DIM], lifted.astype(jnp.bfloat16))
        parts.append(context * (1.0 / totals))
        levels.append(peak + jnp.log2(totals))
    return jnp.concatenate(parts, axis=0).T.astype(jnp.bfloat16), levels


class Fetch:
    HOPS = 10

    def __init__(self, source, target, unit, index, sems):
        self.source, self.target, self.unit, self.index = source, target, unit, index
        self.sent, self.got = sems

    def copy(self, hop):
        dp, t = mine()
        core, x, z = bit_of(dp, 1), bit_of(dp, 2), bit_of(dp, 4)
        quarter = {0: x * 2 + z, 1: (1 - x) * 2 + z, 2: x * 2 + 1 - z, 3: (1 - x) * 2 + 1 - z}
        if hop == 0:
            which, part, peer = 0, None, (dp, 1 - t)
        elif hop == 1:
            which, part, peer = 0, None, (flip(dp, 2), t)
        elif hop == 2:
            which, part, peer = 0, None, (flip(dp, 4), t)
        elif hop == 3:
            which, part, peer = 2, 1, (flip(dp, 2), t)
        elif hop == 4:
            which, part, peer = 1, 2, (flip(dp, 4), t)
        elif hop == 9:
            which, part, peer = 3, 0, (dp, 1 - t)
        else:
            which, part, peer = hop - 5, None, (flip(dp, 1), t)
        place = self.unit(core, quarter[which], part, self.index)
        origin = self.source if hop in (0, 9) else self.target
        return pltpu.make_async_remote_copy(
            src_ref=origin.at[place],
            dst_ref=self.target.at[place],
            send_sem=self.sent.at[self.index, hop],
            recv_sem=self.got.at[self.index, hop],
            device_id=peer,
            device_id_type=MESH,
        )

    def start(self, *hops):
        for hop in hops:
            self.copy(hop).start()

    def arrive(self, *hops):
        for hop in hops:
            self.copy(hop).wait_recv()

    def advance(self, stage):
        if stage == 1:
            self.arrive(0)
            self.start(1, 2, 5)
        elif stage == 2:
            self.arrive(1, 2)
            self.start(3, 4, 6, 7)
        elif stage == 3:
            self.arrive(3, 4, 9)
            self.start(8)
        else:
            self.arrive(5, 6, 7, 8)

    def drain(self):
        for hop in range(self.HOPS):
            self.copy(hop).wait_send()


AHEAD = 2
BANDS = (0, 256, 512)
FORWARD_EVENTS = (
    (),
    (),
    (),
    (),
    (),
    ((1, 0),),
    (),
    ((1, 1), (1, 2), (2, 0), (1, 3), (2, 1), (1, 4), (2, 2), (3, 0), (1, 5), (2, 3), (4, 0)),
    (),
    (),
    (),
    ((3, 1),),
    ((1, 6), (2, 4), (3, 2), (1, 7), (4, 1)),
    (),
    (),
    ((2, 5),),
    ((3, 3),),
    ((4, 2), (2, 6), (1, 8), (3, 4)),
    ((4, 3), (2, 7), (1, 9), (3, 5), (3, 6)),
    ((4, 4), (1, 10)),
    ((2, 8),),
    ((3, 7), (4, 5)),
    ((4, 6),),
    ((2, 9),),
    ((4, 7), (2, 10)),
    ((3, 8),),
    ((3, 9),),
    ((3, 10),),
    ((4, 8),),
    ((4, 9),),
    ((4, 10),),
    (),
    (),
    (),
    (),
)
BANDS = (0, 256, 512)
PACE = 4.0


def unit_of(total, lead=(), base=0, tail=()):
    def unit(core, quarter, part, index):
        size = total // 8
        start = base + core * (total // 2) + quarter * size
        if part is not None:
            sixteens = [size // 48] * 3
            for extra in range(size // 16 - sum(sixteens)):
                sixteens[(index + extra) % 3] += 1
            start = start + 16 * sum(sixteens[:part])
            size = 16 * sixteens[part]
        return (*lead, pl.ds(pl.multiple_of(start, 16), size), *tail)

    return unit


def forward_kernel(
    x_hbm, cot_hbm, wq_hbm, wo_hbm, wu_hbm, wd_hbm,
    bq_ref, bv_ref, bu_ref, bo_ref, g1_ref, s1_ref, bd_ref, g2_ref, s2_ref,
    qkv_out1, qkv_out0, ctx_out1, ctx_out0, act_out1, act_out0, slope_out1, slope_out0,
    hr_out, n1_out, dm_out, dz_out, res_out, wq_out, wo_out, wu_out, wd_out,
    level_ref, scale_ref, sums_ref,
    x, cot, wq1, wq0, wo1, wo0, wu1, wu0, wd1, wd0, qkv1, qkv0, ctx1, ctx0, n1, hr, total, act, slope,
    bias_own, bias_oth, sent, got, bias_sent, bias_got, load_sems, out_sems,
):
    dp, t = mine()
    rows, depth = x.shape
    seqs = rows // SEQ
    width = ctx1.shape[1]
    inner = wu1.shape[1]
    tiles = 4
    span = inner // tiles

    chunks = []

    def chunk(source, target, unit):
        chunks.append(Fetch(source, target, unit, len(chunks), (sent, got)))
        return len(chunks) - 1

    starts = BANDS
    bands = [pl.ds(a, b - a) for a, b in zip(starts, starts[1:])]
    c_qkv = [chunk(wq1, wq0, unit_of(depth, lead=(slice(None),), tail=(cols,))) for cols in bands]
    c_out = chunk(wo1, wo0, unit_of(width))
    c_up, c_down = [], []
    for j in range(tiles):
        c_up.append(chunk(wu1, wu0, unit_of(depth, tail=(pl.ds(j * span, span),))))
        c_down.append(chunk(wd1, wd0, unit_of(span, base=j * span)))

    loads, outs, done = {}, [], []
    here_names = {id(wq1): "q", id(wo1): "o", id(wu1): "u", id(wd1): "d"}
    loaded = set()

    def ensure(name):
        if name not in loaded:
            loaded.add(name)
            loads[name].wait()

    def begin(m):
        ensure(here_names[id(chunks[m].source)])
        chunks[m].start(0, 9)

    def finish(copy):
        copy.wait()
        done.append(copy)

    def load(name, source, target):
        copy = pltpu.make_async_copy(source, target, load_sems.at[len(loads)])
        loads[name] = copy
        copy.start()

    def save(source, target):
        copy = pltpu.make_async_copy(source, target, out_sems.at[len(outs)])
        outs.append(copy)
        copy.start()
        return copy

    load("x", x_hbm, x)
    load("q", wq_hbm, wq1)
    greet()
    ahead = AHEAD
    for m in range(ahead):
        begin(m)
    bias_own[:, :width] = bq_ref[...]
    bias_own[:, width : 2 * width] = bv_ref[...]
    bias_own[:, 2 * width :] = bu_ref[...]
    bias_copy = pltpu.make_async_remote_copy(
        src_ref=bias_own, dst_ref=bias_oth, send_sem=bias_sent, recv_sem=bias_got,
        device_id=(dp, 1 - t), device_id_type=MESH,
    )
    bias_copy.start()
    load("o", wo_hbm, wo1)
    load("u", wu_hbm, wu1)
    load("d", wd_hbm, wd1)
    load("cot", cot_hbm, cot)

    saves = {}
    for i, cols in enumerate(bands):
        saves[c_qkv[i]] = (wq0.at[:, :, cols], wq_out.at[:, :, cols])
    saves[c_out] = (wo0, wo_out)
    for j in range(tiles):
        cols = pl.ds(j * span, span)
        saves[c_up[j]] = (wu0.at[:, cols], wu_out.at[:, cols])
        saves[c_down[j]] = (wd0.at[cols], wd_out.at[cols])

    points = iter(FORWARD_EVENTS)

    def point():
        for stage, m in next(points):
            chunks[m].advance(stage)
            if stage == 1 and m + ahead < len(chunks):
                begin(m + ahead)
            if stage == 4:
                save(*saves[m])

    def project(weights, kind, kept, biases, cols):
        product = dot(x[...], weights[kind, :, cols])
        if kind != 1:
            at = cols.start + (0 if kind == 0 else width)
            product = product + biases[:, at : at + cols.stop - cols.start]
        kept[kind, :, cols] = product.astype(jnp.bfloat16)

    def attend(side, kept, context, pair):
        cols = slice(pair * 128, pair * 128 + 128)

        for s in range(seqs):
            here = pl.ds(s * SEQ, SEQ)
            out, levels = attend_one(kept[0, here, cols], kept[1, here, cols], kept[2, here, cols])
            context[here, cols] = out
            for head in range(2):
                spot = 2 * pair + head
                level_ref[side, s, spot : spot + 1, :] = levels[head]

    loads["x"].wait()
    for kind in range(3):
        point()
        project(wq1, kind, qkv1, bias_own, slice(0, width))
    save(qkv1, qkv_out1)
    for pair in range(width // 128):
        point()
        attend(1, qkv1, ctx1, pair)
    save(ctx1, ctx_out1)
    bias_copy.wait_recv()
    for i, (low, high) in enumerate(zip(starts, starts[1:])):
        for kind in range(3):
            point()
            project(wq0, kind, qkv0, bias_oth, slice(low, high))
        for pair in range(low // 128, high // 128):
            point()
            attend(0, qkv0, ctx0, pair)
    save(qkv0, qkv_out0)
    save(ctx0, ctx_out0)
    ensure("o")
    point()
    step = 256

    for r in range(rows // step):
        here = pl.ds(r * step, step)
        attended = dot(ctx1[here, :], wo1[...]) + dot(ctx0[here, :], wo0[...])
        _, normed, scaled = norm_forward(
            x[here, :].astype(jnp.float32) + attended + bo_ref[...], g1_ref[...], s1_ref[...]
        )
        n1[here, :] = normed
        hr[here, :] = (normed * g1_ref[...] + s1_ref[...]).astype(jnp.bfloat16)
        scale_ref[here, :] = jnp.broadcast_to(scaled, (step, 128))

    save(n1, n1_out)
    hr_saved = save(hr, hr_out)
    ensure("u")
    ensure("d")
    big = 1024
    slots = []
    for side, up, down, biases, act_out, slope_out in (
        (1, wu1, wd1, bias_own, act_out1, slope_out1),
        (0, wu0, wd0, bias_oth, act_out0, slope_out0),
    ):
        for j in range(tiles):
            cols = pl.ds(j * span, span)
            slot = len(slots) % 2
            if len(slots) >= 2:
                for copy in slots[-2]:
                    finish(copy)
            bias = biases[:, 2 * width + j * span : 2 * width + (j + 1) * span]
            fresh = not slots

            for r in range(rows // big):
                point()
                point()
                here = pl.ds(r * big, big)
                activated, leaning = gelu_pair(dot(hr[here, :], up[:, cols]) + bias)
                activated = activated.astype(jnp.bfloat16)
                act[slot, here, :] = activated
                slope[slot, here, :] = leaning.astype(jnp.bfloat16)
                product = dot(activated, down[cols, :])
                total[here, :] = product if fresh else total[here, :] + product

            slots.append((
                save(act.at[slot], act_out.at[:, cols]),
                save(slope.at[slot], slope_out.at[:, cols]),
            ))
    point()
    finish(hr_saved)
    loads["cot"].wait()
    sums_ref[...] = jnp.zeros_like(sums_ref)

    for r in range(rows // step):
        here = pl.ds(r * step, step)
        hidden = n1[here, :] * g1_ref[...] + s1_ref[...]
        result, normed, scaled = norm_forward(hidden + total[here, :] + bd_ref[...], g2_ref[...], s2_ref[...])
        x[here, :] = result.astype(jnp.bfloat16)
        upstream = cot[here, :].astype(jnp.float32)
        grad = norm_backward(upstream, g2_ref[...], normed, scaled)
        total[here, :] = grad
        low = grad.astype(jnp.bfloat16)
        hr[here, :] = low
        sums_ref[0:1, :] += jnp.sum(upstream, axis=0, keepdims=True)
        sums_ref[1:2, :] += jnp.sum(upstream * normed, axis=0, keepdims=True)
        sums_ref[2:3, :] += jnp.sum(low.astype(jnp.float32), axis=0, keepdims=True)
        save(x.at[here], res_out.at[here])
        save(hr.at[here], dm_out.at[here])
        save(total.at[here], dz_out.at[here])

    bias_copy.wait_send()
    for fetch in chunks:
        fetch.drain()
    for copy in outs:
        if not any(copy is other for other in done):
            copy.wait()


def forward(tokens, cotangent, w_qkv, w_out, w_up, w_down, biases, bias_o, gain_one, shift_one, bias_down, gain_two, shift_two):
    rows, depth = tokens.shape
    width, inner = w_out.shape[0], w_up.shape[1]
    seqs, heads = rows // SEQ, width // HEAD_DIM
    low, f32 = jnp.bfloat16, jnp.float32
    any_space = pl.BlockSpec(memory_space=pl.ANY)
    near = pl.BlockSpec(memory_space=pltpu.VMEM)
    qkv = (3, rows, width)
    outs = [
        (qkv, low), (qkv, low), ((rows, width), low), ((rows, width), low),
        ((rows, inner), low), ((rows, inner), low), ((rows, inner), low), ((rows, inner), low),
        ((rows, depth), low), ((rows, depth), f32), ((rows, depth), low), ((rows, depth), f32), ((rows, depth), low),
        (w_qkv.shape, low), (w_out.shape, low), (w_up.shape, low), (w_down.shape, low),
        ((2, seqs, heads, SEQ), f32), ((rows, 128), f32), ((8, depth), f32),
    ]
    span = inner // 4
    flat = (1, 2 * width + inner)
    scratch = [
        ((rows, depth), low), ((rows, depth), low), (w_qkv.shape, low), (w_qkv.shape, low),
        (w_out.shape, low), (w_out.shape, low), (w_up.shape, low), (w_up.shape, low),
        (w_down.shape, low), (w_down.shape, low), (qkv, low), (qkv, low),
        ((rows, width), low), ((rows, width), low), ((rows, depth), f32), ((rows, depth), low),
        ((rows, depth), f32), ((2, rows, span), low), ((2, rows, span), low), (flat, f32), (flat, f32),
    ]
    sems = pltpu.SemaphoreType.DMA((len(BANDS) + 8, Fetch.HOPS))
    one = pltpu.SemaphoreType.DMA
    return pl.pallas_call(
        forward_kernel,
        in_specs=[any_space] * 6 + [near] * 9,
        out_specs=[any_space] * 17 + [near] * 3,
        out_shape=[jax.ShapeDtypeStruct(*out) for out in outs],
        scratch_shapes=[pltpu.VMEM(*buffer) for buffer in scratch]
        + [sems, sems, one, one, pltpu.SemaphoreType.DMA((8,)), pltpu.SemaphoreType.DMA((48,))],
        compiler_params=pltpu.CompilerParams(
            vmem_limit_bytes=60 * 1024 * 1024, collective_id=3, has_side_effects=True
        ),
        cost_estimate=pl.CostEstimate(
            flops=rows * depth * (width * 16 + inner * 8), bytes_accessed=80 * 1024 * 1024, transcendentals=0
        ),
        name="forward",
    )(
        tokens, cotangent, w_qkv, w_out, w_up, w_down,
        *(v.reshape(1, -1) for v in (*biases, bias_o, gain_one, shift_one, bias_down, gain_two, shift_two)),
    )


def body(mesh, *args):
    tokens, w_qkv = args[0], args[2]
    n_dp, n_tensor = mesh.shape["dp"], mesh.shape["tensor"]
    local = (*tokens.shape, w_qkv.shape[2], args[9].shape[1])
    if (n_dp, n_tensor) == (16, 2) and local == (1024, 1024, 512, 2048):
        return body_tokens(*args)
    return body_tensor(*args)


def body_tokens(
    tokens,
    cotangent,
    w_qkv,
    bias_q,
    bias_v,
    w_out,
    bias_o,
    gain_one,
    shift_one,
    w_up,
    bias_up,
    w_down,
    bias_down,
    gain_two,
    shift_two,
):
    (
        qkv, qkv2, ctx, ctx2, active, active2, slope, slope2,
        hidden_rows, normed_one, grad_branch, grad_two, result,
        w_qkv2, w_out2, w_up2, w_down2, levels, scaled_one, sums,
    ) = forward(
        tokens, cotangent, w_qkv, w_out, w_up, w_down, (bias_q, bias_v, bias_up),
        bias_o, gain_one, shift_one, bias_down, gain_two, shift_two,
    )
    grad_down, up_early, vectors, keep_up, grad_one, grad_attended = ffn_backward(
        grad_branch, hidden_rows, grad_two, normed_one, scaled_one, gain_one, sums,
        active, active2, slope, slope2, w_down, w_down2, w_up, w_up2,
    )
    grad_input, up_late, grad_out, grad_qkv, vectors, biases = attend_backward(
        grad_attended, tokens, keep_up, grad_one, vectors, levels, w_qkv, w_qkv2,
        (qkv, ctx, w_out), (qkv2, ctx2, w_out2),
    )
    grad_input, result, grad_up, grad_down, grad_out, grad_qkv, *vectors = deliver(
        grad_input, result, up_early, up_late, grad_down, grad_out, grad_qkv, vectors, biases
    )
    g_shift_two, g_gain_two, g_bias_down, g_shift_one, g_gain_one, g_bias_o, g_bias_up, g_bias_q, g_bias_v = (
        vector.reshape(-1) for vector in vectors
    )
    return (
        result,
        grad_input,
        grad_qkv,
        g_bias_q,
        g_bias_v,
        grad_out.T,
        g_bias_o,
        g_gain_one,
        g_shift_one,
        grad_up,
        g_bias_up,
        grad_down.T,
        g_bias_down,
        g_gain_two,
        g_shift_two,
    )


def solution(mesh):
    in_specs = (
        P(("dp", "tensor"), None),
        P(("dp", "tensor"), None),
        P(None, None, "tensor"),
        P("tensor"),
        P("tensor"),
        P("tensor", None),
        P(),
        P(),
        P(),
        P(None, "tensor"),
        P("tensor"),
        P("tensor", None),
        P(),
        P(),
        P(),
    )
    out_specs = (
        P(("dp", "tensor"), None),
        P(("dp", "tensor"), None),
        P(None, "dp", "tensor"),
        P(),
        P(),
        P("tensor", "dp"),
        P(),
        P(),
        P(),
        P("dp", "tensor"),
        P(),
        P("tensor", "dp"),
        P(),
        P(),
        P(),
    )
    return jax.shard_map(functools.partial(body, mesh), mesh=mesh, in_specs=in_specs, out_specs=out_specs, check_vma=False)
```
